32 devices in a mesh: dp: 8 (over z, core), tensor: 4 (over y, x).
Axes of the slice: x: 2, y: 2, z: 4, core: 2. Of those that a mesh axis runs over, the one named last changes fastest.
Arguments:
- hidden_in: bfloat16 [16384, 1024], P(('dp', 'tensor')), may hold values from -6 to 6
- norm_gain: bfloat16 [1024], P('dp'), may hold values from 0.5 to 1.5
- proj_gate: bfloat16 [1024, 2048], P('dp', 'tensor'), may hold values from -0.1875 to 0.1875
- proj_conv: bfloat16 [1024, 2048], P('dp', 'tensor'), may hold values from -0.1875 to 0.1875
- proj_state: bfloat16 [1024, 288], P('dp'), may hold values from -0.1875 to 0.1875
- conv_kernel: bfloat16 [4, 32, 64], P(None, 'tensor', 'dp'), may hold values from -3 to 3
- conv_offset: bfloat16 [32, 64], P('tensor', 'dp'), may hold values from -0.5 to 0.5
- state_kernel: bfloat16 [4, 256], P(None, 'dp'), may hold values from -3 to 3
- state_offset: bfloat16 [256], P('dp'), may hold values from -0.5 to 0.5
- step_bias: bfloat16 [32], P('dp'), may hold values from -6 to -2.5
- decay_log: bfloat16 [32], P('dp'), may hold values from -1 to 2.5
- skip_gain: bfloat16 [32], P('dp'), may hold values from 0.5 to 2
- gate_gain: bfloat16 [32, 64], P('tensor', 'dp'), may hold values from 0.5 to 1.5
- proj_out: bfloat16 [2048, 1024], P('tensor', 'dp'), may hold values from -0.125 to 0.125
- out_cotangent: bfloat16 [16384, 1024], P(('dp', 'tensor')), may hold values from -6 to 6
- seq_lengths: int32 [8, 1], P('dp'), may hold values from 1024 to 2048, as said below
Outputs:
- block_out: bfloat16 [16384, 1024], P(('dp', 'tensor'))
- grad_hidden: float32 [16384, 1024], P(('dp', 'tensor'))
- grad_norm_gain: float32 [1024], P(('dp', 'tensor'))
- grad_proj_gate: float32 [1024, 2048], P('dp', 'tensor')
- grad_proj_conv: float32 [1024, 2048], P('dp', 'tensor')
- grad_proj_state: float32 [1024, 288], P(('dp', 'tensor'))
- grad_proj_out: float32 [2048, 1024], P('tensor', 'dp')
- grad_conv_kernel: float32 [4, 32, 64], P(None, 'tensor', 'dp')
- grad_conv_offset: float32 [32, 64], P('tensor', 'dp')
- grad_state_kernel: float32 [4, 256], P(None, 'dp')
- grad_state_offset: float32 [256], P('dp')
- grad_step_bias: float32 [32], P('dp')
- grad_decay_log: float32 [32], P('dp')
- grad_skip_gain: float32 [32], P('dp')
- grad_gate_gain: float32 [32, 64], P('tensor', 'dp')
The draws below stay inside these ranges and needn't reach their ends.
Inputs may be any that keep to these rules, and one draw needn't show every extreme that they name: `seq_lengths`: some group's lengths are all 2048 and some length is 1024; in every group the lengths sum to at most 2048.
All inputs are finite; a program needn't handle non-finite values.
Results may differ from the reference program's by a relative error of at most 0.018.
Values may be sent and summed in bfloat16 or wider, within the bound.
No kernel may reach another device: no remote copies, remote signals or barrier semaphores. Data moves between devices by JAX's collectives and lax.ppermute only.
A program may use at most 384 MiB of HBM per device.

```python
import jax
import jax.numpy as jnp
from jax import lax

D = 1024
HEADS = 32
HEADDIM = 64
STATE = 128
CONV = 4
BLOCK = 256
TOK_GROUP = 2048
LEN_MAX = 2048
LEN_MIN = 1024
INNER = 2048
BCDT = 288
GROUPS = 8
SEQS_DEV = 1
TOKENS = 16384


def draw_seq_lengths(key, part):
    first_key = jax.random.fold_in(key, 11)
    second_key = jax.random.fold_in(key, 23)
    lengths = jax.random.randint(first_key, (GROUPS, SEQS_DEV), LEN_MIN, LEN_MAX + 1)
    busiest = jax.random.randint(second_key, (), 0, GROUPS)
    group_index = jnp.arange(GROUPS)[:, None]
    slot_index = jnp.arange(SEQS_DEV)[None, :]
    lengths = jnp.where(group_index == busiest, LEN_MAX, lengths)
    lengths = jnp.where((group_index == (busiest + 1) % GROUPS) & (slot_index == 0), LEN_MIN, lengths)
    return lengths.astype(jnp.int32)


def steps_of(own_key, shape, pieces, low, largest):
    def one(position, parts):
        steps = jax.random.uniform(jax.random.fold_in(jax.random.fold_in(own_key, 6), position), (parts,), jnp.float32, low / len(pieces), largest / len(pieces))
        return jnp.repeat(jnp.exp(steps), shape[position] // parts).reshape((-1,) + (1,) * (len(shape) - position - 1))

    gain = one(*pieces[0])
    for cut in pieces[1:]:
        gain = gain * one(*cut)
    return gain


def scatter_about(rng, dims, width, most, cuts=(), kind=jnp.bfloat16):
    entries = width * jax.random.normal(rng, dims, jnp.float32)
    if cuts:
        entries = entries * steps_of(rng, dims, cuts, -0.22, 0.18)
    return jnp.clip(entries, -most, most).astype(kind)


def setup_inputs(seed: int = 0) -> dict:
    streams_of = jax.random.split(jax.random.key(seed), 17)
    return {
        "hidden_in": scatter_about(streams_of[0], (TOKENS, D), 1.0, 6.0, ((0, 32),)),
        "norm_gain": jnp.clip(1.0 + 0.1 * jax.random.normal(streams_of[1], (D,), jnp.float32), 0.5, 1.5).astype(jnp.bfloat16),
        "proj_gate": scatter_about(streams_of[2], (D, INNER), D ** -0.5, 0.1875, ((0, 8), (1, 4))),
        "proj_conv": scatter_about(streams_of[3], (D, INNER), D ** -0.5, 0.1875, ((0, 8), (1, 4))),
        "proj_state": scatter_about(streams_of[4], (D, BCDT), D ** -0.5, 0.1875, ((0, 8),)),
        "conv_kernel": scatter_about(streams_of[5], (CONV, HEADS, HEADDIM), CONV ** -0.5, 3.0, ((1, 4), (2, 8))),
        "conv_offset": jnp.clip(jax.random.uniform(streams_of[6], (HEADS, HEADDIM), jnp.float32, -0.5, 0.5) * steps_of(streams_of[6], (HEADS, HEADDIM), ((0, 4), (1, 8)), -0.4, 0.0), -0.5, 0.5).astype(jnp.bfloat16),
        "state_kernel": scatter_about(streams_of[7], (CONV, 2 * STATE), CONV ** -0.5, 3.0, ((1, 8),)),
        "state_offset": jnp.clip(jax.random.uniform(streams_of[8], (2 * STATE,), jnp.float32, -0.5, 0.5) * steps_of(streams_of[8], (2 * STATE,), ((0, 8),), -0.4, 0.0), -0.5, 0.5).astype(jnp.bfloat16),
        "step_bias": jnp.clip(-6.0 + 3.5 * jax.random.uniform(streams_of[9], (HEADS,), jnp.float32) ** steps_of(streams_of[9], (HEADS,), ((0, 8),), -0.2, 0.2), -6.0, -2.5).astype(jnp.bfloat16),
        "decay_log": jnp.clip(-1.0 + 3.5 * jax.random.uniform(streams_of[10], (HEADS,), jnp.float32) ** steps_of(streams_of[10], (HEADS,), ((0, 8),), -0.2, 0.2), -1.0, 2.5).astype(jnp.bfloat16),
        "skip_gain": jnp.clip(0.5 + 1.5 * jax.random.uniform(streams_of[11], (HEADS,), jnp.float32) ** steps_of(streams_of[11], (HEADS,), ((0, 8),), -0.2, 0.2), 0.5, 2.0).astype(jnp.bfloat16),
        "gate_gain": jnp.clip(1.0 + 0.1 * jax.random.normal(streams_of[12], (HEADS, HEADDIM), jnp.float32), 0.5, 1.5).astype(jnp.bfloat16),
        "proj_out": scatter_about(streams_of[13], (INNER, D), INNER ** -0.5, 0.125, ((0, 4), (1, 8))),
        "out_cotangent": scatter_about(streams_of[14], (TOKENS, D), 1.0, 6.0, ((0, 32),)),
        "seq_lengths": draw_seq_lengths(jax.random.fold_in(streams_of[16], 71), 0),
    }


epsilon = 1e-05
highest = lax.Precision.HIGHEST

def against_rows(left_matrix, right_matrix):
    return lax.dot_general(left_matrix, right_matrix, (((1,), (1,)), ((), ())), preferred_element_type=jnp.float32)

def along_rows(left_matrix, right_matrix):
    return lax.dot_general(left_matrix, right_matrix, (((0,), (0,)), ((), ())), preferred_element_type=jnp.float32)

def segments(lengths, tokens):
    seq_ends = jnp.cumsum(lengths.astype(jnp.int32)).astype(jnp.int32)
    places = jnp.arange(tokens, dtype=jnp.int32)
    passed = places[:, None] >= seq_ends[None, :]
    segment = lax.optimization_barrier(jnp.sum(passed.astype(jnp.int32), axis=1)).astype(jnp.int32)
    starts = lax.optimization_barrier(jnp.max(jnp.where(passed, seq_ends[None, :], jnp.zeros_like(seq_ends)[None, :]), axis=1)).astype(jnp.int32)
    return (places, starts, segment)

def conv_silu(values, kernel, offset, places, starts):
    taps = kernel.shape[0]
    result = offset[None, :] + kernel[taps - 1][None, :] * values
    for lag_steps in range(1, taps):
        shifted = jnp.concatenate([jnp.zeros((lag_steps, values.shape[1]), values.dtype), values[:-lag_steps]], axis=0)
        usable = (places - lag_steps >= starts)[:, None]
        result = result + kernel[taps - 1 - lag_steps][None, :] * jnp.where(usable, shifted, jnp.zeros_like(shifted))
    return jax.nn.silu(result)

def block_scan(inputs_x, b_rows, c_rows, log_decay, step_size, skip_head, segment, block_size):
    tokens, head_count, head_width = inputs_x.shape
    block_count = tokens // block_size
    states = b_rows.shape[1]
    stacked = (inputs_x.reshape(block_count, block_size, head_count, head_width), b_rows.reshape(block_count, block_size, states), c_rows.reshape(block_count, block_size, states), log_decay.reshape(block_count, block_size, head_count), step_size.reshape(block_count, block_size, head_count), segment.reshape(block_count, block_size))
    lower_mask = jnp.arange(block_size)[:, None] >= jnp.arange(block_size)[None, :]

    def advance(carry_in, block_inputs):
        carry_state, last_segment = carry_in
        block_x, block_b, block_c, block_decay, block_step, block_segment = block_inputs
        cumulative = jnp.cumsum(block_decay, axis=0).T
        pair_mask = ((block_segment[:, None] == block_segment[None, :]) & lower_mask)[None, :, :]
        spread = cumulative[:, :, None] - cumulative[:, None, :]
        kernel = jnp.where(pair_mask, jnp.exp(jnp.where(pair_mask, spread, 0.0)), 0.0)
        gram_matrix = jnp.dot(block_c, block_b.T, precision=highest)
        mixing = kernel * gram_matrix[None, :, :] * block_step.T[:, None, :]
        inner_y = jnp.einsum('hij,jhp->ihp', mixing, block_x, precision=highest)
        follows = (block_segment == last_segment).astype(carry_state.dtype)
        carried = follows[:, None] * jnp.exp(cumulative.T)
        outer_y = jnp.einsum('is,hps->ihp', block_c, carry_state, precision=highest) * carried[:, :, None]
        result = inner_y + outer_y + skip_head[None, :, None] * block_x
        tail_segment = block_segment[-1]
        ending = cumulative[:, -1]
        keep_weight = (block_segment == tail_segment).astype(carry_state.dtype)[:, None] * jnp.exp(ending[None, :] - cumulative.T) * block_step
        fresh_state = jnp.einsum('jhp,js->hps', keep_weight[:, :, None] * block_x, block_b, precision=highest)
        survive = jnp.where(tail_segment == last_segment, jnp.exp(ending), jnp.zeros_like(ending))
        carry_state = carry_state * survive[:, None, None] + fresh_state
        return ((carry_state, tail_segment), result)
    start_state = jnp.zeros((head_count, head_width, states), inputs_x.dtype)
    final_carry, outputs = lax.scan(advance, (start_state, jnp.array(-1, jnp.int32)), stacked)
    return outputs.reshape(tokens, head_count * head_width)

def state_mixer(conv_in, state_in, step_in, conv_kernel, conv_offset, state_kernel, state_offset, step_bias, decay_log, skip_gain, head_start, places, starts, segment):
    channels = conv_in.shape[1]
    heads_here = channels // HEADDIM
    conv_out = conv_silu(conv_in, conv_kernel, conv_offset, places, starts)
    state_out = conv_silu(state_in, state_kernel, state_offset, places, starts)
    first_head = head_start.astype(jnp.int32)
    raw_step = lax.dynamic_slice_in_dim(step_in, first_head, heads_here, 1) + lax.dynamic_slice_in_dim(step_bias, first_head, heads_here, 0)[None, :]
    step_size = jax.nn.softplus(raw_step)
    decay_rates = jnp.exp(lax.dynamic_slice_in_dim(decay_log, first_head, heads_here, 0))
    skip_head = lax.dynamic_slice_in_dim(skip_gain, first_head, heads_here, 0)
    return block_scan(conv_out.reshape(conv_out.shape[0], heads_here, HEADDIM), state_out[:, :STATE], state_out[:, STATE:], -decay_rates[None, :] * step_size, step_size, skip_head, segment, BLOCK)

def reference(hidden_in, norm_gain, proj_gate, proj_conv, proj_state, conv_kernel, conv_offset, state_kernel, state_offset, step_bias, decay_log, skip_gain, gate_gain, proj_out, out_cotangent, seq_lengths):
    weights_in = jnp.concatenate([proj_gate, proj_conv, proj_state], axis=1)
    gain_in = norm_gain.astype(jnp.float32)
    gain_gate = gate_gain.astype(jnp.float32).reshape(INNER)
    small_params = (conv_kernel.astype(jnp.float32).reshape(CONV, INNER), conv_offset.astype(jnp.float32).reshape(INNER), state_kernel.astype(jnp.float32), state_offset.astype(jnp.float32), step_bias.astype(jnp.float32), decay_log.astype(jnp.float32), skip_gain.astype(jnp.float32))
    head_start = jnp.array(0, jnp.int32)

    def group_pass(totals, inputs):
        rows_in, cotangent, lengths = inputs
        places, starts, segment = segments(lengths, TOK_GROUP)
        values = rows_in.astype(jnp.float32)
        inverse_in = lax.rsqrt(lax.optimization_barrier(jnp.mean(values * values, axis=1, keepdims=True)) + epsilon)
        scaled = values * inverse_in
        normed = (scaled * gain_in[None, :]).astype(jnp.bfloat16)
        projected = jnp.dot(normed, weights_in, preferred_element_type=jnp.float32)
        gate_pre = projected[:, :INNER]
        conv_pre = projected[:, INNER:2 * INNER]
        state_pre = projected[:, 2 * INNER:2 * INNER + 2 * STATE]
        step_pre = projected[:, 2 * INNER + 2 * STATE:]

        def local_mixer(conv_in, state_in, step_in, kernel_conv, offset_conv, kernel_state, offset_state, bias_step, rate_log, skip_heads):
            return state_mixer(conv_in, state_in, step_in, kernel_conv, offset_conv, kernel_state, offset_state, bias_step, rate_log, skip_heads, head_start, places, starts, segment)
        mixed_out, mixer_back = jax.vjp(local_mixer, conv_pre, state_pre, step_pre, small_params[0], small_params[1], small_params[2], small_params[3], small_params[4], small_params[5], small_params[6])
        gate_act = jax.nn.silu(gate_pre)
        gated_in = mixed_out * gate_act
        inverse_gate = lax.rsqrt(lax.optimization_barrier(jnp.mean(gated_in * gated_in, axis=1, keepdims=True)) + epsilon)
        gate_hat = gated_in * inverse_gate
        gated_out = (gate_hat * gain_gate[None, :]).astype(jnp.bfloat16)
        block_out = (values + jnp.dot(gated_out, proj_out, preferred_element_type=jnp.float32)).astype(jnp.bfloat16)
        grad_gated = against_rows(cotangent, proj_out)
        grad_out_proj = along_rows(gated_out, cotangent)
        grad_gain_gate = lax.optimization_barrier(jnp.sum(grad_gated * gate_hat, axis=0))
        grad_hat = grad_gated * gain_gate[None, :]
        grad_inner = inverse_gate * (grad_hat - gate_hat * lax.optimization_barrier(jnp.mean(grad_hat * gate_hat, axis=1, keepdims=True)))
        grad_mixed = grad_inner * gate_act
        sigmoid_gate = jax.nn.sigmoid(gate_pre)
        grad_gate_pre = grad_inner * mixed_out * sigmoid_gate * (1.0 + gate_pre * (1.0 - sigmoid_gate))
        mixer_grads = mixer_back(grad_mixed)
        state_bf = jnp.concatenate([mixer_grads[1], mixer_grads[2]], axis=1).astype(jnp.bfloat16)
        gate_bf = grad_gate_pre.astype(jnp.bfloat16)
        conv_bf = mixer_grads[0].astype(jnp.bfloat16)
        grad_normed = against_rows(gate_bf, proj_gate) + against_rows(conv_bf, proj_conv) + against_rows(state_bf, proj_state)
        grad_gain_in = lax.optimization_barrier(jnp.sum(grad_normed * scaled, axis=0))
        grad_scaled = grad_normed * gain_in[None, :]
        grad_rows = cotangent.astype(jnp.float32) + inverse_in * (grad_scaled - scaled * lax.optimization_barrier(jnp.mean(grad_scaled * scaled, axis=1, keepdims=True)))
        terms = (grad_gain_in, along_rows(normed, gate_bf), along_rows(normed, conv_bf), along_rows(normed, state_bf), grad_out_proj, mixer_grads[3], mixer_grads[4], mixer_grads[5], mixer_grads[6], mixer_grads[7], mixer_grads[8], mixer_grads[9], grad_gain_gate)
        totals = jax.tree.map(lambda total_sum, new_term: total_sum + new_term, totals, terms)
        return (totals, (block_out, grad_rows))
    zero_totals = (jnp.zeros((D,), jnp.float32), jnp.zeros((D, INNER), jnp.float32), jnp.zeros((D, INNER), jnp.float32), jnp.zeros((D, BCDT), jnp.float32), jnp.zeros((INNER, D), jnp.float32), jnp.zeros((CONV, INNER), jnp.float32), jnp.zeros((INNER,), jnp.float32), jnp.zeros((CONV, 2 * STATE), jnp.float32), jnp.zeros((2 * STATE,), jnp.float32), jnp.zeros((HEADS,), jnp.float32), jnp.zeros((HEADS,), jnp.float32), jnp.zeros((HEADS,), jnp.float32), jnp.zeros((INNER,), jnp.float32))
    totals, results = lax.scan(group_pass, zero_totals, (hidden_in.reshape(GROUPS, TOK_GROUP, D), out_cotangent.reshape(GROUPS, TOK_GROUP, D), seq_lengths))
    block_outs, grad_rows = results
    return (block_outs.reshape(TOKENS, D), grad_rows.reshape(TOKENS, D), totals[0], totals[1], totals[2], totals[3], totals[4], totals[5].reshape(CONV, HEADS, HEADDIM), totals[6].reshape(HEADS, HEADDIM), totals[7], totals[8], totals[9], totals[10], totals[11], totals[12].reshape(HEADS, HEADDIM))
```

```python
import functools

import jax
import jax.numpy as jnp
import numpy as np
from jax import lax
from jax.experimental import pallas as pl
from jax.experimental.pallas import tpu as pltpu
from jax.sharding import PartitionSpec as P

HEADDIM = 64
STATE = 128
INNER = 2048
LANES = 128
ROWS = 256
WIDE_ROWS = 512
SUB = 128
EPS = 1e-05
LOG2E = 1.4426950408889634

f32 = jnp.float32
bf16 = jnp.bfloat16


def nn(a, b):
    return lax.dot_general(a, b, (((1,), (0,)), ((), ())), preferred_element_type=f32)


def nt(a, b):
    return lax.dot_general(a, b, (((1,), (1,)), ((), ())), preferred_element_type=f32)


def tn(a, b):
    return lax.dot_general(a, b, (((0,), (0,)), ((), ())), preferred_element_type=f32)


def pieces(z, count):
    parts = []
    for _ in range(count - 1):
        part = z.astype(bf16)
        parts.append(part)
        z = z - part.astype(f32)
    parts.append(z.astype(bf16))
    return parts


def head_matrix(channels):
    lane = lax.broadcasted_iota(jnp.int32, (LANES, channels), 1)
    row = lax.broadcasted_iota(jnp.int32, (LANES, channels), 0)
    inside = (lane >= row * HEADDIM) & (lane < row * HEADDIM + HEADDIM)
    return jnp.where(inside, 1.0, 0.0).astype(bf16)


def spread_heads(z, heads):
    return sum(nn(part, heads) for part in pieces(z, 2))


def gather_heads(z, heads):
    return sum(nt(part, heads) for part in pieces(z, 2))


def triangle_sum(triangle, z):
    return sum(nn(triangle, part) for part in pieces(z, 3))


def ends_of(len_ref, count):
    ends, total = [], 0
    for s in range(count):
        total = total + len_ref[0, s]
        ends.append(total)
    return ends


def segment_of(places, ends):
    return sum((places >= end).astype(jnp.int32) for end in ends)


def start_of(places, ends):
    start = jnp.zeros_like(places)
    for end in ends:
        start = jnp.where(places >= end, end, start)
    return start


def scan_terms(raw, decay, base, ends, heads):
    sub = raw.shape[0]
    row = lax.broadcasted_iota(jnp.int32, (sub, sub), 0)
    col = lax.broadcasted_iota(jnp.int32, (sub, sub), 1)
    lower = jnp.where(row >= col, 1.0, 0.0).astype(bf16)
    step = jnp.maximum(raw, 0.0) + jnp.log1p(jnp.exp(-jnp.abs(raw)))
    log_decay = -decay * step
    cum = triangle_sum(lower, log_decay)
    places = base + lax.broadcasted_iota(jnp.int32, (sub, 1), 0)
    segment = segment_of(places, ends)
    before = segment_of(base - 1, ends)
    tail = segment_of(base + sub - 1, ends)
    last = cum[sub - 1 : sub, :]
    carried = jnp.where(segment == before, jnp.exp(cum), 0.0)
    keep = jnp.where(segment == tail, jnp.exp(last - cum), 0.0)
    survive = jnp.where(tail == before, jnp.exp(last), 0.0)
    wide = spread_heads(
        jnp.concatenate([step, carried, keep, jnp.broadcast_to(survive, (8, LANES))], axis=0), heads
    )
    return (
        step,
        log_decay,
        cum * LOG2E,
        wide[:sub],
        wide[sub : 2 * sub],
        wide[2 * sub : 3 * sub],
        wide[3 * sub : 3 * sub + 1],
    )


def pair_stack(z):
    lane = lax.broadcasted_iota(jnp.int32, z.shape, 1)
    zero = jnp.zeros_like(z)
    return jnp.concatenate(
        [jnp.where(lane < HEADDIM, z, zero), jnp.where(lane >= HEADDIM, z, zero)], axis=0
    )


def silu(u):
    return u * jax.nn.sigmoid(u)


def own_lanes(z, shift, count):
    moved = pltpu.roll(z, (z.shape[1] - shift) % z.shape[1], 1)
    lane = lax.broadcasted_iota(jnp.int32, z.shape, 1)
    return jnp.where(lane < count, moved, 0.0)


def nn3(a, b):
    a, a_low = pieces(a, 2)
    b, b_low = pieces(b, 2)
    return nn(jnp.concatenate([a, a_low, a], axis=1), jnp.concatenate([b, b, b_low], axis=0))


def nt3(a, b):
    a, a_low = pieces(a, 2)
    b, b_low = pieces(b, 2)
    return nt(jnp.concatenate([a, a_low, a], axis=1), jnp.concatenate([b, b, b_low], axis=1))


def pair_product(mixing, z):
    high, low = pieces(z, 2)
    both = nn(
        jnp.concatenate(mixing, axis=1),
        jnp.concatenate([pair_stack(high), pair_stack(low)], axis=1),
    )
    return both[:, :LANES] + both[:, LANES:]


def take_rows(refs, which, buffer):
    if len(refs) == 1:
        return refs[0][...]
    half = refs[3].shape[1]
    for k in range(3):

        @pl.when(which == k)
        def _(k=k):
            buffer[...] = refs[k][...]

    @pl.when(which == 3)
    def _():
        buffer[:, :half] = refs[3][...]
        buffer[:, half:] = refs[4][...]

    return buffer[...]


def put_halves(refs, which, product):
    half = product.shape[1] // 2
    left, right = product[:, :half], product[:, half:]
    if len(refs) == 2:
        refs[0][...] = left
        refs[1][...] = right
        return
    left_sent, left_kept, right_sent, right_kept = refs

    @pl.when(which % 2 == 1)
    def _():
        left_sent[...] = left

    @pl.when(which % 2 == 0)
    def _():
        left_kept[...] = left

    @pl.when(which >= 2)
    def _():
        right_sent[...] = right

    @pl.when(which < 2)
    def _():
        right_kept[...] = right


def scan_kernel(len_ref, first_ref, place_ref, *refs, parts, seqs, taps, head_count):
    part_refs, refs = refs[:parts], refs[parts:]
    (
        w_ref,
        gain_ref,
        prm_ref,
        prs_ref,
        prh_ref,
        normed_ref,
        v_ref,
        u_ref,
        vs_ref,
        us_ref,
        raw_ref,
        y_ref,
        st_ref,
        hid_buf,
        vbuf,
        sbuf,
        carry,
    ) = refs
    rows, channels = v_ref.shape
    step_id = pl.program_id(0)
    base = step_id * rows
    ends = ends_of(len_ref, seqs)

    @pl.when(step_id == 0)
    def _():
        vbuf[0:8, :] = jnp.zeros((8, channels), f32)
        sbuf[0:8, :] = jnp.zeros((8, 2 * STATE), f32)
        carry[...] = jnp.zeros_like(carry)

    values = take_rows(part_refs, place_ref[0, step_id], hid_buf).astype(f32)
    inverse = lax.rsqrt(jnp.mean(values * values, axis=1, keepdims=True) + EPS)
    normed = (values * inverse * gain_ref[...]).astype(bf16)
    normed_ref[...] = normed
    conv_pre = nn(normed, w_ref[:, :channels])
    state_all = nn(normed, w_ref[:, channels:])
    v_ref[...] = conv_pre.astype(bf16)
    vs_ref[...] = state_all[:, : 2 * STATE].astype(bf16)
    vbuf[8 : 8 + rows, :] = conv_pre
    sbuf[8 : 8 + rows, :] = state_all[:, : 2 * STATE]
    places = base + lax.broadcasted_iota(jnp.int32, (rows, 1), 0)
    start = start_of(places, ends)
    u = prm_ref[taps : taps + 1, :] + prm_ref[taps - 1 : taps, :] * conv_pre
    us = prs_ref[taps : taps + 1, :] + prs_ref[taps - 1 : taps, :] * state_all[:, : 2 * STATE]
    for lag in range(1, taps):
        usable = places - lag >= start
        tap = taps - 1 - lag
        u = u + prm_ref[tap : tap + 1, :] * jnp.where(usable, vbuf[8 - lag : 8 - lag + rows, :], 0.0)
        us = us + prs_ref[tap : tap + 1, :] * jnp.where(usable, sbuf[8 - lag : 8 - lag + rows, :], 0.0)
    vbuf[0:8, :] = vbuf[rows : rows + 8, :]
    sbuf[0:8, :] = sbuf[rows : rows + 8, :]
    u_ref[...] = u
    us_ref[...] = us
    raw = own_lanes(state_all[:, 2 * STATE :], first_ref[0], head_count) + prh_ref[0:1, :]
    raw_ref[...] = raw

    heads = head_matrix(channels)
    x = silu(u)
    maps_f = silu(us)
    maps = maps_f.astype(bf16)
    decay = prh_ref[1:2, :]
    row = lax.broadcasted_iota(jnp.int32, (SUB, SUB), 0)
    col = lax.broadcasted_iota(jnp.int32, (SUB, SUB), 1)
    for q in range(rows // SUB):
        at = slice(q * SUB, (q + 1) * SUB)
        low = base + q * SUB
        step, log_decay, cum, step_w, carried_w, keep_w, survive_w = scan_terms(
            raw[at], decay, low, ends, heads
        )
        cum_row = cum.T
        mask = (row >= col) & (segment_of(low + row, ends) == segment_of(low + col, ends))
        b_map, c_map = maps[at, :STATE], maps[at, STATE:]
        gram = jnp.where(mask, nt3(maps_f[at, STATE:], maps_f[at, :STATE]), 0.0)
        stepped = step_w * x[at]
        stepped_b = stepped.astype(bf16)
        state = carry[...]
        st_ref[q] = state
        outer = carried_w * nn3(maps_f[at, STATE:], state)
        for pair in range(channels // LANES):
            lanes = slice(pair * LANES, (pair + 1) * LANES)
            mixing = []
            for h in (2 * pair, 2 * pair + 1):
                spread = cum[:, h : h + 1] - cum_row[h : h + 1, :]
                mixing.append((jnp.exp2(jnp.minimum(spread, 0.0)) * gram).astype(bf16))
            inner = pair_product(mixing, stepped[:, lanes])
            y_ref[at, lanes] = inner + outer[:, lanes]
        carry[...] = survive_w * state + nn3(maps_f[at, :STATE].T, keep_w * stepped)


def value_kernel(place_ref, normed_ref, u_ref, y_ref, prm_ref, w_ref, gate_ref, ga_ref, square_ref, *refs, taps):
    rows, channels = gate_ref.shape
    gate_pre = nn(normed_ref[...], w_ref[:, :channels])
    gate_ref[...] = gate_pre
    y = y_ref[...] + prm_ref[taps + 1 : taps + 2, :] * silu(u_ref[...])
    g = y * silu(gate_pre)
    ga = (g * prm_ref[taps + 2 : taps + 3, :]).astype(bf16)
    ga_ref[...] = ga
    square = jnp.sum(g * g, axis=1, keepdims=True)
    square_ref[...] = jnp.broadcast_to(square, (rows, LANES)).T[:8, :]
    product = nt(ga, w_ref[:, channels:]).astype(bf16)
    put_halves(refs, place_ref[0, pl.program_id(0)], product)


def cotangent_kernel(place_ref, *refs, parts):
    part_refs, refs = refs[:parts], refs[parts:]
    w_ref, ga_ref, square_ref, gg_ref, sums_ref, cot_buf = refs
    rows = gg_ref.shape[0]
    cotangent = take_rows(part_refs, place_ref[0, pl.program_id(0)], cot_buf)
    grad_gated = nn(cotangent, w_ref[...])
    gg_ref[...] = grad_gated
    inner = jnp.sum(grad_gated * ga_ref[...].astype(f32), axis=1, keepdims=True)
    inner_row = jnp.broadcast_to(inner, (rows, LANES)).T[:8, :]
    sublane = lax.broadcasted_iota(jnp.int32, (8, rows), 0)
    sums_ref[...] = jnp.where(sublane == 0, square_ref[...], inner_row)


def gate_kernel(sums_ref, prm_ref, gate_ref, u_ref, y_ref, gg_ref, gated_ref, dgate_ref, dy_ref, dprm_ref, *, taps):
    rows = gate_ref.shape[0]

    @pl.when(pl.program_id(0) == 0)
    def _():
        dprm_ref[...] = jnp.zeros_like(dprm_ref)

    sums = jnp.concatenate([sums_ref[...], jnp.zeros((LANES - 8, rows), f32)], axis=0).T
    inverse = lax.rsqrt(sums[:, 0:1] * (1.0 / INNER) + EPS)
    inner_mean = sums[:, 1:2] * inverse * (1.0 / INNER)
    skip = prm_ref[taps + 1 : taps + 2, :]
    gain = prm_ref[taps + 2 : taps + 3, :]
    gate_pre = gate_ref[...]
    sig_gate = jax.nn.sigmoid(gate_pre)
    act = gate_pre * sig_gate
    x = silu(u_ref[...])
    y = y_ref[...] + skip * x
    hat = y * act * inverse
    gated_ref[...] = (hat * gain).astype(bf16)
    grad_gated = gg_ref[...]
    dprm_ref[taps + 2 : taps + 3, :] += jnp.sum(grad_gated * hat, axis=0, keepdims=True)
    grad_inner = inverse * (grad_gated * gain - hat * inner_mean)
    dy = grad_inner * act
    dgate_ref[...] = (grad_inner * y * sig_gate * (1.0 + gate_pre * (1.0 - sig_gate))).astype(bf16)
    dprm_ref[taps + 1 : taps + 2, :] += jnp.sum(dy * x, axis=0, keepdims=True)
    dy_ref[...] = dy


def gain_row(weights, grads):
    terms = jnp.sum(weights.astype(f32) * grads, axis=1, keepdims=True)
    return jnp.broadcast_to(terms, (terms.shape[0], LANES)).T[:8, :]


def first_weights_kernel(place_ref, *refs, parts):
    part_refs, refs = refs[:parts], refs[parts:]
    normed_ref, dgate_ref, gated_ref, w_ref, out_ref, gain_ref, cot_buf, total = refs
    channels = dgate_ref.shape[1]
    step_id = pl.program_id(0)

    @pl.when(step_id == 0)
    def _():
        total[...] = jnp.zeros_like(total)

    total[:, :channels] += tn(normed_ref[...], dgate_ref[...])
    cotangent = take_rows(part_refs, place_ref[0, step_id], cot_buf)
    total[:, channels:] += tn(cotangent, gated_ref[...])

    @pl.when(step_id == pl.num_programs(0) - 1)
    def _():
        out_ref[...] = total[...].astype(bf16)
        gain_ref[...] = gain_row(w_ref[...], total[:, :channels])


def last_weights_kernel(
    first_ref,
    normed_ref,
    gb_ref,
    w_ref,
    gain_ref,
    terms_ref,
    dprm_gate_ref,
    dprm_ref,
    dprs_ref,
    dprh_ref,
    out_ref,
    small_ref,
    total,
    *,
    taps,
):
    step_id = pl.program_id(0)
    channels = dprm_ref.shape[1]

    @pl.when(step_id == 0)
    def _():
        total[...] = jnp.zeros_like(total)

    total[...] += tn(normed_ref[...], gb_ref[...])

    @pl.when(step_id == pl.num_programs(0) - 1)
    def _():
        grads = total[...]
        out_ref[...] = grads.astype(bf16)
        terms = (gain_row(w_ref[...], grads) + terms_ref[...]) / gain_ref[...]
        row = lax.broadcasted_iota(jnp.int32, (8, 1), 0)
        both = jnp.where(row > taps, dprm_gate_ref[...], dprm_ref[...])
        skip = gather_heads(dprm_gate_ref[...], head_matrix(channels))
        by_head = jnp.where(row == 2, pltpu.roll(skip, 8 - (taps - 1), 0), dprh_ref[...])
        small_ref[...] = jnp.zeros_like(small_ref)
        small_ref[0:8, :channels] = both
        small_ref[0:8, channels : channels + 2 * STATE] = dprs_ref[...]
        small_ref[0:8, channels + 2 * STATE : channels + 2 * STATE + LANES] = pltpu.roll(
            by_head, first_ref[0], 1
        )
        small_ref[8:16, :] = terms


def backward_kernel(len_ref, first_ref, place_ref, *refs, seqs, taps, halves):
    (
        wg_ref,
        w_ref,
        prm_ref,
        prs_ref,
        prh_ref,
        dgate_ref,
        dy_ref,
        v_ref,
        u_ref,
        vs_ref,
        us_ref,
        raw_ref,
        y_ref,
        st_ref,
        gb_ref,
    ) = refs[:15]
    half_refs = refs[15 : 15 + halves]
    dprm_ref, dprs_ref, dprh_ref, dbuf, dsbuf, carry, ending = refs[15 + halves :]
    rows, channels = dgate_ref.shape
    step_id = pl.program_id(0)
    base = (pl.num_programs(0) - 1 - step_id) * rows
    ends = ends_of(len_ref, seqs)

    @pl.when(step_id == 0)
    def _():
        dbuf[rows : rows + 8, :] = jnp.zeros((8, channels), f32)
        dsbuf[rows : rows + 8, :] = jnp.zeros((8, 2 * STATE), f32)
        carry[...] = jnp.zeros_like(carry)
        ending[...] = jnp.zeros_like(ending)
        dprm_ref[...] = jnp.zeros_like(dprm_ref)
        dprs_ref[...] = jnp.zeros_like(dprs_ref)
        dprh_ref[...] = jnp.zeros_like(dprh_ref)

    def add_row(ref, at, z):
        ref[at : at + 1, :] += jnp.sum(z, axis=0, keepdims=True)

    skip = prm_ref[taps + 1 : taps + 2, :]
    u = u_ref[...]
    sig_u = jax.nn.sigmoid(u)
    x = u * sig_u
    y_scan = y_ref[...]
    dy_f = dy_ref[...]
    dy_b = dy_f.astype(bf16)

    heads = head_matrix(channels)
    us = us_ref[...]
    sig_us = jax.nn.sigmoid(us)
    maps_f = us * sig_us
    maps = maps_f.astype(bf16)
    raw = raw_ref[...]
    decay = prh_ref[1:2, :]
    row = lax.broadcasted_iota(jnp.int32, (SUB, SUB), 0)
    col = lax.broadcasted_iota(jnp.int32, (SUB, SUB), 1)
    upper = jnp.where(row <= col, 1.0, 0.0).astype(bf16)
    dxs, dmaps, draws = [], [], []
    for q in reversed(range(rows // SUB)):
        at = slice(q * SUB, (q + 1) * SUB)
        low = base + q * SUB
        step, log_decay, cum, step_w, carried_w, keep_w, survive_w = scan_terms(
            raw[at], decay, low, ends, heads
        )
        cum_row = cum.T
        mask = (row <= col) & (segment_of(low + row, ends) == segment_of(low + col, ends))
        b_map, c_map = maps[at, :STATE], maps[at, STATE:]
        gram = jnp.where(mask, nt3(maps_f[at, :STATE], maps_f[at, STATE:]), 0.0)
        stepped = step_w * x[at]
        stepped_b = stepped.astype(bf16)
        state = st_ref[q]
        dstate = carry[...]
        dstate_b = dstate.astype(bf16)
        dgram = jnp.zeros((SUB, SUB), f32)
        inner = []
        for pair in range(channels // LANES):
            lanes = slice(pair * LANES, (pair + 1) * LANES)
            dy_pair = dy_b[at, lanes]
            dmix = nt(pair_stack(stepped_b[:, lanes]), dy_pair)
            mixing = []
            for i, h in enumerate((2 * pair, 2 * pair + 1)):
                spread = cum_row[h : h + 1, :] - cum[:, h : h + 1]
                weight = jnp.exp2(jnp.minimum(spread, 0.0))
                mixing.append((weight * gram).astype(bf16))
                dgram = dgram + dmix[i * SUB : (i + 1) * SUB] * weight
            inner.append(pair_product(mixing, dy_f[at, lanes]))
        dstepped = jnp.concatenate(inner, axis=1) + keep_w * nn3(maps_f[at, :STATE], dstate)
        dgram = jnp.where(mask, dgram, 0.0).astype(bf16)
        dy_q = dy_f[at]
        dy_carried = (carried_w * dy_q).astype(bf16)
        db = nn(dgram, c_map) + nt((keep_w * stepped).astype(bf16), dstate_b)
        dc = tn(dgram, b_map) + nt(dy_carried, state.astype(bf16))
        dprev = survive_w * dstate + nn3(maps_f[at, STATE:].T, carried_w * dy_q)
        carry[...] = dprev
        balance = dy_q * y_scan[at] - stepped * dstepped
        state_end = ending[0:1, :]
        ending[0:1, :] = jnp.sum(state * dprev, axis=0, keepdims=True)
        by_head = gather_heads(
            jnp.concatenate(
                [balance, x[at] * dstepped, jnp.broadcast_to(state_end, (8, channels))], axis=0
            ),
            heads,
        )
        dlog = triangle_sum(upper, by_head[:SUB]) + by_head[2 * SUB : 2 * SUB + 1]
        dstep = by_head[SUB : 2 * SUB] - decay * dlog
        draw = dstep * jax.nn.sigmoid(raw[at])
        add_row(dprh_ref, 0, draw)
        add_row(dprh_ref, 1, dlog * log_decay)
        dxs.append(step_w * dstepped + skip * dy_q)
        dmaps.append(jnp.concatenate([db, dc], axis=1))
        draws.append(draw)
    dx = jnp.concatenate(dxs[::-1], axis=0)
    dmap = jnp.concatenate(dmaps[::-1], axis=0)
    draw = jnp.concatenate(draws[::-1], axis=0)
    du = dx * sig_u * (1.0 + u * (1.0 - sig_u))
    dus = dmap * sig_us * (1.0 + us * (1.0 - sig_us))
    dbuf[0:rows, :] = du
    dsbuf[0:rows, :] = dus
    v = v_ref[...].astype(f32)
    vs = vs_ref[...].astype(f32)
    places = base + lax.broadcasted_iota(jnp.int32, (rows, 1), 0)
    segment = segment_of(places, ends)
    dv = prm_ref[taps - 1 : taps, :] * du
    dvs = prs_ref[taps - 1 : taps, :] * dus
    add_row(dprm_ref, taps - 1, du * v)
    add_row(dprs_ref, taps - 1, dus * vs)
    add_row(dprm_ref, taps, du)
    add_row(dprs_ref, taps, dus)
    for lag in range(1, taps):
        usable = segment_of(places + lag, ends) == segment
        tap = taps - 1 - lag
        later = jnp.where(usable, dbuf[lag : lag + rows, :], 0.0)
        later_s = jnp.where(usable, dsbuf[lag : lag + rows, :], 0.0)
        dv = dv + prm_ref[tap : tap + 1, :] * later
        dvs = dvs + prs_ref[tap : tap + 1, :] * later_s
        add_row(dprm_ref, tap, later * v)
        add_row(dprs_ref, tap, later_s * vs)
    dbuf[rows : rows + 8, :] = dbuf[0:8, :]
    dsbuf[rows : rows + 8, :] = dsbuf[0:8, :]
    gb_ref[:, :channels] = dv.astype(bf16)
    gb_ref[:, channels : channels + 2 * STATE] = dvs.astype(bf16)
    gb_ref[:, channels + 2 * STATE :] = pltpu.roll(draw, first_ref[0], 1).astype(bf16)
    product = nt(dgate_ref[...], wg_ref[...]) + nt(gb_ref[...], w_ref[...])
    put_halves(half_refs, place_ref[0, step_id], product.astype(bf16))


def held(places):
    last = next(p for p in places if p is not None)
    filled = []
    for p in places:
        last = last if p is None else p
        filled.append(last)
    return filled


def place_table(tensor_place, quarter_blocks, order):
    relative = [(b // quarter_blocks) ^ tensor_place for b in order]
    inside = [b % quarter_blocks for b in order]

    def places(slots):
        return held(
            [slots.index(r) * quarter_blocks + w if r in slots else None for r, w in zip(relative, inside)]
        )

    return [
        relative,
        places([0]),
        places([1]),
        places([2]),
        places([3]),
        places([1, 3]),
        places([0, 2]),
        places([2, 3]),
        places([0, 1]),
    ]


def over_x(z):
    return lax.ppermute(z, "tensor", [(0, 1), (1, 0), (2, 3), (3, 2)])


def over_y(z):
    return lax.ppermute(z, "tensor", [(0, 2), (2, 0), (1, 3), (3, 1)])


def gather_start(z):
    return over_x(z), over_y(z)


def gather_end(z, from_x, from_y):
    half = z.shape[1] // 2
    return [z, from_x, from_y, over_y(from_x[:, :half]), over_x(from_y[:, half:])]


def scatter_start(halves):
    return over_x(halves[0]), over_y(halves[2])


def scatter_middle(halves, from_x, from_y, after=()):
    rows = from_x.shape[0] // 2
    left, right = halves[1], halves[3]
    left_far = left[rows:].astype(f32) + from_x[rows:].astype(f32)
    right_far = right[rows:].astype(f32) + from_y[rows:].astype(f32)
    far = (left_far.astype(bf16), right_far.astype(bf16))
    far, after = lax.optimization_barrier((far, after))
    return (over_y(far[0]), over_x(far[1])), after


def scatter_end(halves, from_x, from_y, far_left, far_right):
    rows = from_x.shape[0] // 2
    left, right = halves[1][:rows].astype(f32), halves[3][:rows].astype(f32)
    left = left + from_x[:rows].astype(f32) + far_left.astype(f32)
    right = right + from_y[:rows].astype(f32) + far_right.astype(f32)
    return jnp.concatenate([left, right], axis=1)


def sum_over_tensor(z):
    z = (z.astype(f32) + over_x(z).astype(f32)).astype(z.dtype)
    return z.astype(f32) + over_y(z).astype(f32)


def sum_over_dp(z):
    count = lax.axis_size("dp")
    bit = 1
    while bit < count:
        z = z + lax.ppermute(z, "dp", [(i, i ^ bit) for i in range(count)])
        bit *= 2
    return z


class Kernels:
    def __init__(self, lengths, first, tensor_place, tensor_count, group_rows, width, channels, taps, head_count):
        self.lengths, self.first = lengths, first
        self.tensor_place, self.tensor_count = tensor_place, tensor_count
        self.square = tensor_count == 4
        self.group_rows, self.width, self.channels = group_rows, width, channels
        self.taps, self.head_count = taps, head_count
        self.seqs = lengths.shape[1]

    def table(self, block, backwards=False):
        order = list(range(self.group_rows // block))
        if backwards:
            order = order[::-1]
        if not self.square:
            return jnp.asarray([order], jnp.int32)
        each = len(order) // 4
        tables = np.array([place_table(t, each, order) for t in range(4)], np.int32)
        return lax.dynamic_index_in_dim(jnp.asarray(tables), self.tensor_place, 0, keepdims=False)

    def call(self, kernel, scalars, block, ins, outs, scratch, flops, transcendentals=0):
        steps = self.group_rows // block
        specs, arrays = zip(*ins)
        out_specs, out_shapes = zip(*outs)
        return pl.pallas_call(
            kernel,
            grid_spec=pltpu.PrefetchScalarGridSpec(
                num_scalar_prefetch=len(scalars),
                grid=(steps,),
                in_specs=list(specs),
                out_specs=list(out_specs),
                scratch_shapes=scratch,
            ),
            out_shape=list(out_shapes),
            compiler_params=pltpu.CompilerParams(vmem_limit_bytes=56 * 2**20),
            cost_estimate=pl.CostEstimate(flops=1000, bytes_accessed=1000, transcendentals=0),
            name=getattr(kernel, "func", kernel).__name__,
        )(*scalars, *arrays)

    def whole(self, array):
        return pl.BlockSpec(array.shape, lambda i, *s: (0,) * len(array.shape)), array

    def columns(self, array, width, place):
        return pl.BlockSpec((array.shape[0], width), lambda i, *s: (0, place)), array

    def rows(self, array, block, backwards=False):
        last = self.group_rows // block - 1

        def at(i, *s):
            return (last - i if backwards else i,) + (0,) * (len(array.shape) - 1)

        size = array.shape[0] * block // self.group_rows
        return pl.BlockSpec((size,) + array.shape[1:], at), array

    def across(self, array, block):
        return pl.BlockSpec((8, block), lambda i, *s: (0, i)), array

    def out(self, columns, dtype):
        return jax.ShapeDtypeStruct((self.group_rows, columns), dtype)

    def parts(self, arrays, block):
        if not self.square:
            return [self.rows(arrays[0], block)]
        return [
            (pl.BlockSpec((block, z.shape[1]), lambda i, *s, k=k: (s[-1][k, i], 0)), z)
            for k, z in zip((1, 2, 3, 4, 4), arrays)
        ]

    def halves(self, block):
        half = self.width // 2
        if not self.square:
            return [
                (pl.BlockSpec((block, half), lambda i, *s: (s[-1][0, i], 0)), self.out(half, bf16))
                for _ in range(2)
            ]
        shape = jax.ShapeDtypeStruct((self.group_rows // 2, half), bf16)
        return [
            (pl.BlockSpec((block, half), lambda i, *s, k=k: (s[-1][k, i], 0)), shape) for k in (5, 6, 7, 8)
        ]

    def scan(self, hidden, weights, gain, prm, prs, prh):
        channels, count = self.channels, self.group_rows
        parts = self.parts(hidden, ROWS)
        outs = [
            self.out(self.width, bf16),
            self.out(channels, bf16),
            self.out(channels, f32),
            self.out(2 * STATE, bf16),
            self.out(2 * STATE, f32),
            self.out(LANES, f32),
            self.out(channels, f32),
            jax.ShapeDtypeStruct((count // SUB, STATE, channels), f32),
        ]
        return self.call(
            functools.partial(
                scan_kernel, parts=len(parts), seqs=self.seqs, taps=self.taps, head_count=self.head_count
            ),
            (self.lengths, self.first, self.table(ROWS)),
            ROWS,
            parts + [self.whole(z) for z in (weights, gain, prm, prs, prh)],
            [self.rows(z, ROWS) for z in outs],
            [
                pltpu.VMEM((ROWS, self.width), bf16),
                pltpu.VMEM((ROWS + 8, channels), f32),
                pltpu.VMEM((ROWS + 8, 2 * STATE), f32),
                pltpu.VMEM((STATE, channels), f32),
            ],
            count * self.width * channels * 8,
            count * channels * 8,
        )

    def value(self, normed, u, y, prm, weights):
        channels, count = self.channels, self.group_rows
        outs = [self.rows(self.out(channels, f32), WIDE_ROWS), self.rows(self.out(channels, bf16), WIDE_ROWS)]
        outs += [self.across(jax.ShapeDtypeStruct((8, count), f32), WIDE_ROWS)]
        result = self.call(
            functools.partial(value_kernel, taps=self.taps),
            (self.table(WIDE_ROWS),),
            WIDE_ROWS,
            [self.rows(z, WIDE_ROWS) for z in (normed, u, y)] + [self.whole(prm), self.whole(weights)],
            outs + self.halves(WIDE_ROWS),
            [],
            4 * count * self.width * channels,
        )
        return result[:3], result[3:]

    def cotangent(self, cotangent, weights, ga, square):
        channels, count = self.channels, self.group_rows
        parts = self.parts(cotangent, WIDE_ROWS)
        return self.call(
            functools.partial(cotangent_kernel, parts=len(parts)),
            (self.table(WIDE_ROWS),),
            WIDE_ROWS,
            parts
            + [
                self.columns(weights, channels, 1),
                self.rows(ga, WIDE_ROWS),
                self.across(square, WIDE_ROWS),
            ],
            [
                self.rows(self.out(channels, f32), WIDE_ROWS),
                self.across(jax.ShapeDtypeStruct((8, count), f32), WIDE_ROWS),
            ],
            [pltpu.VMEM((WIDE_ROWS, self.width), bf16)],
            2 * count * self.width * channels,
        )

    def gate(self, sums, prm, gate, u, y, gg):
        channels = self.channels
        return self.call(
            functools.partial(gate_kernel, taps=self.taps),
            (),
            WIDE_ROWS,
            [self.across(sums, WIDE_ROWS), self.whole(prm)] + [self.rows(z, WIDE_ROWS) for z in (gate, u, y, gg)],
            [self.rows(self.out(channels, bf16), WIDE_ROWS)] * 2
            + [self.rows(self.out(channels, f32), WIDE_ROWS)]
            + [self.whole(jax.ShapeDtypeStruct(prm.shape, f32))],
            [],
            self.group_rows * channels * 60,
        )

    def first_weights(self, cotangent, normed, dgate, gated, weights):
        channels = self.channels
        parts = self.parts(cotangent, WIDE_ROWS)
        return self.call(
            functools.partial(first_weights_kernel, parts=len(parts)),
            (self.table(WIDE_ROWS),),
            WIDE_ROWS,
            parts
            + [self.rows(z, WIDE_ROWS) for z in (normed, dgate, gated)]
            + [self.columns(weights, channels, 0)],
            [
                self.whole(jax.ShapeDtypeStruct((self.width, 2 * channels), bf16)),
                self.whole(jax.ShapeDtypeStruct((8, self.width), f32)),
            ],
            [pltpu.VMEM((WIDE_ROWS, self.width), bf16), pltpu.VMEM((self.width, 2 * channels), f32)],
            4 * self.group_rows * self.width * channels,
        )

    def last_weights(self, normed, gb, weights, gain, terms, dprm_gate, dprm, dprs, dprh):
        gradients = gb.shape[1]
        return self.call(
            functools.partial(last_weights_kernel, taps=self.taps),
            (self.first,),
            WIDE_ROWS,
            [self.rows(normed, WIDE_ROWS), self.rows(gb, WIDE_ROWS)]
            + [self.whole(z) for z in (weights, gain, terms, dprm_gate, dprm, dprs, dprh)],
            [
                self.whole(jax.ShapeDtypeStruct((self.width, gradients), bf16)),
                self.whole(jax.ShapeDtypeStruct((16, self.width), f32)),
            ],
            [pltpu.VMEM((self.width, gradients), f32)],
            2 * self.group_rows * self.width * gradients,
        )

    def backward(self, first_weights, weights, prm, prs, prh, saved):
        channels, count = self.channels, self.group_rows
        halves = self.halves(ROWS)
        result = self.call(
            functools.partial(backward_kernel, seqs=self.seqs, taps=self.taps, halves=len(halves)),
            (self.lengths, self.first, self.table(ROWS, True)),
            ROWS,
            [self.columns(first_weights, channels, 0)]
            + [self.whole(z) for z in (weights, prm, prs, prh)]
            + [self.rows(z, ROWS, True) for z in saved],
            [self.rows(self.out(channels + 3 * STATE, bf16), ROWS, True)]
            + halves
            + [self.whole(jax.ShapeDtypeStruct(z.shape, f32)) for z in (prm, prs, prh)],
            [
                pltpu.VMEM((ROWS + 8, channels), f32),
                pltpu.VMEM((ROWS + 8, 2 * STATE), f32),
                pltpu.VMEM((STATE, channels), f32),
                pltpu.VMEM((8, channels), f32),
            ],
            count * self.width * channels * 14,
            count * channels * 8,
        )
        return result[0], result[1 : 1 + len(halves)], result[1 + len(halves) :]


def per_device(
    hidden_in,
    norm_gain,
    proj_gate,
    proj_conv,
    proj_state,
    conv_kernel,
    conv_offset,
    state_kernel,
    state_offset,
    step_bias,
    decay_log,
    skip_gain,
    gate_gain,
    proj_out,
    out_cotangent,
    seq_lengths,
):
    tensor_count = lax.axis_size("tensor")
    tensor_place = lax.axis_index("tensor")
    dp_count = lax.axis_size("dp")
    dp_place = lax.axis_index("dp")
    square_mesh = tensor_count == 4
    own_rows, width = hidden_in.shape
    depth, channels = proj_gate.shape
    taps, heads_here, cut = conv_kernel.shape
    head_cut = step_bias.shape[0]
    state_cut = state_kernel.shape[1]
    state_width = proj_state.shape[1]
    group_rows = own_rows * tensor_count
    first_head = (tensor_place * heads_here).astype(jnp.int32)

    if square_mesh:
        hidden_all = gather_end(hidden_in, *gather_start(hidden_in))
    else:
        hidden_all = [lax.all_gather(hidden_in, "tensor", axis=0, tiled=True)]
    state_part = jnp.pad(proj_state, ((0, 0), (0, 3 * STATE - state_width)))
    weights = lax.all_gather(
        jnp.concatenate([proj_conv, state_part], axis=1), "dp", axis=0, tiled=True
    )
    first_weights = lax.all_gather(
        jnp.concatenate([proj_gate, proj_out.T], axis=1), "dp", axis=0, tiled=True
    )

    small = [
        norm_gain,
        conv_kernel,
        conv_offset,
        state_kernel,
        state_offset,
        step_bias,
        decay_log,
        skip_gain,
        gate_gain,
    ]
    flat = jnp.concatenate([z.reshape(-1) for z in small])
    flat = jnp.pad(flat, (0, -flat.shape[0] % 1024)).reshape(-1, LANES)
    small_all = lax.all_gather(flat, "dp", axis=0).reshape(dp_count, -1).astype(f32)
    shares, at = [], 0
    for z in small:
        shares.append(small_all[:, at : at + z.size].reshape((dp_count,) + z.shape))
        at += z.size
    gain_in = shares[0].reshape(1, width)
    taps_conv = shares[1].transpose(1, 2, 0, 3).reshape(taps, channels)
    off_conv = shares[2].transpose(1, 0, 2).reshape(1, channels)
    taps_state = shares[3].transpose(1, 0, 2).reshape(taps, 2 * STATE)
    off_state = shares[4].reshape(1, 2 * STATE)
    gain_gate = shares[8].transpose(1, 0, 2).reshape(1, channels)

    def own_heads(z):
        return lax.dynamic_slice_in_dim(z.reshape(-1), first_head, heads_here, 0)

    skip = jnp.repeat(own_heads(shares[7]), HEADDIM).reshape(1, channels)
    prm = jnp.concatenate([taps_conv, off_conv, skip, gain_gate], axis=0)
    prm = jnp.pad(prm, ((0, -prm.shape[0] % 8), (0, 0)))
    prs = jnp.concatenate([taps_state, off_state], axis=0)
    prs = jnp.pad(prs, ((0, -prs.shape[0] % 8), (0, 0)))
    prh = jnp.stack([own_heads(shares[5]), jnp.exp(own_heads(shares[6]))])
    prh = jnp.pad(prh, ((0, 6), (0, LANES - heads_here)))

    kernels = Kernels(
        seq_lengths,
        first_head.reshape(1),
        tensor_place,
        tensor_count,
        group_rows,
        width,
        channels,
        taps,
        heads_here,
    )

    hidden_all, cot = lax.optimization_barrier((hidden_all, out_cotangent))
    if square_mesh:
        moving = gather_start(cot)
    else:
        cotangent_all = [lax.all_gather(cot, "tensor", axis=0, tiled=True)]
    saved = kernels.scan(hidden_all, weights, gain_in, prm, prs, prh)
    if square_mesh:
        saved, moving = lax.optimization_barrier((saved, moving))
        cotangent_all = gather_end(cot, *moving)
    normed, v, u, vs, us, raw, y_scan, states = saved
    (gate_pre, ga, square), out_halves = kernels.value(normed, u, y_scan, prm, first_weights)
    if square_mesh:
        out_halves, cotangent_all = lax.optimization_barrier((out_halves, cotangent_all))
        moving = scatter_start(out_halves)
    gg, sums = kernels.cotangent(cotangent_all, first_weights, ga, square)
    if square_mesh:
        sums = sum_over_tensor(sums)
    else:
        sums = lax.psum(sums, "tensor")
    gated, dgate, dy, dprm_gate = kernels.gate(sums, prm, gate_pre, u, y_scan, gg)

    if square_mesh:
        gated, moving = lax.optimization_barrier((gated, moving))
        far, _ = scatter_middle(out_halves, *moving)
    grad_first, terms = kernels.first_weights(cotangent_all, normed, dgate, gated, first_weights)
    if square_mesh:
        grad_first, dy, far = lax.optimization_barrier((grad_first, dy, far))
        out_moving = moving + far
    own_first = lax.psum_scatter(grad_first, "dp", scatter_dimension=0, tiled=True)
    gb, gn_halves, small_grads = kernels.backward(
        first_weights, weights, prm, prs, prh, [dgate, dy, v, u, vs, us, raw, y_scan, states]
    )

    def own_sum(halves):
        return lax.psum_scatter(
            jnp.concatenate(halves, axis=1), "tensor", scatter_dimension=0, tiled=True
        ).astype(f32)

    if square_mesh:
        moving = scatter_start(gn_halves)
    grad_last, small_sum = kernels.last_weights(
        normed, gb, weights, gain_in, terms, dprm_gate, *small_grads
    )
    grad_last, own_first = lax.optimization_barrier((grad_last, own_first))
    own_last = lax.psum_scatter(grad_last, "dp", scatter_dimension=0, tiled=True)
    if square_mesh:
        small_sum, moving = lax.optimization_barrier((small_sum, moving))
        far, small_sum = scatter_middle(gn_halves, *moving, small_sum)
    small_sum = sum_over_dp(small_sum)
    small_shared = sum_over_tensor(small_sum) if square_mesh else lax.psum(small_sum, "tensor")

    if square_mesh:
        grad_normed = scatter_end(gn_halves, *moving, *far)
        branch = scatter_end(out_halves, *out_moving)
    else:
        grad_normed = own_sum(gn_halves)
        branch = own_sum(out_halves)

    own_square = lax.dynamic_slice_in_dim(sums[0], tensor_place * own_rows, own_rows, 0)
    inverse_gate = lax.rsqrt(own_square * (1.0 / INNER) + EPS)[:, None]
    values = hidden_in.astype(f32)
    block_out = (values + branch * inverse_gate).astype(bf16)

    inverse_in = lax.rsqrt(jnp.mean(values * values, axis=1, keepdims=True) + EPS)
    scaled = values * inverse_in
    grad_scaled = grad_normed * gain_in
    grad_hidden = out_cotangent.astype(f32) + inverse_in * (
        grad_scaled - scaled * jnp.mean(grad_scaled * scaled, axis=1, keepdims=True)
    )

    own_state = own_last[:, channels:]
    own_state = sum_over_tensor(own_state) if square_mesh else lax.psum(own_state.astype(f32), "tensor")
    own_part = depth // tensor_count
    own_state = lax.dynamic_slice_in_dim(own_state, tensor_place * own_part, own_part, 0)[:, :state_width]

    def own_cut(z, size, axis):
        return lax.dynamic_slice_in_dim(z, dp_place * size, size, axis)

    by_channel = small_sum[: taps + 3, :channels].reshape(taps + 3, heads_here, HEADDIM)
    by_channel = own_cut(by_channel, cut, 2)
    by_map = own_cut(small_shared[: taps + 1, channels : channels + 2 * STATE], state_cut, 1)
    heads_at = channels + 2 * STATE
    by_head = own_cut(small_shared[:3, heads_at : heads_at + LANES], head_cut, 1)
    gain_grad = lax.dynamic_slice_in_dim(
        small_shared[8], (dp_place * tensor_count + tensor_place) * own_part, own_part, 0
    )
    own_first = own_first.astype(f32)
    return (
        block_out,
        grad_hidden,
        gain_grad,
        own_first[:, :channels],
        own_last[:, :channels].astype(f32),
        own_state,
        own_first[:, channels:].T,
        by_channel[:taps],
        by_channel[taps],
        by_map[:taps],
        by_map[taps],
        by_head[0],
        by_head[1],
        by_head[2],
        by_channel[taps + 2],
    )


def solution(mesh):
    placed = (
        P(("dp", "tensor"), None),
        P("dp"),
        P("dp", "tensor"),
        P("dp", "tensor"),
        P("dp", None),
        P(None, "tensor", "dp"),
        P("tensor", "dp"),
        P(None, "dp"),
        P("dp"),
        P("dp"),
        P("dp"),
        P("dp"),
        P("tensor", "dp"),
        P("tensor", "dp"),
        P(("dp", "tensor"), None),
        P("dp", None),
    )
    return jax.shard_map(
        per_device,
        mesh=mesh,
        in_specs=placed,
        out_specs=(
            P(("dp", "tensor"), None),
            P(("dp", "tensor"), None),
            P(("dp", "tensor")),
            P("dp", "tensor"),
            P("dp", "tensor"),
            P(("dp", "tensor"), None),
            P("tensor", "dp"),
            P(None, "tensor", "dp"),
            P("tensor", "dp"),
            P(None, "dp"),
            P("dp"),
            P("dp"),
            P("dp"),
            P("dp"),
            P("tensor", "dp"),
        ),
        check_vma=False,
    )
```

```python
import functools

import jax
import jax.numpy as jnp
import numpy as np
from jax import lax
from jax.experimental import pallas as pl
from jax.experimental.pallas import tpu as pltpu
from jax.sharding import PartitionSpec as P

HEADDIM = 64
STATE = 128
INNER = 2048
LANES = 128
ROWS = 256
WIDE_ROWS = 512
FIELD = 32
SUB = 128
EPS = 1e-05
LOG2E = 1.4426950408889634

f32 = jnp.float32
bf16 = jnp.bfloat16


def nn(a, b):
    return lax.dot_general(a, b, (((1,), (0,)), ((), ())), preferred_element_type=f32)


def nt(a, b):
    return lax.dot_general(a, b, (((1,), (1,)), ((), ())), preferred_element_type=f32)


def tn(a, b):
    return lax.dot_general(a, b, (((0,), (0,)), ((), ())), preferred_element_type=f32)


def pieces(z, count):
    parts = []
    for _ in range(count - 1):
        part = z.astype(bf16)
        parts.append(part)
        z = z - part.astype(f32)
    parts.append(z.astype(bf16))
    return parts


def spread_heads(z, heads):
    return nn(jnp.concatenate(pieces(z, 2), axis=1), heads)


def gather_heads(z, heads):
    return nn(jnp.concatenate(pieces(z, 2), axis=1), heads)


def triangle_sum(triangle, z):
    return nn(triangle, jnp.concatenate(pieces(z, 3), axis=0))


def constants(channels):
    row, col = np.arange(ROWS)[:, None], np.arange(ROWS)[None, :]
    same = row // SUB == col // SUB
    lower = np.concatenate([same & (row >= col)] * 3, axis=1)
    upper = np.concatenate([same & (row <= col)] * 3, axis=1)
    heads = np.arange(LANES)[:, None] == np.arange(channels)[None, :] // HEADDIM
    spread = np.concatenate([heads] * 2, axis=0)
    gather = np.concatenate([heads.T] * 2, axis=0)
    return [jnp.asarray(z, bf16) for z in (lower, upper, spread, gather)]


def ends_of(len_ref, count):
    ends, total = [], 0
    for s in range(count):
        total = total + len_ref[0, s]
        ends.append(total)
    return ends


def segment_of(places, ends):
    return sum((places >= end).astype(jnp.int32) for end in ends)


def start_of(places, ends):
    start = jnp.zeros_like(places)
    for end in ends:
        start = jnp.where(places >= end, end, start)
    return start


def scan_steps(raw, decay, lower):
    step = jnp.maximum(raw, 0.0) + jnp.log1p(jnp.exp(-jnp.abs(raw)))
    return step, triangle_sum(lower, -decay * step)


def scan_weights(step, cum, base, ends, spread):
    rows = step.shape[0]
    segment = segment_of(base + lax.broadcasted_iota(jnp.int32, (rows, 1), 0), ends)
    carried, keep, survive = [], [], []
    for low in range(0, rows, SUB):
        before = segment_of(base + low - 1, ends)
        tail = segment_of(base + low + SUB - 1, ends)
        part, own = cum[low : low + SUB], segment[low : low + SUB]
        last = part[SUB - 1 :]
        carried.append(jnp.where(own == before, jnp.exp(part), 0.0))
        keep.append(jnp.where(own == tail, jnp.exp(last - part), 0.0))
        survive.append(jnp.where(tail == before, jnp.exp(last), 0.0))
    survive.append(jnp.zeros((-len(survive) % 8, LANES), f32))
    wide = spread_heads(jnp.concatenate([step] + carried + keep + survive, axis=0), spread)
    return wide[:rows], wide[rows : 2 * rows], wide[2 * rows : 3 * rows], wide[3 * rows :]


def pair_stack(z):
    lane = lax.broadcasted_iota(jnp.int32, z.shape, 1)
    zero = jnp.zeros_like(z)
    return jnp.concatenate(
        [jnp.where(lane < HEADDIM, z, zero), jnp.where(lane >= HEADDIM, z, zero)], axis=0
    )


def silu(u):
    return u * jax.nn.sigmoid(u)


def own_lanes(z, shift, count):
    moved = pltpu.roll(z, (z.shape[1] - shift) % z.shape[1], 1)
    lane = lax.broadcasted_iota(jnp.int32, z.shape, 1)
    return jnp.where(lane < count, moved, 0.0)


def nn3(a, b):
    a, a_low = pieces(a, 2)
    b, b_low = pieces(b, 2)
    return nn(jnp.concatenate([a, a_low, a], axis=1), jnp.concatenate([b, b, b_low], axis=0))


def nt3(a, b):
    a, a_low = pieces(a, 2)
    b, b_low = pieces(b, 2)
    return nt(jnp.concatenate([a, a_low, a], axis=1), jnp.concatenate([b, b, b_low], axis=1))


def pair_product(mixing, z):
    high, low = pieces(z, 2)
    both = nn(
        jnp.concatenate(mixing, axis=1),
        jnp.concatenate([pair_stack(high), pair_stack(low)], axis=1),
    )
    return both[:, :LANES] + both[:, LANES:]


def take_rows(refs, which, buffer):
    if len(refs) == 1:
        return refs[0][...]
    half = refs[3].shape[1]
    for k in range(3):

        @pl.when(which == k)
        def _(k=k):
            buffer[...] = refs[k][...]

    @pl.when(which == 3)
    def _():
        buffer[:, :half] = refs[3][...]
        buffer[:, half:] = refs[4][...]

    return buffer[...]


def put_halves(refs, which, product):
    half = product.shape[1] // 2
    left, right = product[:, :half], product[:, half:]
    if len(refs) == 2:
        refs[0][...] = left
        refs[1][...] = right
        return
    left_sent, left_kept, right_sent, right_kept = refs

    @pl.when(which % 2 == 1)
    def _():
        left_sent[...] = left

    @pl.when(which % 2 == 0)
    def _():
        left_kept[...] = left

    @pl.when(which >= 2)
    def _():
        right_sent[...] = right

    @pl.when(which < 2)
    def _():
        right_kept[...] = right


def scan_kernel(
    len_ref, first_ref, place_ref, *refs, parts, seqs, taps, head_count, first_block, kept, starts, place_at
):
    part_refs, refs = refs[:parts], refs[parts:]
    w_ref, gain_ref, prm_ref, prs_ref, prh_ref, lower_ref, spread_ref = refs[:7]
    start_refs, refs = refs[7 : 7 + starts], refs[7 + starts :]
    (
        normed_ref,
        v_ref,
        u_ref,
        vs_ref,
        us_ref,
        terms_ref,
        y_ref,
        st_ref,
        gate_ref,
        ga_ref,
        total_ref,
        square_ref,
        vtail_out,
        stail_out,
        carry,
        hid_buf,
        vbuf,
        sbuf,
    ) = refs[kept:]
    rows, channels = v_ref.shape
    step_id = pl.program_id(0)
    block = step_id + first_block
    base = block * rows
    ends = ends_of(len_ref, seqs)

    @pl.when(step_id == 0)
    def _():
        if start_refs:
            vbuf[0:8, :] = start_refs[0][...]
            sbuf[0:8, :] = start_refs[1][...]
            carry[...] = start_refs[2][...]
        else:
            vbuf[0:8, :] = jnp.zeros((8, channels), f32)
            sbuf[0:8, :] = jnp.zeros((8, 2 * STATE), f32)
            carry[...] = jnp.zeros_like(carry)

    values = take_rows(part_refs, place_ref[place_at + block], hid_buf).astype(f32)
    inverse = lax.rsqrt(jnp.mean(values * values, axis=1, keepdims=True) + EPS)
    normed = (values * inverse * gain_ref[...]).astype(bf16)
    normed_ref[...] = normed
    gate_pre = nn(normed, w_ref[:, :channels])
    gate_ref[...] = gate_pre.astype(bf16)
    conv_pre = nn(normed, w_ref[:, channels : 2 * channels])
    state_all = nn(normed, w_ref[:, 2 * channels :])
    v_ref[...] = conv_pre.astype(bf16)
    vs_ref[...] = state_all[:, : 2 * STATE].astype(bf16)
    vbuf[8 : 8 + rows, :] = conv_pre
    sbuf[8 : 8 + rows, :] = state_all[:, : 2 * STATE]
    start = start_of(base + lax.broadcasted_iota(jnp.int32, (rows, 1), 0), ends)
    u = prm_ref[taps : taps + 1, :] + prm_ref[taps - 1 : taps, :] * conv_pre
    us = prs_ref[taps : taps + 1, :] + prs_ref[taps - 1 : taps, :] * state_all[:, : 2 * STATE]
    for lag in range(1, taps):
        usable = base + lax.broadcasted_iota(jnp.int32, (rows, 1), 0) - lag >= start
        tap = taps - 1 - lag
        u = u + prm_ref[tap : tap + 1, :] * jnp.where(usable, vbuf[8 - lag : 8 - lag + rows, :], 0.0)
        us = us + prs_ref[tap : tap + 1, :] * jnp.where(usable, sbuf[8 - lag : 8 - lag + rows, :], 0.0)
    vbuf[0:8, :] = vbuf[rows : rows + 8, :]
    sbuf[0:8, :] = sbuf[rows : rows + 8, :]
    vtail_out[...] = vbuf[0:8, :]
    stail_out[...] = sbuf[0:8, :]
    u_ref[...] = u
    us_ref[...] = us
    raw = own_lanes(state_all[:, 2 * STATE :], first_ref[0], head_count) + prh_ref[0:1, :]

    x = silu(u)
    maps = silu(us)
    step, cum = scan_steps(raw, prh_ref[1:2, :], lower_ref[...])
    lane = lax.broadcasted_iota(jnp.int32, (rows, LANES), 1)
    terms_ref[...] = jnp.where(
        lane < FIELD,
        step,
        jnp.where(lane < 2 * FIELD, pltpu.roll(raw, FIELD, 1), pltpu.roll(cum, 2 * FIELD, 1)),
    )
    step_w, carried_w, keep_w, survive_w = scan_weights(step, cum, base, ends, spread_ref[...])
    cum = cum * LOG2E
    cum_row = cum.T
    stepped = step_w * x
    kept_b = keep_w * stepped
    row = lax.broadcasted_iota(jnp.int32, (SUB, SUB), 0)
    col = lax.broadcasted_iota(jnp.int32, (SUB, SUB), 1)
    state = carry[...]
    y_parts = []
    for q in range(rows // SUB):
        at = slice(q * SUB, (q + 1) * SUB)
        low = base + q * SUB
        mask = (row >= col) & (segment_of(low + row, ends) == segment_of(low + col, ends))
        b_map, c_map = maps[at, :STATE], maps[at, STATE:]
        gram = jnp.where(mask, nt3(c_map, b_map), 0.0)
        st_ref[q] = state
        outer = carried_w[at] * nn3(c_map, state)
        inner = []
        for pair in range(channels // LANES):
            mixing = []
            for h in (2 * pair, 2 * pair + 1):
                spread = cum[at, h : h + 1] - cum_row[h : h + 1, at]
                mixing.append((jnp.exp2(jnp.minimum(spread, 0.0)) * gram).astype(bf16))
            inner.append(pair_product(mixing, stepped[at, pair * LANES : (pair + 1) * LANES]))
        y_parts.append(jnp.concatenate(inner, axis=1) + outer)
        state = survive_w[q : q + 1] * state + nn3(b_map.T, kept_b[at])
    carry[...] = state
    y_scan = jnp.concatenate(y_parts, axis=0)
    y_ref[...] = y_scan
    y_total = y_scan + prm_ref[taps + 1 : taps + 2, :] * x
    total_ref[...] = y_total.astype(bf16)
    g = y_total * silu(gate_pre)
    ga_ref[...] = (g * prm_ref[taps + 2 : taps + 3, :]).astype(bf16)
    square = jnp.sum(g * g, axis=1, keepdims=True)
    square_ref[...] = jnp.broadcast_to(square, (rows, LANES)).T[:8, :]


def product_kernel(place_ref, ga_ref, w_ref, *refs, place_at):
    product = nt(ga_ref[...], w_ref[...]).astype(bf16)
    put_halves(refs, place_ref[place_at + pl.program_id(0)], product)


def cotangent_kernel(place_ref, *refs, parts, place_at):
    part_refs, refs = refs[:parts], refs[parts:]
    w_ref, ga_ref, square_ref, gg_ref, sums_ref, cot_buf = refs
    rows = gg_ref.shape[0]
    cotangent = take_rows(part_refs, place_ref[place_at + pl.program_id(0)], cot_buf)
    grad_gated = nn(cotangent, w_ref[...])
    gg_ref[...] = grad_gated.astype(bf16)
    inner = jnp.sum(grad_gated * ga_ref[...].astype(f32), axis=1, keepdims=True)
    inner_row = jnp.broadcast_to(inner, (rows, LANES)).T[:8, :]
    sublane = lax.broadcasted_iota(jnp.int32, (8, rows), 0)
    sums_ref[...] = jnp.where(sublane == 0, square_ref[...], inner_row)


def gain_row(weights, grads):
    terms = jnp.sum(weights.astype(f32) * grads, axis=1, keepdims=True)
    return jnp.broadcast_to(terms, (terms.shape[0], LANES)).T[:8, :]


def gate_kernel(place_ref, *refs, parts, taps, place_at):
    part_refs, refs = refs[:parts], refs[parts:]
    (
        sums_ref,
        prm_ref,
        w_ref,
        gate_ref,
        y_ref,
        gg_ref,
        normed_ref,
        dgate_ref,
        dy_ref,
        dprm_ref,
        out_ref,
        gain_ref,
        cot_buf,
        total,
    ) = refs
    rows, channels = gate_ref.shape
    step_id = pl.program_id(0)

    @pl.when(step_id == 0)
    def _():
        dprm_ref[...] = jnp.zeros_like(dprm_ref)
        total[...] = jnp.zeros_like(total)

    sums = jnp.concatenate([sums_ref[...], jnp.zeros((LANES - 8, rows), f32)], axis=0).T
    inverse = lax.rsqrt(sums[:, 0:1] * (1.0 / INNER) + EPS)
    inner_mean = sums[:, 1:2] * inverse * (1.0 / INNER)
    gain = prm_ref[taps + 2 : taps + 3, :]
    gate_pre = gate_ref[...].astype(f32)
    sig_gate = jax.nn.sigmoid(gate_pre)
    act = gate_pre * sig_gate
    y = y_ref[...].astype(f32)
    hat = y * act * inverse
    gated = (hat * gain).astype(bf16)
    grad_gated = gg_ref[...].astype(f32)
    dprm_ref[taps + 2 : taps + 3, :] += jnp.sum(grad_gated * hat, axis=0, keepdims=True)
    grad_inner = inverse * (grad_gated * gain - hat * inner_mean)
    dy = grad_inner * act
    dgate = (grad_inner * y * sig_gate * (1.0 + gate_pre * (1.0 - sig_gate))).astype(bf16)
    dgate_ref[...] = dgate
    dy_ref[...] = dy
    total[:, :channels] += tn(normed_ref[...], dgate)
    cotangent = take_rows(part_refs, place_ref[place_at + step_id], cot_buf)
    total[:, channels:] += tn(cotangent, gated)

    @pl.when(step_id == pl.num_programs(0) - 1)
    def _():
        out_ref[...] = total[...].astype(bf16)
        gain_ref[...] = gain_row(w_ref[...], total[:, :channels])


def backward_kernel(len_ref, first_ref, place_ref, *refs, seqs, taps, halves, place_at):
    (
        w_ref,
        gain_ref,
        terms_ref,
        dprm_gate_ref,
        prm_ref,
        prs_ref,
        prh_ref,
        upper_ref,
        spread_ref,
        gather_ref,
        normed_ref,
        dgate_ref,
        dy_ref,
        v_ref,
        u_ref,
        vs_ref,
        us_ref,
        scan_ref,
        y_ref,
        st_ref,
    ) = refs[:20]
    half_refs = refs[20 : 20 + halves]
    out_ref, small_ref, dprm_ref, dprs_ref, dprh_ref, dbuf, dsbuf, carry, ending, gb_ref, total = refs[20 + halves :]
    rows, channels = dgate_ref.shape
    step_id = pl.program_id(0)
    base = (pl.num_programs(0) - 1 - step_id) * rows
    ends = ends_of(len_ref, seqs)

    @pl.when(step_id == 0)
    def _():
        dbuf[rows : rows + 8, :] = jnp.zeros((8, channels), f32)
        dsbuf[rows : rows + 8, :] = jnp.zeros((8, 2 * STATE), f32)
        carry[...] = jnp.zeros_like(carry)
        ending[...] = jnp.zeros_like(ending)
        dprm_ref[...] = jnp.zeros_like(dprm_ref)
        dprs_ref[...] = jnp.zeros_like(dprs_ref)
        dprh_ref[...] = jnp.zeros_like(dprh_ref)
        total[...] = jnp.zeros_like(total)

    def add_row(ref, at, z):
        ref[at : at + 1, :] += jnp.sum(z, axis=0, keepdims=True)

    skip = prm_ref[taps + 1 : taps + 2, :]
    u = u_ref[...]
    sig_u = jax.nn.sigmoid(u)
    x = u * sig_u
    y_scan = y_ref[...]
    dy = dy_ref[...]
    dy_b = dy.astype(bf16)

    add_row(dprm_ref, taps + 1, dy * x)
    us = us_ref[...]
    sig_us = jax.nn.sigmoid(us)
    maps = us * sig_us
    maps_b = maps.astype(bf16)
    terms = scan_ref[...]
    lane = lax.broadcasted_iota(jnp.int32, (rows, LANES), 1)
    inside = lane < FIELD
    step = jnp.where(inside, terms, 0.0)
    raw = jnp.where(inside, pltpu.roll(terms, LANES - FIELD, 1), 0.0)
    cum = jnp.where(inside, pltpu.roll(terms, LANES - 2 * FIELD, 1), 0.0)
    decay = prh_ref[1:2, :]
    step_w, carried_w, keep_w, survive_w = scan_weights(step, cum, base, ends, spread_ref[...])
    cum = cum * LOG2E
    cum_row = cum.T
    stepped = step_w * x
    stepped_b = stepped.astype(bf16)
    kept_b = (keep_w * stepped).astype(bf16)
    dy_carried = carried_w * dy
    dy_carried_b = dy_carried.astype(bf16)
    row = lax.broadcasted_iota(jnp.int32, (SUB, SUB), 0)
    col = lax.broadcasted_iota(jnp.int32, (SUB, SUB), 1)
    dstate = carry[...]
    state_end = ending[0:1, :]
    subs = rows // SUB
    dsteppeds, dmaps, state_ends = [None] * subs, [None] * subs, [None] * subs
    for q in reversed(range(subs)):
        at = slice(q * SUB, (q + 1) * SUB)
        low = base + q * SUB
        mask = (row <= col) & (segment_of(low + row, ends) == segment_of(low + col, ends))
        b_map, c_map = maps[at, :STATE], maps[at, STATE:]
        gram = jnp.where(mask, nt3(b_map, c_map), 0.0)
        state = st_ref[q]
        dstate_b = dstate.astype(bf16)
        dgram = jnp.zeros((SUB, SUB), f32)
        inner = []
        for pair in range(channels // LANES):
            lanes = slice(pair * LANES, (pair + 1) * LANES)
            dmix = nt(pair_stack(stepped_b[at, lanes]), dy_b[at, lanes])
            mixing = []
            for i, h in enumerate((2 * pair, 2 * pair + 1)):
                spread = cum_row[h : h + 1, at] - cum[at, h : h + 1]
                weight = jnp.exp2(jnp.minimum(spread, 0.0))
                mixing.append((weight * gram).astype(bf16))
                dgram = dgram + dmix[i * SUB : (i + 1) * SUB] * weight
            inner.append(pair_product(mixing, dy[at, lanes]))
        dsteppeds[q] = jnp.concatenate(inner, axis=1) + keep_w[at] * nn3(b_map, dstate)
        dgram = jnp.where(mask, dgram, 0.0).astype(bf16)
        db = nn(dgram, maps_b[at, STATE:]) + nt(kept_b[at], dstate_b)
        dc = tn(dgram, maps_b[at, :STATE]) + nt(dy_carried_b[at], state.astype(bf16))
        dmaps[q] = jnp.concatenate([db, dc], axis=1)
        state_ends[q] = state_end
        dstate = survive_w[q : q + 1] * dstate + nn3(c_map.T, dy_carried[at])
        state_end = jnp.sum(state * dstate, axis=0, keepdims=True)
    carry[...] = dstate
    ending[0:1, :] = state_end
    dstepped = jnp.concatenate(dsteppeds, axis=0)
    dmap = jnp.concatenate(dmaps, axis=0)
    state_ends.append(jnp.zeros((-subs % 8, channels), f32))
    by_head = gather_heads(
        jnp.concatenate([dy * y_scan - stepped * dstepped, x * dstepped] + state_ends, axis=0),
        gather_ref[...],
    )
    dlog = triangle_sum(upper_ref[...], by_head[:rows])
    dlog = jnp.concatenate(
        [
            dlog[q * SUB : (q + 1) * SUB] + by_head[2 * rows + q : 2 * rows + q + 1]
            for q in range(subs)
        ],
        axis=0,
    )
    draw = (by_head[rows : 2 * rows] - decay * dlog) * jax.nn.sigmoid(raw)
    add_row(dprh_ref, 0, draw)
    add_row(dprh_ref, 1, dlog * step * -decay)
    du = (step_w * dstepped + skip * dy) * sig_u * (1.0 + u * (1.0 - sig_u))
    dus = dmap * sig_us * (1.0 + us * (1.0 - sig_us))
    dbuf[0:rows, :] = du
    dsbuf[0:rows, :] = dus
    v = v_ref[...].astype(f32)
    vs = vs_ref[...].astype(f32)
    places = base + lax.broadcasted_iota(jnp.int32, (rows, 1), 0)
    segment = segment_of(places, ends)
    dv = prm_ref[taps - 1 : taps, :] * du
    dvs = prs_ref[taps - 1 : taps, :] * dus
    add_row(dprm_ref, taps - 1, du * v)
    add_row(dprs_ref, taps - 1, dus * vs)
    add_row(dprm_ref, taps, du)
    add_row(dprs_ref, taps, dus)
    for lag in range(1, taps):
        usable = segment_of(places + lag, ends) == segment
        tap = taps - 1 - lag
        later = jnp.where(usable, dbuf[lag : lag + rows, :], 0.0)
        later_s = jnp.where(usable, dsbuf[lag : lag + rows, :], 0.0)
        dv = dv + prm_ref[tap : tap + 1, :] * later
        dvs = dvs + prs_ref[tap : tap + 1, :] * later_s
        add_row(dprm_ref, tap, later * v)
        add_row(dprs_ref, tap, later_s * vs)
    dbuf[rows : rows + 8, :] = dbuf[0:8, :]
    dsbuf[rows : rows + 8, :] = dsbuf[0:8, :]
    gb_ref[:, :channels] = dv.astype(bf16)
    gb_ref[:, channels : channels + 2 * STATE] = dvs.astype(bf16)
    gb_ref[:, channels + 2 * STATE :] = pltpu.roll(draw, first_ref[0], 1).astype(bf16)
    product = nt(dgate_ref[...], w_ref[:, :channels]) + nt(gb_ref[...], w_ref[:, channels:])
    put_halves(half_refs, place_ref[place_at + step_id], product.astype(bf16))
    total[...] += tn(normed_ref[...], gb_ref[...])

    @pl.when(step_id == pl.num_programs(0) - 1)
    def _():
        grads = total[...]
        out_ref[...] = grads.astype(bf16)
        gains = (gain_row(w_ref[:, channels:], grads) + terms_ref[...]) / gain_ref[...]
        line = lax.broadcasted_iota(jnp.int32, (8, 1), 0)
        both = jnp.where(line == taps + 2, dprm_gate_ref[...], dprm_ref[...])
        skips = gather_heads(dprm_ref[...], gather_ref[...])
        by_head = jnp.where(line == 2, pltpu.roll(skips, 8 - (taps - 1), 0), dprh_ref[...])
        small_ref[...] = jnp.zeros_like(small_ref)
        small_ref[0:8, :channels] = both
        small_ref[0:8, channels : channels + 2 * STATE] = dprs_ref[...]
        small_ref[0:8, channels + 2 * STATE : channels + 2 * STATE + LANES] = pltpu.roll(
            by_head, first_ref[0], 1
        )
        small_ref[8:16, :] = gains


def held(places):
    last = next(p for p in places if p is not None)
    filled = []
    for p in places:
        last = last if p is None else p
        filled.append(last)
    return filled


def place_table(tensor_place, quarter_blocks, order):
    relative = [(b // quarter_blocks) ^ tensor_place for b in order]
    inside = [b % quarter_blocks for b in order]

    def places(slots):
        return held(
            [slots.index(r) * quarter_blocks + w if r in slots else None for r, w in zip(relative, inside)]
        )

    return [
        relative,
        places([0]),
        places([1]),
        places([2]),
        places([3]),
        places([1, 3]),
        places([0, 2]),
        places([2, 3]),
        places([0, 1]),
    ]


def over_x(z):
    return lax.ppermute(z, "tensor", [(0, 1), (1, 0), (2, 3), (3, 2)])


def over_y(z):
    return lax.ppermute(z, "tensor", [(0, 2), (2, 0), (1, 3), (3, 1)])


def gather_start(z):
    return over_x(z), over_y(z)


def gather_end(z, from_x, from_y, after=()):
    half = z.shape[1] // 2
    far = (from_x[:, :half], from_y[:, half:])
    far, after = lax.optimization_barrier((far, after))
    return [z, from_x, from_y, over_y(far[0]), over_x(far[1])], after


def scatter_start(halves):
    return over_x(halves[0]), over_y(halves[2])


def scatter_middle(halves, from_x, from_y, after=()):
    rows = from_x.shape[0] // 2
    left, right = halves[1], halves[3]
    left_far = left[rows:].astype(f32) + from_x[rows:].astype(f32)
    right_far = right[rows:].astype(f32) + from_y[rows:].astype(f32)
    far = (left_far.astype(bf16), right_far.astype(bf16))
    far, after = lax.optimization_barrier((far, after))
    return (over_y(far[0]), over_x(far[1])), after


def scatter_end(halves, from_x, from_y, far_left, far_right):
    rows = from_x.shape[0] // 2
    left, right = halves[1][:rows].astype(f32), halves[3][:rows].astype(f32)
    left = left + from_x[:rows].astype(f32) + far_left.astype(f32)
    right = right + from_y[:rows].astype(f32) + far_right.astype(f32)
    return jnp.concatenate([left, right], axis=1)


def sum_over_tensor(z):
    z = (z.astype(f32) + over_x(z).astype(f32)).astype(z.dtype)
    return z.astype(f32) + over_y(z).astype(f32)


def sum_over_dp(z):
    count = lax.axis_size("dp")
    bit = 1
    while bit < count:
        z = z + lax.ppermute(z, "dp", [(i, i ^ bit) for i in range(count)])
        bit *= 2
    return z


class Kernels:
    def __init__(self, lengths, first, tensor_place, tensor_count, group_rows, width, channels, taps, head_count):
        self.lengths, self.first = lengths, first
        self.tensor_place, self.tensor_count = tensor_place, tensor_count
        self.square = tensor_count == 4
        self.group_rows, self.width, self.channels = group_rows, width, channels
        self.taps, self.head_count = taps, head_count
        self.seqs = lengths.shape[1]
        self.lower, self.upper, self.spread, self.gather = constants(channels)
        self.tables()

    def tables(self):
        kinds = ((ROWS, False), (ROWS, True), (WIDE_ROWS, False))
        self.kinds = {kind: k for k, kind in enumerate(kinds)}
        places = range(4) if self.square else range(1)
        made = []
        for t in places:
            lines = []
            for block, backwards in kinds:
                order = list(range(self.group_rows // block))[:: -1 if backwards else 1]
                table = place_table(t, len(order) // 4, order) if self.square else [order]
                lines += [line + [0] * (self.group_rows // ROWS - len(order)) for line in table]
            made.append(lines)
        self.lines = len(made[0]) // len(kinds)
        made = jnp.asarray(np.array(made, np.int32).reshape(len(made), -1))
        place = self.tensor_place if self.square else 0
        self.place = lax.dynamic_index_in_dim(made, place, 0, keepdims=False)
        self.steps = self.group_rows // ROWS

    def at(self, block, backwards, line):
        return (self.kinds[(block, backwards)] * self.lines + line) * self.steps

    def call(self, kernel, scalars, steps, ins, outs, scratch, aliases=None):
        specs, arrays = zip(*ins)
        out_specs, out_shapes = zip(*outs)
        return pl.pallas_call(
            kernel,
            grid_spec=pltpu.PrefetchScalarGridSpec(
                num_scalar_prefetch=len(scalars),
                grid=(steps,),
                in_specs=list(specs),
                out_specs=list(out_specs),
                scratch_shapes=scratch,
            ),
            out_shape=list(out_shapes),
            input_output_aliases=aliases or {},
            compiler_params=pltpu.CompilerParams(vmem_limit_bytes=56 * 2**20),
            cost_estimate=pl.CostEstimate(flops=1000, bytes_accessed=1000, transcendentals=0),
            name=getattr(kernel, "func", kernel).__name__,
        )(*scalars, *arrays)

    def whole(self, array):
        return pl.BlockSpec(array.shape, lambda i, *s: (0,) * len(array.shape)), array

    def columns(self, array, width, place):
        return pl.BlockSpec((array.shape[0], width), lambda i, *s: (0, place)), array

    def rows(self, array, block, backwards=False, low=0):
        last = self.group_rows // block - 1

        def at(i, *s):
            return (last - i if backwards else i + low,) + (0,) * (len(array.shape) - 1)

        size = array.shape[0] * block // self.group_rows
        return pl.BlockSpec((size,) + array.shape[1:], at), array

    def across(self, array, block, low=0):
        return pl.BlockSpec((8, block), lambda i, *s: (0, i + low)), array

    def out(self, columns, dtype):
        return jax.ShapeDtypeStruct((self.group_rows, columns), dtype)

    def parts(self, arrays, block, low=0):
        if not self.square:
            return [self.rows(arrays[0], block, low=low)]
        return [
            (
                pl.BlockSpec(
                    (block, z.shape[1]), lambda i, *s, at=self.at(block, False, k): (s[-1][at + i + low], 0)
                ),
                z,
            )
            for k, z in zip((1, 2, 3, 4, 4), arrays)
        ]

    def halves(self, block, backwards=False):
        half = self.width // 2
        lines = (5, 6, 7, 8) if self.square else (0, 0)
        rows = self.group_rows // 2 if self.square else self.group_rows
        shape = jax.ShapeDtypeStruct((rows, half), bf16)
        return [
            (
                pl.BlockSpec((block, half), lambda i, *s, at=self.at(block, backwards, k): (s[-1][at + i], 0)),
                shape,
            )
            for k in lines
        ]

    def scan(self, low, high, hidden, weights, gain, prm, prs, prh, carried, before=()):
        channels, count = self.channels, self.group_rows
        parts = self.parts(hidden, ROWS, low)
        shapes = [
            self.out(self.width, bf16),
            self.out(channels, bf16),
            self.out(channels, f32),
            self.out(2 * STATE, bf16),
            self.out(2 * STATE, f32),
            self.out(LANES, f32),
            self.out(channels, f32),
            jax.ShapeDtypeStruct((count // SUB, STATE, channels), f32),
            self.out(channels, bf16),
            self.out(channels, bf16),
            self.out(channels, bf16),
        ]
        outs = [self.rows(z, ROWS, low=low) for z in shapes]
        outs.append(self.across(jax.ShapeDtypeStruct((8, count), f32), ROWS, low))
        kept = len(outs)
        ins = parts + [self.whole(z) for z in [weights, gain, prm, prs, prh, self.lower, self.spread] + list(carried)]
        aliases = {3 + len(ins) + k: k for k in range(len(before))}
        ins += [(pl.BlockSpec(memory_space=pl.ANY), z) for z in before]
        sizes = ((8, channels), (8, 2 * STATE), (STATE, channels))
        outs += [self.whole(jax.ShapeDtypeStruct(size, f32)) for size in sizes]
        result = self.call(
            functools.partial(
                scan_kernel,
                parts=len(parts),
                seqs=self.seqs,
                taps=self.taps,
                head_count=self.head_count,
                first_block=low,
                kept=len(before),
                starts=len(carried),
                place_at=self.at(ROWS, False, 0),
            ),
            (self.lengths, self.first, self.place),
            high - low,
            ins,
            outs,
            [
                pltpu.VMEM((ROWS, self.width), bf16),
                pltpu.VMEM((ROWS + 8, channels), f32),
                pltpu.VMEM((ROWS + 8, 2 * STATE), f32),
            ],
            aliases,
        )
        return result[:kept], result[kept:]

    def product(self, ga, weights):
        return self.call(
            functools.partial(product_kernel, place_at=self.at(WIDE_ROWS, False, 0)),
            (self.place,),
            self.group_rows // WIDE_ROWS,
            [self.rows(ga, WIDE_ROWS), self.whole(weights)],
            self.halves(WIDE_ROWS),
            [],
        )

    def cotangent(self, cotangent, weights, ga, square):
        parts = self.parts(cotangent, WIDE_ROWS)
        return self.call(
            functools.partial(cotangent_kernel, parts=len(parts), place_at=self.at(WIDE_ROWS, False, 0)),
            (self.place,),
            self.group_rows // WIDE_ROWS,
            parts + [self.whole(weights), self.rows(ga, WIDE_ROWS), self.across(square, WIDE_ROWS)],
            [
                self.rows(self.out(self.channels, bf16), WIDE_ROWS),
                self.across(jax.ShapeDtypeStruct((8, self.group_rows), f32), WIDE_ROWS),
            ],
            [pltpu.VMEM((WIDE_ROWS, self.width), bf16)],
        )

    def gate(self, cotangent, sums, prm, weights, gate, y, gg, normed):
        channels = self.channels
        parts = self.parts(cotangent, WIDE_ROWS)
        return self.call(
            functools.partial(
                gate_kernel, parts=len(parts), taps=self.taps, place_at=self.at(WIDE_ROWS, False, 0)
            ),
            (self.place,),
            self.group_rows // WIDE_ROWS,
            parts
            + [self.across(sums, WIDE_ROWS), self.whole(prm), self.columns(weights, channels, 0)]
            + [self.rows(z, WIDE_ROWS) for z in (gate, y, gg, normed)],
            [
                self.rows(self.out(channels, bf16), WIDE_ROWS),
                self.rows(self.out(channels, f32), WIDE_ROWS),
                self.whole(jax.ShapeDtypeStruct(prm.shape, f32)),
                self.whole(jax.ShapeDtypeStruct((self.width, 2 * channels), bf16)),
                self.whole(jax.ShapeDtypeStruct((8, self.width), f32)),
            ],
            [pltpu.VMEM((WIDE_ROWS, self.width), bf16), pltpu.VMEM((self.width, 2 * channels), f32)],
        )

    def backward(self, weights, gain, terms, dprm_gate, prm, prs, prh, saved):
        channels = self.channels
        gradients = channels + 3 * STATE
        halves = self.halves(ROWS, True)
        shapes = [
            jax.ShapeDtypeStruct((self.width, gradients), bf16),
            jax.ShapeDtypeStruct((16, self.width), f32),
        ]
        shapes += [jax.ShapeDtypeStruct(z.shape, f32) for z in (prm, prs, prh)]
        result = self.call(
            functools.partial(
                backward_kernel,
                seqs=self.seqs,
                taps=self.taps,
                halves=len(halves),
                place_at=self.at(ROWS, True, 0),
            ),
            (self.lengths, self.first, self.place),
            self.group_rows // ROWS,
            [
                self.whole(z)
                for z in (weights, gain, terms, dprm_gate, prm, prs, prh, self.upper, self.spread, self.gather)
            ]
            + [self.rows(z, ROWS, True) for z in saved],
            halves + [self.whole(z) for z in shapes],
            [
                pltpu.VMEM((ROWS + 8, channels), f32),
                pltpu.VMEM((ROWS + 8, 2 * STATE), f32),
                pltpu.VMEM((STATE, channels), f32),
                pltpu.VMEM((8, channels), f32),
                pltpu.VMEM((ROWS, gradients), bf16),
                pltpu.VMEM((self.width, gradients), f32),
            ],
        )
        return result[: len(halves)], result[len(halves)], result[len(halves) + 1]


def per_device(
    hidden_in,
    norm_gain,
    proj_gate,
    proj_conv,
    proj_state,
    conv_kernel,
    conv_offset,
    state_kernel,
    state_offset,
    step_bias,
    decay_log,
    skip_gain,
    gate_gain,
    proj_out,
    out_cotangent,
    seq_lengths,
):
    tensor_count = lax.axis_size("tensor")
    tensor_place = lax.axis_index("tensor")
    dp_count = lax.axis_size("dp")
    dp_place = lax.axis_index("dp")
    square_mesh = tensor_count == 4
    own_rows, width = hidden_in.shape
    depth, channels = proj_gate.shape
    taps, heads_here, cut = conv_kernel.shape
    head_cut = step_bias.shape[0]
    state_cut = state_kernel.shape[1]
    state_width = proj_state.shape[1]
    group_rows = own_rows * tensor_count
    first_head = (tensor_place * heads_here).astype(jnp.int32)

    state_part = jnp.pad(proj_state, ((0, 0), (0, 3 * STATE - state_width)))
    weights = lax.all_gather(
        jnp.concatenate([proj_gate, proj_conv, state_part], axis=1), "dp", axis=0, tiled=True
    )
    out_weights = lax.all_gather(proj_out.T, "dp", axis=0, tiled=True)
    if square_mesh:
        from_x, from_y = gather_start(hidden_in)

    small = [
        norm_gain,
        conv_kernel,
        conv_offset,
        state_kernel,
        state_offset,
        step_bias,
        decay_log,
        skip_gain,
        gate_gain,
    ]
    flat = jnp.concatenate([z.reshape(-1) for z in small])
    flat = jnp.pad(flat, (0, -flat.shape[0] % 1024)).reshape(-1, LANES)
    small_all = lax.all_gather(flat, "dp", axis=0)
    if square_mesh:
        from_x, from_y, small_all = lax.optimization_barrier((from_x, from_y, small_all))
        hidden_all, _ = gather_end(hidden_in, from_x, from_y)
        hidden_all, cot = lax.optimization_barrier((hidden_all, out_cotangent))
    else:
        hidden_all = [lax.all_gather(hidden_in, "tensor", axis=0, tiled=True)]
    small_all = small_all.reshape(dp_count, -1).astype(f32)
    shares, at = [], 0
    for z in small:
        shares.append(small_all[:, at : at + z.size].reshape((dp_count,) + z.shape))
        at += z.size
    gain_in = shares[0].reshape(1, width)
    taps_conv = shares[1].transpose(1, 2, 0, 3).reshape(taps, channels)
    off_conv = shares[2].transpose(1, 0, 2).reshape(1, channels)
    taps_state = shares[3].transpose(1, 0, 2).reshape(taps, 2 * STATE)
    off_state = shares[4].reshape(1, 2 * STATE)
    gain_gate = shares[8].transpose(1, 0, 2).reshape(1, channels)

    def own_heads(z):
        return lax.dynamic_slice_in_dim(z.reshape(-1), first_head, heads_here, 0)

    skip = jnp.repeat(own_heads(shares[7]), HEADDIM).reshape(1, channels)
    prm = jnp.concatenate([taps_conv, off_conv, skip, gain_gate], axis=0)
    prm = jnp.pad(prm, ((0, -prm.shape[0] % 8), (0, 0)))
    prs = jnp.concatenate([taps_state, off_state], axis=0)
    prs = jnp.pad(prs, ((0, -prs.shape[0] % 8), (0, 0)))
    prh = jnp.stack([own_heads(shares[5]), jnp.exp(own_heads(shares[6]))])
    prh = jnp.pad(prh, ((0, 6), (0, LANES - heads_here)))

    kernels = Kernels(
        seq_lengths,
        first_head.reshape(1),
        tensor_place,
        tensor_count,
        group_rows,
        width,
        channels,
        taps,
        heads_here,
    )

    blocks = group_rows // ROWS
    common = (hidden_all, weights, gain_in, prm, prs, prh)
    if square_mesh:
        moving = gather_start(cot)
        middle = blocks * 3 // 4
        saved, carried = kernels.scan(0, middle, *common, ())
        carried, moving = lax.optimization_barrier((carried, moving))
        cotangent_all, carried = gather_end(cot, *moving, carried)
        saved, _ = kernels.scan(middle, blocks, *common, carried, saved)
    else:
        cotangent_all = [lax.all_gather(out_cotangent, "tensor", axis=0, tiled=True)]
        saved, _ = kernels.scan(0, blocks, *common, ())
    normed, v, u, vs, us, scan_terms, y_scan, states, gate_pre, ga, y_total, square = saved
    gg, sums = kernels.cotangent(cotangent_all, out_weights, ga, square)
    gg, ga = lax.optimization_barrier((gg, ga))
    out_halves = kernels.product(ga, out_weights)
    if square_mesh:
        sums = sums + over_x(sums)
        sums, out_halves = lax.optimization_barrier((sums, out_halves))
        sums = sums + over_y(sums)
        sums, out_halves = lax.optimization_barrier((sums, out_halves))
        moving = scatter_start(out_halves)
    else:
        sums = lax.psum(sums, "tensor")

    dgate, dy, dprm_gate, grad_first, terms = kernels.gate(
        cotangent_all, sums, prm, weights, gate_pre, y_total, gg, normed
    )
    if square_mesh:
        dy, grad_first, moving = lax.optimization_barrier((dy, grad_first, moving))
        far, dy = scatter_middle(out_halves, *moving, dy)
        out_moving = moving + far
    own_first = lax.psum_scatter(grad_first, "dp", scatter_dimension=0, tiled=True)
    gn_halves, grad_last, small_sum = kernels.backward(
        weights,
        gain_in,
        terms,
        dprm_gate,
        prm,
        prs,
        prh,
        [normed, dgate, dy, v, u, vs, us, scan_terms, y_scan, states],
    )

    def own_sum(halves):
        return lax.psum_scatter(
            jnp.concatenate(halves, axis=1), "tensor", scatter_dimension=0, tiled=True
        ).astype(f32)

    if square_mesh:
        gn_halves, grad_last, small_sum, own_first, out_moving = lax.optimization_barrier(
            (gn_halves, grad_last, small_sum, own_first, out_moving)
        )
        moving = scatter_start(gn_halves)
    own_last = lax.psum_scatter(grad_last, "dp", scatter_dimension=0, tiled=True)
    small_sum = sum_over_dp(small_sum)
    if square_mesh:
        small_sum, moving = lax.optimization_barrier((small_sum, moving))
        far, small_sum = scatter_middle(gn_halves, *moving, small_sum)
    small_shared = sum_over_tensor(small_sum) if square_mesh else lax.psum(small_sum, "tensor")

    if square_mesh:
        own_state = own_last[:, channels:].astype(f32)
        own_state = (own_state + over_x(own_last[:, channels:]).astype(f32)).astype(bf16)
        far, own_state, small_shared = lax.optimization_barrier((far, own_state, small_shared))
        own_state = own_state.astype(f32) + over_y(own_state).astype(f32)
        grad_normed = scatter_end(gn_halves, *moving, *far)
        branch = scatter_end(out_halves, *out_moving)
    else:
        grad_normed = own_sum(gn_halves)
        own_state = lax.psum(own_last[:, channels:].astype(f32), "tensor")
        branch = own_sum(out_halves)

    own_square = lax.dynamic_slice_in_dim(sums[0], tensor_place * own_rows, own_rows, 0)
    inverse_gate = lax.rsqrt(own_square * (1.0 / INNER) + EPS)[:, None]
    values = hidden_in.astype(f32)
    block_out = (values + branch * inverse_gate).astype(bf16)

    inverse_in = lax.rsqrt(jnp.mean(values * values, axis=1, keepdims=True) + EPS)
    scaled = values * inverse_in
    grad_scaled = grad_normed * gain_in
    grad_hidden = out_cotangent.astype(f32) + inverse_in * (
        grad_scaled - scaled * jnp.mean(grad_scaled * scaled, axis=1, keepdims=True)
    )

    own_part = depth // tensor_count
    own_state = lax.dynamic_slice_in_dim(own_state, tensor_place * own_part, own_part, 0)[:, :state_width]

    def own_cut(z, size, axis):
        return lax.dynamic_slice_in_dim(z, dp_place * size, size, axis)

    by_channel = small_sum[: taps + 3, :channels].reshape(taps + 3, heads_here, HEADDIM)
    by_channel = own_cut(by_channel, cut, 2)
    by_map = own_cut(small_shared[: taps + 1, channels : channels + 2 * STATE], state_cut, 1)
    heads_at = channels + 2 * STATE
    by_head = own_cut(small_shared[:3, heads_at : heads_at + LANES], head_cut, 1)
    gain_grad = lax.dynamic_slice_in_dim(
        small_shared[8], (dp_place * tensor_count + tensor_place) * own_part, own_part, 0
    )
    own_first = own_first.astype(f32)
    return (
        block_out,
        grad_hidden,
        gain_grad,
        own_first[:, :channels],
        own_last[:, :channels].astype(f32),
        own_state,
        own_first[:, channels:].T,
        by_channel[:taps],
        by_channel[taps],
        by_map[:taps],
        by_map[taps],
        by_head[0],
        by_head[1],
        by_head[2],
        by_channel[taps + 2],
    )


def solution(mesh):
    placed = (
        P(("dp", "tensor"), None),
        P("dp"),
        P("dp", "tensor"),
        P("dp", "tensor"),
        P("dp", None),
        P(None, "tensor", "dp"),
        P("tensor", "dp"),
        P(None, "dp"),
        P("dp"),
        P("dp"),
        P("dp"),
        P("dp"),
        P("tensor", "dp"),
        P("tensor", "dp"),
        P(("dp", "tensor"), None),
        P("dp", None),
    )
    return jax.shard_map(
        per_device,
        mesh=mesh,
        in_specs=placed,
        out_specs=(
            P(("dp", "tensor"), None),
            P(("dp", "tensor"), None),
            P(("dp", "tensor")),
            P("dp", "tensor"),
            P("dp", "tensor"),
            P(("dp", "tensor"), None),
            P("tensor", "dp"),
            P(None, "tensor", "dp"),
            P("tensor", "dp"),
            P(None, "dp"),
            P("dp"),
            P("dp"),
            P("dp"),
            P("dp"),
            P("tensor", "dp"),
        ),
        check_vma=False,
    )
```

```python
import functools

import jax
import jax.numpy as jnp
import numpy as np
from jax import lax
from jax.experimental import pallas as pl
from jax.experimental.pallas import tpu as pltpu
from jax.sharding import PartitionSpec as P

HEADDIM = 64
STATE = 128
INNER = 2048
LANES = 128
ROWS = 256
WIDE_ROWS = 512
FIELD = 32
PARAMS = 8
SUB = 128
EPS = 1e-05
LOG2E = 1.4426950408889634

f32 = jnp.float32
bf16 = jnp.bfloat16


def nn(a, b):
    return lax.dot_general(a, b, (((1,), (0,)), ((), ())), preferred_element_type=f32)


def nt(a, b):
    return lax.dot_general(a, b, (((1,), (1,)), ((), ())), preferred_element_type=f32)


def tn(a, b):
    return lax.dot_general(a, b, (((0,), (0,)), ((), ())), preferred_element_type=f32)


def pieces(z, count):
    parts = []
    for _ in range(count - 1):
        part = z.astype(bf16)
        parts.append(part)
        z = z - part.astype(f32)
    parts.append(z.astype(bf16))
    return parts


def spread_heads(z, heads):
    return nn(jnp.concatenate(pieces(z, 2), axis=1), heads)


def gather_heads(z, heads):
    return nn(jnp.concatenate(pieces(z, 2), axis=1), heads)


def triangle_sum(triangle, z):
    return nn(triangle, jnp.concatenate(pieces(z, 3), axis=0))


def constants(channels):
    row, col = np.arange(ROWS)[:, None], np.arange(ROWS)[None, :]
    same = row // SUB == col // SUB
    lower = np.concatenate([same & (row >= col)] * 3, axis=1)
    upper = np.concatenate([same & (row <= col)] * 3, axis=1)
    heads = np.arange(LANES)[:, None] == np.arange(channels)[None, :] // HEADDIM
    spread = np.concatenate([heads] * 2, axis=0)
    gather = np.concatenate([heads.T] * 2, axis=0)
    return [jnp.asarray(z, bf16) for z in (lower, upper, spread, gather)]


def ends_of(len_ref, count):
    ends, total = [], 0
    for s in range(count):
        total = total + len_ref[0, s]
        ends.append(total)
    return ends


def segment_of(places, ends):
    return sum((places >= end).astype(jnp.int32) for end in ends)


def start_of(places, ends):
    start = jnp.zeros_like(places)
    for end in ends:
        start = jnp.where(places >= end, end, start)
    return start


def scan_steps(raw, decay, lower):
    step = jnp.maximum(raw, 0.0) + jnp.log1p(jnp.exp(-jnp.abs(raw)))
    return step, triangle_sum(lower, -decay * step)


def scan_weights(step, cum, base, ends, spread):
    rows = step.shape[0]
    segment = segment_of(base + lax.broadcasted_iota(jnp.int32, (rows, 1), 0), ends)
    carried, keep, survive = [], [], []
    for low in range(0, rows, SUB):
        before = segment_of(base + low - 1, ends)
        tail = segment_of(base + low + SUB - 1, ends)
        part, own = cum[low : low + SUB], segment[low : low + SUB]
        last = part[SUB - 1 :]
        carried.append(jnp.where(own == before, jnp.exp(part), 0.0))
        keep.append(jnp.where(own == tail, jnp.exp(last - part), 0.0))
        survive.append(jnp.where(tail == before, jnp.exp(last), 0.0))
    survive.append(jnp.zeros((-len(survive) % 8, LANES), f32))
    wide = spread_heads(jnp.concatenate([step] + carried + keep + survive, axis=0), spread)
    return wide[:rows], wide[rows : 2 * rows], wide[2 * rows : 3 * rows], wide[3 * rows :]


def pair_stack(z):
    lane = lax.broadcasted_iota(jnp.int32, z.shape, 1)
    zero = jnp.zeros_like(z)
    return jnp.concatenate(
        [jnp.where(lane < HEADDIM, z, zero), jnp.where(lane >= HEADDIM, z, zero)], axis=0
    )


def silu(u):
    return u * jax.nn.sigmoid(u)


def own_lanes(z, shift, count):
    moved = pltpu.roll(z, (z.shape[1] - shift) % z.shape[1], 1)
    lane = lax.broadcasted_iota(jnp.int32, z.shape, 1)
    return jnp.where(lane < count, moved, 0.0)


def nn3(a, b):
    a, a_low = pieces(a, 2)
    b, b_low = pieces(b, 2)
    return nn(jnp.concatenate([a, a_low, a], axis=1), jnp.concatenate([b, b, b_low], axis=0))


def nt3(a, b):
    a, a_low = pieces(a, 2)
    b, b_low = pieces(b, 2)
    return nt(jnp.concatenate([a, a_low, a], axis=1), jnp.concatenate([b, b, b_low], axis=1))


def pair_product(mixing, z):
    high, low = pieces(z, 2)
    both = nn(
        jnp.concatenate(mixing, axis=1),
        jnp.concatenate([pair_stack(high), pair_stack(low)], axis=1),
    )
    return both[:, :LANES] + both[:, LANES:]


def take_rows(refs, which, buffer):
    if len(refs) == 1:
        return refs[0][...]
    half = refs[3].shape[1]
    for k in range(3):

        @pl.when(which == k)
        def _(k=k):
            buffer[...] = refs[k][...]

    @pl.when(which == 3)
    def _():
        buffer[:, :half] = refs[3][...]
        buffer[:, half:] = refs[4][...]

    return buffer[...]


def put_halves(refs, which, product):
    half = product.shape[1] // 2
    left, right = product[:, :half], product[:, half:]
    if len(refs) == 2:
        refs[0][...] = left
        refs[1][...] = right
        return
    left_sent, left_kept, right_sent, right_kept = refs

    @pl.when(which % 2 == 1)
    def _():
        left_sent[...] = left

    @pl.when(which % 2 == 0)
    def _():
        left_kept[...] = left

    @pl.when(which >= 2)
    def _():
        right_sent[...] = right

    @pl.when(which < 2)
    def _():
        right_kept[...] = right


def scan_kernel(
    len_ref, first_ref, place_ref, *refs, parts, seqs, taps, head_count, first_block, kept, starts, place_at
):
    part_refs, refs = refs[:parts], refs[parts:]
    w_ref, gain_ref, prm_ref, prs_ref, prh_ref, lower_ref, spread_ref = refs[:7]
    start_refs, refs = refs[7 : 7 + starts], refs[7 + starts :]
    (
        normed_ref,
        v_ref,
        u_ref,
        vs_ref,
        us_ref,
        terms_ref,
        y_ref,
        st_ref,
        gate_ref,
        ga_ref,
        total_ref,
        square_ref,
        vtail_out,
        stail_out,
        carry,
        hid_buf,
        vbuf,
        sbuf,
    ) = refs[kept:]
    rows, channels = v_ref.shape
    step_id = pl.program_id(0)
    block = step_id + first_block
    base = block * rows
    ends = ends_of(len_ref, seqs)

    @pl.when(step_id == 0)
    def _():
        if start_refs:
            vbuf[0:8, :] = start_refs[0][...]
            sbuf[0:8, :] = start_refs[1][...]
            carry[...] = start_refs[2][...]
        else:
            vbuf[0:8, :] = jnp.zeros((8, channels), f32)
            sbuf[0:8, :] = jnp.zeros((8, 2 * STATE), f32)
            carry[...] = jnp.zeros_like(carry)

    values = take_rows(part_refs, place_ref[place_at + block], hid_buf).astype(f32)
    inverse = lax.rsqrt(jnp.mean(values * values, axis=1, keepdims=True) + EPS)
    normed = (values * inverse * gain_ref[...]).astype(bf16)
    normed_ref[...] = normed
    gate_pre = nn(normed, w_ref[:, :channels])
    gate_ref[...] = gate_pre.astype(bf16)
    conv_pre = nn(normed, w_ref[:, channels : 2 * channels])
    state_all = nn(normed, w_ref[:, 2 * channels :])
    v_ref[...] = conv_pre.astype(bf16)
    vs_ref[...] = state_all[:, : 2 * STATE].astype(bf16)
    vbuf[8 : 8 + rows, :] = conv_pre
    sbuf[8 : 8 + rows, :] = state_all[:, : 2 * STATE]
    start = start_of(base + lax.broadcasted_iota(jnp.int32, (rows, 1), 0), ends)
    u = prm_ref[taps : taps + 1, :] + prm_ref[taps - 1 : taps, :] * conv_pre
    us = prs_ref[taps : taps + 1, :] + prs_ref[taps - 1 : taps, :] * state_all[:, : 2 * STATE]
    for lag in range(1, taps):
        usable = base + lax.broadcasted_iota(jnp.int32, (rows, 1), 0) - lag >= start
        tap = taps - 1 - lag
        u = u + prm_ref[tap : tap + 1, :] * jnp.where(usable, vbuf[8 - lag : 8 - lag + rows, :], 0.0)
        us = us + prs_ref[tap : tap + 1, :] * jnp.where(usable, sbuf[8 - lag : 8 - lag + rows, :], 0.0)
    vbuf[0:8, :] = vbuf[rows : rows + 8, :]
    sbuf[0:8, :] = sbuf[rows : rows + 8, :]
    vtail_out[...] = vbuf[0:8, :]
    stail_out[...] = sbuf[0:8, :]
    u_ref[...] = u
    us_ref[...] = us
    raw = own_lanes(state_all[:, 2 * STATE :], first_ref[0], head_count) + prh_ref[0:1, :]

    x = silu(u)
    maps = silu(us)
    step, cum = scan_steps(raw, prh_ref[1:2, :], lower_ref[...])
    lane = lax.broadcasted_iota(jnp.int32, (rows, LANES), 1)
    terms_ref[...] = jnp.where(
        lane < FIELD,
        step,
        jnp.where(lane < 2 * FIELD, pltpu.roll(raw, FIELD, 1), pltpu.roll(cum, 2 * FIELD, 1)),
    )
    step_w, carried_w, keep_w, survive_w = scan_weights(step, cum, base, ends, spread_ref[...])
    cum = cum * LOG2E
    cum_row = cum.T
    stepped = step_w * x
    kept_b = keep_w * stepped
    row = lax.broadcasted_iota(jnp.int32, (SUB, SUB), 0)
    col = lax.broadcasted_iota(jnp.int32, (SUB, SUB), 1)
    state = carry[...]
    y_parts = []
    for q in range(rows // SUB):
        at = slice(q * SUB, (q + 1) * SUB)
        low = base + q * SUB
        mask = (row >= col) & (segment_of(low + row, ends) == segment_of(low + col, ends))
        b_map, c_map = maps[at, :STATE], maps[at, STATE:]
        gram = jnp.where(mask, nt3(c_map, b_map), 0.0)
        st_ref[q] = state
        outer = carried_w[at] * nn3(c_map, state)
        inner = []
        for pair in range(channels // LANES):
            mixing = []
            for h in (2 * pair, 2 * pair + 1):
                spread = cum[at, h : h + 1] - cum_row[h : h + 1, at]
                mixing.append((jnp.exp2(jnp.minimum(spread, 0.0)) * gram).astype(bf16))
            inner.append(pair_product(mixing, stepped[at, pair * LANES : (pair + 1) * LANES]))
        y_parts.append(jnp.concatenate(inner, axis=1) + outer)
        state = survive_w[q : q + 1] * state + nn3(b_map.T, kept_b[at])
    carry[...] = state
    y_scan = jnp.concatenate(y_parts, axis=0)
    y_ref[...] = y_scan
    y_total = y_scan + prm_ref[taps + 1 : taps + 2, :] * x
    total_ref[...] = y_total.astype(bf16)
    g = y_total * silu(gate_pre)
    ga_ref[...] = (g * prm_ref[taps + 2 : taps + 3, :]).astype(bf16)
    square = jnp.sum(g * g, axis=1, keepdims=True)
    square_ref[...] = jnp.broadcast_to(square, (rows, LANES)).T[:8, :]


def parameter_kernel(
    first_ref, packed_ref, prm_ref, prs_ref, prh_ref, gain_ref, *, taps, heads_here, cut, state_cut, head_cut, depth
):
    packed = packed_ref[...]
    total = packed.shape[1]
    source = lax.broadcasted_iota(jnp.int32, (total, 1), 0)
    maps_at = heads_here * cut

    def split(z, size):
        return z >> (size.bit_length() - 1), z & (size - 1)

    def moved(columns, lane_of):
        lane = lane_of(lax.broadcasted_iota(jnp.int32, (1, columns), 1))
        return nn(packed, jnp.where(source == lane, 1.0, 0.0).astype(bf16))

    def by_channel(c):
        head, inside = split(c, HEADDIM)
        owner, place = split(inside, cut)
        return owner * LANES + head * cut + place

    def by_part(size, at):
        def lane_of(c):
            owner, place = split(c, size)
            return owner * LANES + at + place

        return lane_of

    def own_head(at):
        part = by_part(head_cut, at)
        return lambda h: jnp.where(h < heads_here, part(first_ref[0] + h), -1)

    channels = prm_ref.shape[1]
    row = lax.broadcasted_iota(jnp.int32, (PARAMS, 1), 0)
    by_head = moved(channels, by_channel)
    skip = by_part(head_cut, maps_at + 2 * head_cut)
    skips = moved(channels, lambda c: skip(first_ref[0] + split(c, HEADDIM)[0]))
    prm_ref[...] = jnp.where(
        row <= taps,
        by_head,
        jnp.where(row == taps + 1, skips, jnp.where(row == taps + 2, pltpu.roll(by_head, 1, 0), 0.0)),
    )
    prs_ref[...] = jnp.where(row <= taps, moved(2 * STATE, by_part(state_cut, maps_at)), 0.0)
    bias = moved(LANES, own_head(maps_at))[taps + 1 : taps + 2]
    rate = jnp.exp(moved(LANES, own_head(maps_at + head_cut))[taps + 1 : taps + 2])
    lane = lax.broadcasted_iota(jnp.int32, (1, LANES), 1)
    rate = jnp.where(lane < heads_here, rate, 0.0)
    prh_ref[...] = jnp.where(row == 0, bias, jnp.where(row == 1, rate, 0.0))
    gain_ref[...] = moved(gain_ref.shape[1], by_part(depth, 0))[taps + 2 : taps + 3]


def product_kernel(place_ref, ga_ref, w_ref, *refs, place_at):
    product = nt(ga_ref[...], w_ref[...]).astype(bf16)
    put_halves(refs, place_ref[place_at + pl.program_id(0)], product)


def cotangent_kernel(place_ref, *refs, parts, place_at):
    part_refs, refs = refs[:parts], refs[parts:]
    w_ref, ga_ref, square_ref, gg_ref, sums_ref, cot_buf = refs
    rows = gg_ref.shape[0]
    cotangent = take_rows(part_refs, place_ref[place_at + pl.program_id(0)], cot_buf)
    grad_gated = nn(cotangent, w_ref[...])
    gg_ref[...] = grad_gated.astype(bf16)
    inner = jnp.sum(grad_gated * ga_ref[...].astype(f32), axis=1, keepdims=True)
    inner_row = jnp.broadcast_to(inner, (rows, LANES)).T[:8, :]
    sublane = lax.broadcasted_iota(jnp.int32, (8, rows), 0)
    sums_ref[...] = jnp.where(sublane == 0, square_ref[...], inner_row)


def gain_row(weights, grads):
    terms = jnp.sum(weights.astype(f32) * grads, axis=1, keepdims=True)
    return jnp.broadcast_to(terms, (terms.shape[0], LANES)).T[:8, :]


def gate_kernel(place_ref, *refs, parts, taps, place_at):
    part_refs, refs = refs[:parts], refs[parts:]
    (
        sums_ref,
        prm_ref,
        w_ref,
        gate_ref,
        y_ref,
        gg_ref,
        normed_ref,
        dgate_ref,
        dy_ref,
        dprm_ref,
        out_ref,
        gain_ref,
        cot_buf,
        total,
    ) = refs
    rows, channels = gate_ref.shape
    step_id = pl.program_id(0)

    @pl.when(step_id == 0)
    def _():
        dprm_ref[...] = jnp.zeros_like(dprm_ref)
        total[...] = jnp.zeros_like(total)

    sums = jnp.concatenate([sums_ref[...], jnp.zeros((LANES - 8, rows), f32)], axis=0).T
    inverse = lax.rsqrt(sums[:, 0:1] * (1.0 / INNER) + EPS)
    inner_mean = sums[:, 1:2] * inverse * (1.0 / INNER)
    normed = normed_ref[...]
    cotangent = take_rows(part_refs, place_ref[place_at + step_id], cot_buf)
    gain = prm_ref[taps + 2 : taps + 3, :]
    gate_pre = gate_ref[...].astype(f32)
    sig_gate = jax.nn.sigmoid(gate_pre)
    act = gate_pre * sig_gate
    y = y_ref[...].astype(f32)
    hat = y * act * inverse
    gated = (hat * gain).astype(bf16)
    total[:, channels:] += tn(cotangent, gated)
    grad_gated = gg_ref[...].astype(f32)
    dprm_ref[taps + 2 : taps + 3, :] += jnp.sum(grad_gated * hat, axis=0, keepdims=True)
    grad_inner = inverse * (grad_gated * gain - hat * inner_mean)
    dy_ref[...] = grad_inner * act
    dgate = (grad_inner * y * sig_gate * (1.0 + gate_pre * (1.0 - sig_gate))).astype(bf16)
    dgate_ref[...] = dgate
    total[:, :channels] += tn(normed, dgate)

    @pl.when(step_id == pl.num_programs(0) - 1)
    def _():
        out_ref[...] = total[...].astype(bf16)
        gain_ref[...] = gain_row(w_ref[...], total[:, :channels])


def backward_kernel(len_ref, first_ref, place_ref, *refs, seqs, taps, halves, place_at):
    (
        w_ref,
        gain_ref,
        terms_ref,
        dprm_gate_ref,
        prm_ref,
        prs_ref,
        prh_ref,
        upper_ref,
        spread_ref,
        gather_ref,
        normed_ref,
        dgate_ref,
        dy_ref,
        v_ref,
        u_ref,
        vs_ref,
        us_ref,
        scan_ref,
        y_ref,
        st_ref,
    ) = refs[:20]
    half_refs = refs[20 : 20 + halves]
    out_ref, small_ref, dprm_ref, dprs_ref, dprh_ref, dbuf, dsbuf, carry, ending, total = refs[20 + halves :]
    rows, channels = dgate_ref.shape
    step_id = pl.program_id(0)
    base = (pl.num_programs(0) - 1 - step_id) * rows
    ends = ends_of(len_ref, seqs)

    @pl.when(step_id == 0)
    def _():
        dbuf[rows : rows + 8, :] = jnp.zeros((8, channels), f32)
        dsbuf[rows : rows + 8, :] = jnp.zeros((8, 2 * STATE), f32)
        carry[...] = jnp.zeros_like(carry)
        ending[...] = jnp.zeros_like(ending)
        dprm_ref[...] = jnp.zeros_like(dprm_ref)
        dprs_ref[...] = jnp.zeros_like(dprs_ref)
        dprh_ref[...] = jnp.zeros_like(dprh_ref)
        total[...] = jnp.zeros_like(total)

    def add_row(ref, at, z):
        ref[at : at + 1, :] += jnp.sum(z, axis=0, keepdims=True)

    skip = prm_ref[taps + 1 : taps + 2, :]
    u = u_ref[...]
    sig_u = jax.nn.sigmoid(u)
    x = u * sig_u
    y_scan = y_ref[...]
    dy = dy_ref[...]
    dy_b = dy.astype(bf16)

    add_row(dprm_ref, taps + 1, dy * x)
    us = us_ref[...]
    sig_us = jax.nn.sigmoid(us)
    maps = us * sig_us
    maps_b = maps.astype(bf16)
    terms = scan_ref[...]
    lane = lax.broadcasted_iota(jnp.int32, (rows, LANES), 1)
    inside = lane < FIELD
    step = jnp.where(inside, terms, 0.0)
    raw = jnp.where(inside, pltpu.roll(terms, LANES - FIELD, 1), 0.0)
    cum = jnp.where(inside, pltpu.roll(terms, LANES - 2 * FIELD, 1), 0.0)
    decay = prh_ref[1:2, :]
    step_w, carried_w, keep_w, survive_w = scan_weights(step, cum, base, ends, spread_ref[...])
    cum = cum * LOG2E
    cum_row = cum.T
    stepped = step_w * x
    stepped_b = stepped.astype(bf16)
    kept_b = (keep_w * stepped).astype(bf16)
    dy_carried = carried_w * dy
    dy_carried_b = dy_carried.astype(bf16)
    row = lax.broadcasted_iota(jnp.int32, (SUB, SUB), 0)
    col = lax.broadcasted_iota(jnp.int32, (SUB, SUB), 1)
    dstate = carry[...]
    state_end = ending[0:1, :]
    subs = rows // SUB
    dsteppeds, dmaps, state_ends = [None] * subs, [None] * subs, [None] * subs
    for q in reversed(range(subs)):
        at = slice(q * SUB, (q + 1) * SUB)
        low = base + q * SUB
        mask = (row <= col) & (segment_of(low + row, ends) == segment_of(low + col, ends))
        b_map, c_map = maps[at, :STATE], maps[at, STATE:]
        gram = jnp.where(mask, nt3(b_map, c_map), 0.0)
        state = st_ref[q]
        dstate_b = dstate.astype(bf16)
        dgram = jnp.zeros((SUB, SUB), f32)
        inner = []
        for pair in range(channels // LANES):
            lanes = slice(pair * LANES, (pair + 1) * LANES)
            dmix = nt(pair_stack(stepped_b[at, lanes]), dy_b[at, lanes])
            mixing = []
            for i, h in enumerate((2 * pair, 2 * pair + 1)):
                spread = cum_row[h : h + 1, at] - cum[at, h : h + 1]
                weight = jnp.exp2(jnp.minimum(spread, 0.0))
                mixing.append((weight * gram).astype(bf16))
                dgram = dgram + dmix[i * SUB : (i + 1) * SUB] * weight
            inner.append(pair_product(mixing, dy[at, lanes]))
        dsteppeds[q] = jnp.concatenate(inner, axis=1) + keep_w[at] * nn3(b_map, dstate)
        dgram = jnp.where(mask, dgram, 0.0).astype(bf16)
        db = nn(dgram, maps_b[at, STATE:]) + nt(kept_b[at], dstate_b)
        dc = tn(dgram, maps_b[at, :STATE]) + nt(dy_carried_b[at], state.astype(bf16))
        dmaps[q] = jnp.concatenate([db, dc], axis=1)
        state_ends[q] = state_end
        dstate = survive_w[q : q + 1] * dstate + nn3(c_map.T, dy_carried[at])
        state_end = jnp.sum(state * dstate, axis=0, keepdims=True)
    carry[...] = dstate
    ending[0:1, :] = state_end
    dstepped = jnp.concatenate(dsteppeds, axis=0)
    dmap = jnp.concatenate(dmaps, axis=0)
    state_ends.append(jnp.zeros((-subs % 8, channels), f32))
    by_head = gather_heads(
        jnp.concatenate([dy * y_scan - stepped * dstepped, x * dstepped] + state_ends, axis=0),
        gather_ref[...],
    )
    dlog = triangle_sum(upper_ref[...], by_head[:rows])
    dlog = jnp.concatenate(
        [
            dlog[q * SUB : (q + 1) * SUB] + by_head[2 * rows + q : 2 * rows + q + 1]
            for q in range(subs)
        ],
        axis=0,
    )
    draw = (by_head[rows : 2 * rows] - decay * dlog) * jax.nn.sigmoid(raw)
    add_row(dprh_ref, 0, draw)
    add_row(dprh_ref, 1, dlog * step * -decay)
    places = base + lax.broadcasted_iota(jnp.int32, (rows, 1), 0)
    segment = segment_of(places, ends)
    usable = [None] + [segment_of(places + lag, ends) == segment for lag in range(1, taps)]
    normed = normed_ref[...]

    def conv_back(du, v, weight_ref, buffer, sums_ref):
        buffer[0:rows, :] = du
        dv = weight_ref[taps - 1 : taps, :] * du
        lines = [jnp.sum(du * v, axis=0, keepdims=True), jnp.sum(du, axis=0, keepdims=True)]
        for lag in range(1, taps):
            later = jnp.where(usable[lag], buffer[lag : lag + rows, :], 0.0)
            dv = dv + weight_ref[taps - 1 - lag : taps - lag, :] * later
            lines.insert(0, jnp.sum(later * v, axis=0, keepdims=True))
        buffer[rows : rows + 8, :] = buffer[0:8, :]
        sums_ref[0 : taps + 1, :] += jnp.concatenate(lines, axis=0)
        return dv.astype(bf16)

    product = nt(dgate_ref[...], w_ref[:, :channels])
    du = (step_w * dstepped + skip * dy) * sig_u * (1.0 + u * (1.0 - sig_u))
    dv = conv_back(du, v_ref[...].astype(f32), prm_ref, dbuf, dprm_ref)
    product = product + nt(dv, w_ref[:, channels : 2 * channels])
    total[:, :channels] += tn(normed, dv)
    dus = dmap * sig_us * (1.0 + us * (1.0 - sig_us))
    dvs = conv_back(dus, vs_ref[...].astype(f32), prs_ref, dsbuf, dprs_ref)
    state_part = jnp.concatenate([dvs, pltpu.roll(draw, first_ref[0], 1).astype(bf16)], axis=1)
    product = product + nt(state_part, w_ref[:, 2 * channels :])
    total[:, channels:] += tn(normed, state_part)
    put_halves(half_refs, place_ref[place_at + step_id], product.astype(bf16))

    @pl.when(step_id == pl.num_programs(0) - 1)
    def _():
        grads = total[...]
        out_ref[...] = grads.astype(bf16)
        gains = (gain_row(w_ref[:, channels:], grads) + terms_ref[...]) / gain_ref[...]
        line = lax.broadcasted_iota(jnp.int32, (8, 1), 0)
        both = jnp.where(line == taps + 2, dprm_gate_ref[...], dprm_ref[...])
        skips = gather_heads(dprm_ref[...], gather_ref[...])
        by_head = jnp.where(line == 2, pltpu.roll(skips, 8 - (taps - 1), 0), dprh_ref[...])
        small_ref[...] = jnp.zeros_like(small_ref)
        small_ref[0:8, :channels] = both
        small_ref[0:8, channels : channels + 2 * STATE] = dprs_ref[...]
        small_ref[0:8, channels + 2 * STATE : channels + 2 * STATE + LANES] = pltpu.roll(
            by_head, first_ref[0], 1
        )
        small_ref[8:16, :] = gains


def held(places):
    last = next(p for p in places if p is not None)
    filled = []
    for p in places:
        last = last if p is None else p
        filled.append(last)
    return filled


def place_table(tensor_place, quarter_blocks, order):
    relative = [(b // quarter_blocks) ^ tensor_place for b in order]
    inside = [b % quarter_blocks for b in order]

    def places(slots):
        return held(
            [slots.index(r) * quarter_blocks + w if r in slots else None for r, w in zip(relative, inside)]
        )

    return [
        relative,
        places([0]),
        places([1]),
        places([2]),
        places([3]),
        places([1, 3]),
        places([0, 2]),
        places([2, 3]),
        places([0, 1]),
    ]


def over_x(z):
    return lax.ppermute(z, "tensor", [(0, 1), (1, 0), (2, 3), (3, 2)])


def over_y(z):
    return lax.ppermute(z, "tensor", [(0, 2), (2, 0), (1, 3), (3, 1)])


def gather_start(z):
    return over_x(z), over_y(z)


def gather_end(z, from_x, from_y, after=()):
    half = z.shape[1] // 2
    far = (from_x[:, :half], from_y[:, half:])
    far, after = lax.optimization_barrier((far, after))
    return [z, from_x, from_y, over_y(far[0]), over_x(far[1])], after


def scatter_start(halves):
    return over_x(halves[0]), over_y(halves[2])


def scatter_middle(halves, from_x, from_y, after=()):
    rows = from_x.shape[0] // 2
    left, right = halves[1], halves[3]
    left_far = left[rows:].astype(f32) + from_x[rows:].astype(f32)
    right_far = right[rows:].astype(f32) + from_y[rows:].astype(f32)
    far = (left_far.astype(bf16), right_far.astype(bf16))
    far, after = lax.optimization_barrier((far, after))
    return (over_y(far[0]), over_x(far[1])), after


def scatter_end(halves, from_x, from_y, far_left, far_right):
    rows = from_x.shape[0] // 2
    left, right = halves[1][:rows].astype(f32), halves[3][:rows].astype(f32)
    left = left + from_x[:rows].astype(f32) + far_left.astype(f32)
    right = right + from_y[:rows].astype(f32) + far_right.astype(f32)
    return left, right


def sum_over_tensor(z):
    z = (z.astype(f32) + over_x(z).astype(f32)).astype(z.dtype)
    return z.astype(f32) + over_y(z).astype(f32)


def sum_over_dp(z):
    count = lax.axis_size("dp")
    bit = 1
    while bit < count:
        z = z + lax.ppermute(z, "dp", [(i, i ^ bit) for i in range(count)])
        bit *= 2
    return z


class Kernels:
    def __init__(self, lengths, first, tensor_place, tensor_count, group_rows, width, channels, taps, head_count):
        self.lengths, self.first = lengths, first
        self.tensor_place, self.tensor_count = tensor_place, tensor_count
        self.square = tensor_count == 4
        self.group_rows, self.width, self.channels = group_rows, width, channels
        self.taps, self.head_count = taps, head_count
        self.seqs = lengths.shape[1]
        self.lower, self.upper, self.spread, self.gather = constants(channels)
        self.tables()

    def tables(self):
        kinds = ((ROWS, False), (ROWS, True), (WIDE_ROWS, False))
        self.kinds = {kind: k for k, kind in enumerate(kinds)}
        places = range(4) if self.square else range(1)
        made = []
        for t in places:
            lines = []
            for block, backwards in kinds:
                order = list(range(self.group_rows // block))[:: -1 if backwards else 1]
                table = place_table(t, len(order) // 4, order) if self.square else [order]
                lines += [line + [0] * (self.group_rows // ROWS - len(order)) for line in table]
            made.append(lines)
        self.lines = len(made[0]) // len(kinds)
        made = jnp.asarray(np.array(made, np.int32).reshape(len(made), -1))
        place = self.tensor_place if self.square else 0
        self.place = lax.dynamic_index_in_dim(made, place, 0, keepdims=False)
        self.steps = self.group_rows // ROWS

    def at(self, block, backwards, line):
        return (self.kinds[(block, backwards)] * self.lines + line) * self.steps

    def call(self, kernel, scalars, steps, ins, outs, scratch, aliases=None, flops=1000):
        specs, arrays = zip(*ins)
        out_specs, out_shapes = zip(*outs)
        return pl.pallas_call(
            kernel,
            grid_spec=pltpu.PrefetchScalarGridSpec(
                num_scalar_prefetch=len(scalars),
                grid=(steps,),
                in_specs=list(specs),
                out_specs=list(out_specs),
                scratch_shapes=scratch,
            ),
            out_shape=list(out_shapes),
            input_output_aliases=aliases or {},
            compiler_params=pltpu.CompilerParams(vmem_limit_bytes=56 * 2**20),
            cost_estimate=pl.CostEstimate(flops=flops, bytes_accessed=1000, transcendentals=0),
            name=getattr(kernel, "func", kernel).__name__,
        )(*scalars, *arrays)

    def whole(self, array):
        return pl.BlockSpec(array.shape, lambda i, *s: (0,) * len(array.shape)), array

    def columns(self, array, width, place):
        return pl.BlockSpec((array.shape[0], width), lambda i, *s: (0, place)), array

    def rows(self, array, block, backwards=False, low=0):
        last = self.group_rows // block - 1

        def at(i, *s):
            return (last - i if backwards else i + low,) + (0,) * (len(array.shape) - 1)

        size = array.shape[0] * block // self.group_rows
        return pl.BlockSpec((size,) + array.shape[1:], at), array

    def across(self, array, block, low=0):
        return pl.BlockSpec((8, block), lambda i, *s: (0, i + low)), array

    def out(self, columns, dtype):
        return jax.ShapeDtypeStruct((self.group_rows, columns), dtype)

    def parts(self, arrays, block, low=0):
        if not self.square:
            return [self.rows(arrays[0], block, low=low)]
        return [
            (
                pl.BlockSpec(
                    (block, z.shape[1]), lambda i, *s, at=self.at(block, False, k): (s[-1][at + i + low], 0)
                ),
                z,
            )
            for k, z in zip((1, 2, 3, 4, 4), arrays)
        ]

    def halves(self, block, backwards=False):
        half = self.width // 2
        lines = (5, 6, 7, 8) if self.square else (0, 0)
        rows = self.group_rows // 2 if self.square else self.group_rows
        shape = jax.ShapeDtypeStruct((rows, half), bf16)
        return [
            (
                pl.BlockSpec((block, half), lambda i, *s, at=self.at(block, backwards, k): (s[-1][at + i], 0)),
                shape,
            )
            for k in lines
        ]

    def parameters(self, packed, cut, state_cut, head_cut, depth):
        shapes = ((PARAMS, self.channels), (PARAMS, 2 * STATE), (PARAMS, LANES), (1, self.width))
        return self.call(
            functools.partial(
                parameter_kernel,
                taps=self.taps,
                heads_here=self.head_count,
                cut=cut,
                state_cut=state_cut,
                head_cut=head_cut,
                depth=depth,
            ),
            (self.first,),
            1,
            [self.whole(packed)],
            [self.whole(jax.ShapeDtypeStruct(shape, f32)) for shape in shapes],
            [],
        )

    def scan(self, low, high, hidden, weights, gain, prm, prs, prh, carried, before=()):
        channels, count = self.channels, self.group_rows
        parts = self.parts(hidden, ROWS, low)
        shapes = [
            self.out(self.width, bf16),
            self.out(channels, bf16),
            self.out(channels, f32),
            self.out(2 * STATE, bf16),
            self.out(2 * STATE, f32),
            self.out(LANES, f32),
            self.out(channels, f32),
            jax.ShapeDtypeStruct((count // SUB, STATE, channels), f32),
            self.out(channels, bf16),
            self.out(channels, bf16),
            self.out(channels, bf16),
        ]
        outs = [self.rows(z, ROWS, low=low) for z in shapes]
        outs.append(self.across(jax.ShapeDtypeStruct((8, count), f32), ROWS, low))
        kept = len(outs)
        ins = parts + [self.whole(z) for z in [weights, gain, prm, prs, prh, self.lower, self.spread] + list(carried)]
        aliases = {3 + len(ins) + k: k for k in range(len(before))}
        ins += [(pl.BlockSpec(memory_space=pl.ANY), z) for z in before]
        sizes = ((8, channels), (8, 2 * STATE), (STATE, channels))
        outs += [self.whole(jax.ShapeDtypeStruct(size, f32)) for size in sizes]
        result = self.call(
            functools.partial(
                scan_kernel,
                parts=len(parts),
                seqs=self.seqs,
                taps=self.taps,
                head_count=self.head_count,
                first_block=low,
                kept=len(before),
                starts=len(carried),
                place_at=self.at(ROWS, False, 0),
            ),
            (self.lengths, self.first, self.place),
            high - low,
            ins,
            outs,
            [
                pltpu.VMEM((ROWS, self.width), bf16),
                pltpu.VMEM((ROWS + 8, channels), f32),
                pltpu.VMEM((ROWS + 8, 2 * STATE), f32),
            ],
            aliases,
        )
        return result[:kept], result[kept:]

    def product(self, ga, weights):
        return self.call(
            functools.partial(product_kernel, place_at=self.at(WIDE_ROWS, False, 0)),
            (self.place,),
            self.group_rows // WIDE_ROWS,
            [self.rows(ga, WIDE_ROWS), self.whole(weights)],
            self.halves(WIDE_ROWS),
            [],
        )

    def cotangent(self, cotangent, weights, ga, square):
        parts = self.parts(cotangent, WIDE_ROWS)
        return self.call(
            functools.partial(cotangent_kernel, parts=len(parts), place_at=self.at(WIDE_ROWS, False, 0)),
            (self.place,),
            self.group_rows // WIDE_ROWS,
            parts + [self.whole(weights), self.rows(ga, WIDE_ROWS), self.across(square, WIDE_ROWS)],
            [
                self.rows(self.out(self.channels, bf16), WIDE_ROWS),
                self.across(jax.ShapeDtypeStruct((8, self.group_rows), f32), WIDE_ROWS),
            ],
            [pltpu.VMEM((WIDE_ROWS, self.width), bf16)],
        )

    def gate(self, cotangent, sums, prm, weights, gate, y, gg, normed):
        channels = self.channels
        parts = self.parts(cotangent, WIDE_ROWS)
        return self.call(
            functools.partial(
                gate_kernel, parts=len(parts), taps=self.taps, place_at=self.at(WIDE_ROWS, False, 0)
            ),
            (self.place,),
            self.group_rows // WIDE_ROWS,
            parts
            + [self.across(sums, WIDE_ROWS), self.whole(prm), self.columns(weights, channels, 0)]
            + [self.rows(z, WIDE_ROWS) for z in (gate, y, gg, normed)],
            [
                self.rows(self.out(channels, bf16), WIDE_ROWS),
                self.rows(self.out(channels, f32), WIDE_ROWS),
                self.whole(jax.ShapeDtypeStruct(prm.shape, f32)),
                self.whole(jax.ShapeDtypeStruct((self.width, 2 * channels), bf16)),
                self.whole(jax.ShapeDtypeStruct((8, self.width), f32)),
            ],
            [pltpu.VMEM((WIDE_ROWS, self.width), bf16), pltpu.VMEM((self.width, 2 * channels), f32)],
            flops=8 * self.group_rows * self.width * channels * 4,
        )

    def backward(self, weights, gain, terms, dprm_gate, prm, prs, prh, saved):
        channels = self.channels
        gradients = channels + 3 * STATE
        halves = self.halves(ROWS, True)
        shapes = [
            jax.ShapeDtypeStruct((self.width, gradients), bf16),
            jax.ShapeDtypeStruct((16, self.width), f32),
        ]
        shapes += [jax.ShapeDtypeStruct(z.shape, f32) for z in (prm, prs, prh)]
        result = self.call(
            functools.partial(
                backward_kernel,
                seqs=self.seqs,
                taps=self.taps,
                halves=len(halves),
                place_at=self.at(ROWS, True, 0),
            ),
            (self.lengths, self.first, self.place),
            self.group_rows // ROWS,
            [
                self.whole(z)
                for z in (weights, gain, terms, dprm_gate, prm, prs, prh, self.upper, self.spread, self.gather)
            ]
            + [self.rows(z, ROWS, True) for z in saved],
            halves + [self.whole(z) for z in shapes],
            [
                pltpu.VMEM((ROWS + 8, channels), f32),
                pltpu.VMEM((ROWS + 8, 2 * STATE), f32),
                pltpu.VMEM((STATE, channels), f32),
                pltpu.VMEM((8, channels), f32),
                pltpu.VMEM((self.width, gradients), f32),
            ],
        )
        return result[: len(halves)], result[len(halves)], result[len(halves) + 1]


def per_device(
    hidden_in,
    norm_gain,
    proj_gate,
    proj_conv,
    proj_state,
    conv_kernel,
    conv_offset,
    state_kernel,
    state_offset,
    step_bias,
    decay_log,
    skip_gain,
    gate_gain,
    proj_out,
    out_cotangent,
    seq_lengths,
):
    tensor_count = lax.axis_size("tensor")
    tensor_place = lax.axis_index("tensor")
    dp_count = lax.axis_size("dp")
    dp_place = lax.axis_index("dp")
    square_mesh = tensor_count == 4
    own_rows, width = hidden_in.shape
    depth, channels = proj_gate.shape
    taps, heads_here, cut = conv_kernel.shape
    head_cut = step_bias.shape[0]
    state_cut = state_kernel.shape[1]
    state_width = proj_state.shape[1]
    group_rows = own_rows * tensor_count
    first_head = (tensor_place * heads_here).astype(jnp.int32)

    state_part = jnp.pad(proj_state, ((0, 0), (0, 3 * STATE - state_width)))
    weights = lax.all_gather(
        jnp.concatenate([proj_gate, proj_conv, state_part], axis=1), "dp", axis=0, tiled=True
    )
    out_weights = lax.all_gather(proj_out.T, "dp", axis=0, tiled=True)
    if square_mesh:
        from_x, from_y = gather_start(hidden_in)

    def padded(z):
        return jnp.pad(z, ((0, 0), (0, LANES - z.shape[1])))

    packed = jnp.concatenate(
        [
            padded(jnp.concatenate([conv_kernel.reshape(taps, -1), state_kernel], axis=1)),
            padded(jnp.concatenate([conv_offset.reshape(1, -1), state_offset[None]], axis=1)),
            padded(
                jnp.concatenate(
                    [gate_gain.reshape(1, -1), step_bias[None], decay_log[None], skip_gain[None]], axis=1
                )
            ),
            padded(norm_gain[None]),
        ],
        axis=0,
    )
    packed = jnp.pad(packed, ((0, PARAMS - packed.shape[0]), (0, 0)))
    packed = lax.all_gather(packed, "dp", axis=1, tiled=True)
    if square_mesh:
        from_x, from_y, packed = lax.optimization_barrier((from_x, from_y, packed))
        hidden_all, _ = gather_end(hidden_in, from_x, from_y)
    else:
        hidden_all = [lax.all_gather(hidden_in, "tensor", axis=0, tiled=True)]

    kernels = Kernels(
        seq_lengths,
        first_head.reshape(1),
        tensor_place,
        tensor_count,
        group_rows,
        width,
        channels,
        taps,
        heads_here,
    )

    prm, prs, prh, gain_in = kernels.parameters(packed, cut, state_cut, head_cut, depth)
    if square_mesh:
        hidden_all, prm, kernels.place, cot = lax.optimization_barrier(
            (hidden_all, prm, kernels.place, out_cotangent)
        )

    blocks = group_rows // ROWS
    common = (hidden_all, weights, gain_in, prm, prs, prh)
    if square_mesh:
        moving = gather_start(cot)
        middle = blocks * 3 // 4
        saved, carried = kernels.scan(0, middle, *common, ())
        carried, moving = lax.optimization_barrier((carried, moving))
        cotangent_all, carried = gather_end(cot, *moving, carried)
        saved, _ = kernels.scan(middle, blocks, *common, carried, saved)
    else:
        cotangent_all = [lax.all_gather(out_cotangent, "tensor", axis=0, tiled=True)]
        saved, _ = kernels.scan(0, blocks, *common, ())
    normed, v, u, vs, us, scan_terms, y_scan, states, gate_pre, ga, y_total, square = saved
    gg, sums = kernels.cotangent(cotangent_all, out_weights, ga, square)
    gg, ga = lax.optimization_barrier((gg, ga))
    out_halves = kernels.product(ga, out_weights)
    if square_mesh:
        sums = sums + over_x(sums)
        sums, out_halves = lax.optimization_barrier((sums, out_halves))
        sums = sums + over_y(sums)
        moving = scatter_start(out_halves)
    else:
        sums = lax.psum(sums, "tensor")

    dgate, dy, dprm_gate, grad_first, terms = kernels.gate(
        cotangent_all, sums, prm, weights, gate_pre, y_total, gg, normed
    )
    if square_mesh:
        dy, grad_first, moving = lax.optimization_barrier((dy, grad_first, moving))
        far, dy = scatter_middle(out_halves, *moving, dy)
        out_moving = moving + far
    own_first = lax.psum_scatter(grad_first, "dp", scatter_dimension=0, tiled=True)
    gn_halves, grad_last, small_sum = kernels.backward(
        weights,
        gain_in,
        terms,
        dprm_gate,
        prm,
        prs,
        prh,
        [normed, dgate, dy, v, u, vs, us, scan_terms, y_scan, states],
    )

    def own_sum(halves):
        return lax.psum_scatter(
            jnp.concatenate(halves, axis=1), "tensor", scatter_dimension=0, tiled=True
        ).astype(f32)

    if square_mesh:
        gn_halves, grad_last, small_sum, own_first, out_moving = lax.optimization_barrier(
            (gn_halves, grad_last, small_sum, own_first, out_moving)
        )
        moving = scatter_start(gn_halves)
    own_last = lax.psum_scatter(grad_last, "dp", scatter_dimension=0, tiled=True)
    small_sum = sum_over_dp(small_sum)
    if square_mesh:
        small_sum, moving = lax.optimization_barrier((small_sum, moving))
        far, small_sum = scatter_middle(gn_halves, *moving, small_sum)
    small_shared = sum_over_tensor(small_sum) if square_mesh else lax.psum(small_sum, "tensor")

    if square_mesh:
        far, own_last, small_shared = lax.optimization_barrier((far, own_last, small_shared))
        own_state = own_last[:, channels:].astype(f32)
        own_state = (own_state + over_x(own_last[:, channels:]).astype(f32)).astype(bf16)
        grad_normed = scatter_end(gn_halves, *moving, *far)
        grad_normed, own_state = lax.optimization_barrier((grad_normed, own_state))
        own_state = own_state.astype(f32) + over_y(own_state).astype(f32)
        grad_normed = jnp.concatenate(grad_normed, axis=1)
        branch = jnp.concatenate(scatter_end(out_halves, *out_moving), axis=1)
    else:
        grad_normed = own_sum(gn_halves)
        own_state = lax.psum(own_last[:, channels:].astype(f32), "tensor")
        branch = own_sum(out_halves)

    own_square = lax.dynamic_slice_in_dim(sums[0], tensor_place * own_rows, own_rows, 0)
    inverse_gate = lax.rsqrt(own_square * (1.0 / INNER) + EPS)[:, None]
    values = hidden_in.astype(f32)
    block_out = (values + branch * inverse_gate).astype(bf16)

    inverse_in = lax.rsqrt(jnp.mean(values * values, axis=1, keepdims=True) + EPS)
    scaled = values * inverse_in
    grad_scaled = grad_normed * gain_in
    grad_hidden = out_cotangent.astype(f32) + inverse_in * (
        grad_scaled - scaled * jnp.mean(grad_scaled * scaled, axis=1, keepdims=True)
    )

    own_part = depth // tensor_count
    own_state = lax.dynamic_slice_in_dim(own_state, tensor_place * own_part, own_part, 0)[:, :state_width]

    def own_cut(z, size, axis):
        return lax.dynamic_slice_in_dim(z, dp_place * size, size, axis)

    by_channel = small_sum[: taps + 3, :channels].reshape(taps + 3, heads_here, HEADDIM)
    by_channel = own_cut(by_channel, cut, 2)
    by_map = own_cut(small_shared[: taps + 1, channels : channels + 2 * STATE], state_cut, 1)
    heads_at = channels + 2 * STATE
    by_head = own_cut(small_shared[:3, heads_at : heads_at + LANES], head_cut, 1)
    gain_grad = lax.dynamic_slice_in_dim(
        small_shared[8], (dp_place * tensor_count + tensor_place) * own_part, own_part, 0
    )
    own_first = own_first.astype(f32)
    return (
        block_out,
        grad_hidden,
        gain_grad,
        own_first[:, :channels],
        own_last[:, :channels].astype(f32),
        own_state,
        own_first[:, channels:].T,
        by_channel[:taps],
        by_channel[taps],
        by_map[:taps],
        by_map[taps],
        by_head[0],
        by_head[1],
        by_head[2],
        by_channel[taps + 2],
    )


def solution(mesh):
    placed = (
        P(("dp", "tensor"), None),
        P("dp"),
        P("dp", "tensor"),
        P("dp", "tensor"),
        P("dp", None),
        P(None, "tensor", "dp"),
        P("tensor", "dp"),
        P(None, "dp"),
        P("dp"),
        P("dp"),
        P("dp"),
        P("dp"),
        P("tensor", "dp"),
        P("tensor", "dp"),
        P(("dp", "tensor"), None),
        P("dp", None),
    )
    return jax.shard_map(
        per_device,
        mesh=mesh,
        in_specs=placed,
        out_specs=(
            P(("dp", "tensor"), None),
            P(("dp", "tensor"), None),
            P(("dp", "tensor")),
            P("dp", "tensor"),
            P("dp", "tensor"),
            P(("dp", "tensor"), None),
            P("tensor", "dp"),
            P(None, "tensor", "dp"),
            P("tensor", "dp"),
            P(None, "dp"),
            P("dp"),
            P("dp"),
            P("dp"),
            P("dp"),
            P("tensor", "dp"),
        ),
        check_vma=False,
    )
```

```python
import functools

import jax
import jax.numpy as jnp
import numpy as np
from jax import lax
from jax.experimental import pallas as pl
from jax.experimental.pallas import tpu as pltpu
from jax.sharding import PartitionSpec as P

HEADDIM = 64
STATE = 128
INNER = 2048
LANES = 128
ROWS = 256
WIDE_ROWS = 512
FIELD = 32
PARAMS = 16
SUB = 128
EPS = 1e-05
LOG2E = 1.4426950408889634

f32 = jnp.float32
bf16 = jnp.bfloat16


def nn(a, b):
    return lax.dot_general(a, b, (((1,), (0,)), ((), ())), preferred_element_type=f32)


def nt(a, b):
    return lax.dot_general(a, b, (((1,), (1,)), ((), ())), preferred_element_type=f32)


def tn(a, b):
    return lax.dot_general(a, b, (((0,), (0,)), ((), ())), preferred_element_type=f32)


def pieces(z, count):
    parts = []
    for _ in range(count - 1):
        part = z.astype(bf16)
        parts.append(part)
        z = z - part.astype(f32)
    parts.append(z.astype(bf16))
    return parts


def spread_heads(z, heads):
    return nn(jnp.concatenate(pieces(z, 2), axis=1), heads)


def gather_heads(z, heads):
    return nn(jnp.concatenate(pieces(z, 2), axis=1), heads)


def triangle_sum(triangle, z):
    return nn(triangle, jnp.concatenate(pieces(z, 3), axis=0))


def constants(channels):
    row, col = np.arange(ROWS)[:, None], np.arange(ROWS)[None, :]
    same = row // SUB == col // SUB
    lower = np.concatenate([same & (row >= col)] * 3, axis=1)
    upper = np.concatenate([same & (row <= col)] * 3, axis=1)
    heads = np.arange(LANES)[:, None] == np.arange(channels)[None, :] // HEADDIM
    spread = np.concatenate([heads] * 2, axis=0)
    gather = np.concatenate([heads.T] * 2, axis=0)
    return [jnp.asarray(z, bf16) for z in (lower, upper, spread, gather)]


def ends_of(len_ref, count):
    ends, total = [], 0
    for s in range(count):
        total = total + len_ref[0, s]
        ends.append(total)
    return ends


def segment_of(places, ends):
    return sum((places >= end).astype(jnp.int32) for end in ends)


def start_of(places, ends):
    start = jnp.zeros_like(places)
    for end in ends:
        start = jnp.where(places >= end, end, start)
    return start


def scan_steps(raw, decay, lower):
    step = jnp.maximum(raw, 0.0) + jnp.log1p(jnp.exp(-jnp.abs(raw)))
    return step, triangle_sum(lower, -decay * step)


def scan_weights(step, cum, base, ends, spread):
    rows = step.shape[0]
    segment = segment_of(base + lax.broadcasted_iota(jnp.int32, (rows, 1), 0), ends)
    carried, keep, survive = [], [], []
    for low in range(0, rows, SUB):
        before = segment_of(base + low - 1, ends)
        tail = segment_of(base + low + SUB - 1, ends)
        part, own = cum[low : low + SUB], segment[low : low + SUB]
        last = part[SUB - 1 :]
        carried.append(jnp.where(own == before, jnp.exp(part), 0.0))
        keep.append(jnp.where(own == tail, jnp.exp(last - part), 0.0))
        survive.append(jnp.where(tail == before, jnp.exp(last), 0.0))
    survive.append(jnp.zeros((-len(survive) % 8, LANES), f32))
    wide = spread_heads(jnp.concatenate([step] + carried + keep + survive, axis=0), spread)
    return wide[:rows], wide[rows : 2 * rows], wide[2 * rows : 3 * rows], wide[3 * rows :]


def pair_stack(z):
    lane = lax.broadcasted_iota(jnp.int32, z.shape, 1)
    zero = jnp.zeros_like(z)
    return jnp.concatenate(
        [jnp.where(lane < HEADDIM, z, zero), jnp.where(lane >= HEADDIM, z, zero)], axis=0
    )


def silu(u):
    return u * jax.nn.sigmoid(u)


def own_lanes(z, shift, count):
    moved = pltpu.roll(z, (z.shape[1] - shift) % z.shape[1], 1)
    lane = lax.broadcasted_iota(jnp.int32, z.shape, 1)
    return jnp.where(lane < count, moved, 0.0)


def nn3(a, b):
    a, a_low = pieces(a, 2)
    b, b_low = pieces(b, 2)
    return nn(jnp.concatenate([a, a_low, a], axis=1), jnp.concatenate([b, b, b_low], axis=0))


def nt3(a, b):
    a, a_low = pieces(a, 2)
    b, b_low = pieces(b, 2)
    return nt(jnp.concatenate([a, a_low, a], axis=1), jnp.concatenate([b, b, b_low], axis=1))


def pair_product(mixing, z):
    high, low = pieces(z, 2)
    both = nn(
        jnp.concatenate(mixing, axis=1),
        jnp.concatenate([pair_stack(high), pair_stack(low)], axis=1),
    )
    return both[:, :LANES] + both[:, LANES:]


def take_rows(refs, which, buffer):
    if len(refs) == 1:
        return refs[0][...]
    half = refs[3].shape[1]
    for k in range(3):

        @pl.when(which == k)
        def _(k=k):
            buffer[...] = refs[k][...]

    @pl.when(which == 3)
    def _():
        buffer[:, :half] = refs[3][...]
        buffer[:, half:] = refs[4][...]

    return buffer[...]


def put_halves(refs, which, product):
    half = product.shape[1] // 2
    left, right = product[:, :half], product[:, half:]
    if len(refs) == 2:
        refs[0][...] = left
        refs[1][...] = right
        return
    left_sent, left_kept, right_sent, right_kept = refs

    @pl.when(which % 2 == 1)
    def _():
        left_sent[...] = left

    @pl.when(which % 2 == 0)
    def _():
        left_kept[...] = left

    @pl.when(which >= 2)
    def _():
        right_sent[...] = right

    @pl.when(which < 2)
    def _():
        right_kept[...] = right


def scan_kernel(
    len_ref, first_ref, place_ref, *refs, parts, seqs, taps, head_count, first_block, kept, starts, place_at
):
    part_refs, refs = refs[:parts], refs[parts:]
    w_ref, gain_ref, prm_ref, prs_ref, prh_ref, lower_ref, spread_ref = refs[:7]
    start_refs, refs = refs[7 : 7 + starts], refs[7 + starts :]
    (
        normed_ref,
        v_ref,
        u_ref,
        vs_ref,
        us_ref,
        terms_ref,
        y_ref,
        st_ref,
        gate_ref,
        ga_ref,
        total_ref,
        square_ref,
        vtail_out,
        stail_out,
        carry,
        hid_buf,
        vbuf,
        sbuf,
    ) = refs[kept:]
    rows, channels = v_ref.shape
    step_id = pl.program_id(0)
    block = step_id + first_block
    base = block * rows
    ends = ends_of(len_ref, seqs)

    @pl.when(step_id == 0)
    def _():
        if start_refs:
            vbuf[0:8, :] = start_refs[0][...]
            sbuf[0:8, :] = start_refs[1][...]
            carry[...] = start_refs[2][...]
        else:
            vbuf[0:8, :] = jnp.zeros((8, channels), f32)
            sbuf[0:8, :] = jnp.zeros((8, 2 * STATE), f32)
            carry[...] = jnp.zeros_like(carry)

    values = take_rows(part_refs, place_ref[place_at + block], hid_buf).astype(f32)
    inverse = lax.rsqrt(jnp.mean(values * values, axis=1, keepdims=True) + EPS)
    normed = (values * inverse * gain_ref[...]).astype(bf16)
    normed_ref[...] = normed
    gate_pre = nn(normed, w_ref[:, :channels])
    gate_ref[...] = gate_pre.astype(bf16)
    conv_pre = nn(normed, w_ref[:, channels : 2 * channels])
    state_all = nn(normed, w_ref[:, 2 * channels :])
    v_ref[...] = conv_pre.astype(bf16)
    vs_ref[...] = state_all[:, : 2 * STATE].astype(bf16)
    vbuf[8 : 8 + rows, :] = conv_pre
    sbuf[8 : 8 + rows, :] = state_all[:, : 2 * STATE]
    start = start_of(base + lax.broadcasted_iota(jnp.int32, (rows, 1), 0), ends)
    u = prm_ref[taps : taps + 1, :] + prm_ref[taps - 1 : taps, :] * conv_pre
    us = prs_ref[taps : taps + 1, :] + prs_ref[taps - 1 : taps, :] * state_all[:, : 2 * STATE]
    for lag in range(1, taps):
        usable = base + lax.broadcasted_iota(jnp.int32, (rows, 1), 0) - lag >= start
        tap = taps - 1 - lag
        u = u + prm_ref[tap : tap + 1, :] * jnp.where(usable, vbuf[8 - lag : 8 - lag + rows, :], 0.0)
        us = us + prs_ref[tap : tap + 1, :] * jnp.where(usable, sbuf[8 - lag : 8 - lag + rows, :], 0.0)
    vbuf[0:8, :] = vbuf[rows : rows + 8, :]
    sbuf[0:8, :] = sbuf[rows : rows + 8, :]
    vtail_out[...] = vbuf[0:8, :]
    stail_out[...] = sbuf[0:8, :]
    u_ref[...] = u
    us_ref[...] = us
    raw = own_lanes(state_all[:, 2 * STATE :], first_ref[0], head_count) + prh_ref[0:1, :]

    x = silu(u)
    maps = silu(us)
    step, cum = scan_steps(raw, prh_ref[1:2, :], lower_ref[...])
    lane = lax.broadcasted_iota(jnp.int32, (rows, LANES), 1)
    terms_ref[...] = jnp.where(
        lane < FIELD,
        step,
        jnp.where(lane < 2 * FIELD, pltpu.roll(raw, FIELD, 1), pltpu.roll(cum, 2 * FIELD, 1)),
    )
    step_w, carried_w, keep_w, survive_w = scan_weights(step, cum, base, ends, spread_ref[...])
    cum = cum * LOG2E
    cum_row = cum.T
    stepped = step_w * x
    kept_b = keep_w * stepped
    row = lax.broadcasted_iota(jnp.int32, (SUB, SUB), 0)
    col = lax.broadcasted_iota(jnp.int32, (SUB, SUB), 1)
    state = carry[...]
    y_parts = []
    for q in range(rows // SUB):
        at = slice(q * SUB, (q + 1) * SUB)
        low = base + q * SUB
        mask = (row >= col) & (segment_of(low + row, ends) == segment_of(low + col, ends))
        b_map, c_map = maps[at, :STATE], maps[at, STATE:]
        gram = jnp.where(mask, nt3(c_map, b_map), 0.0)
        st_ref[q] = state
        outer = carried_w[at] * nn3(c_map, state)
        inner = []
        for pair in range(channels // LANES):
            mixing = []
            for h in (2 * pair, 2 * pair + 1):
                spread = cum[at, h : h + 1] - cum_row[h : h + 1, at]
                mixing.append((jnp.exp2(jnp.minimum(spread, 0.0)) * gram).astype(bf16))
            inner.append(pair_product(mixing, stepped[at, pair * LANES : (pair + 1) * LANES]))
        y_parts.append(jnp.concatenate(inner, axis=1) + outer)
        state = survive_w[q : q + 1] * state + nn3(b_map.T, kept_b[at])
    carry[...] = state
    y_scan = jnp.concatenate(y_parts, axis=0)
    y_ref[...] = y_scan
    y_total = y_scan + prm_ref[taps + 1 : taps + 2, :] * x
    total_ref[...] = y_total.astype(bf16)
    g = y_total * silu(gate_pre)
    ga_ref[...] = (g * prm_ref[taps + 2 : taps + 3, :]).astype(bf16)
    square = jnp.sum(g * g, axis=1, keepdims=True)
    square_ref[...] = jnp.broadcast_to(square, (rows, LANES)).T[:8, :]


def parameter_kernel(
    first_ref, packed_ref, prm_ref, prs_ref, prh_ref, gain_ref, *, taps, heads_here, cut, state_cut, head_cut, depth
):
    packed = packed_ref[...]
    total = packed.shape[1]
    rows = prm_ref.shape[0]
    source = lax.broadcasted_iota(jnp.int32, (total, 1), 0)
    maps_at = heads_here * cut

    def split(z, size):
        return z >> (size.bit_length() - 1), z & (size - 1)

    def moved(columns, lane_of):
        lane = lane_of(lax.broadcasted_iota(jnp.int32, (1, columns), 1))
        return nn(packed, jnp.where(source == lane, 1.0, 0.0).astype(bf16))[:rows]

    def by_channel(c):
        head, inside = split(c, HEADDIM)
        owner, place = split(inside, cut)
        return owner * LANES + head * cut + place

    def by_part(size, at):
        def lane_of(c):
            owner, place = split(c, size)
            return owner * LANES + at + place

        return lane_of

    def own_head(at):
        part = by_part(head_cut, at)
        return lambda h: jnp.where(h < heads_here, part(first_ref[0] + h), -1)

    channels = prm_ref.shape[1]
    row = lax.broadcasted_iota(jnp.int32, (rows, 1), 0)
    by_head = moved(channels, by_channel)
    skip = by_part(head_cut, maps_at + 2 * head_cut)
    skips = moved(channels, lambda c: skip(first_ref[0] + split(c, HEADDIM)[0]))
    prm_ref[...] = jnp.where(
        row <= taps,
        by_head,
        jnp.where(row == taps + 1, skips, jnp.where(row == taps + 2, pltpu.roll(by_head, 1, 0), 0.0)),
    )
    prs_ref[...] = jnp.where(row <= taps, moved(2 * STATE, by_part(state_cut, maps_at)), 0.0)
    bias = moved(LANES, own_head(maps_at))[taps + 1 : taps + 2]
    rate = jnp.exp(moved(LANES, own_head(maps_at + head_cut))[taps + 1 : taps + 2])
    lane = lax.broadcasted_iota(jnp.int32, (1, LANES), 1)
    rate = jnp.where(lane < heads_here, rate, 0.0)
    prh_ref[...] = jnp.where(row == 0, bias, jnp.where(row == 1, rate, 0.0))
    gain_ref[...] = moved(gain_ref.shape[1], by_part(depth, 0))[taps + 2 : taps + 3]


def product_kernel(place_ref, ga_ref, w_ref, *refs, place_at):
    product = nt(ga_ref[...], w_ref[...]).astype(bf16)
    put_halves(refs, place_ref[place_at + pl.program_id(0)], product)


def cotangent_kernel(place_ref, *refs, parts, place_at):
    part_refs, refs = refs[:parts], refs[parts:]
    w_ref, ga_ref, square_ref, gg_ref, sums_ref, cot_buf = refs
    rows = gg_ref.shape[0]
    cotangent = take_rows(part_refs, place_ref[place_at + pl.program_id(0)], cot_buf)
    grad_gated = nn(cotangent, w_ref[...])
    gg_ref[...] = grad_gated.astype(bf16)
    inner = jnp.sum(grad_gated * ga_ref[...].astype(f32), axis=1, keepdims=True)
    inner_row = jnp.broadcast_to(inner, (rows, LANES)).T[:8, :]
    sublane = lax.broadcasted_iota(jnp.int32, (8, rows), 0)
    sums_ref[...] = jnp.where(sublane == 0, square_ref[...], inner_row)


def gain_row(weights, grads):
    terms = jnp.sum(weights.astype(f32) * grads, axis=1, keepdims=True)
    return jnp.broadcast_to(terms, (terms.shape[0], LANES)).T[:8, :]


def gate_kernel(place_ref, *refs, parts, taps, place_at):
    part_refs, refs = refs[:parts], refs[parts:]
    (
        sums_ref,
        prm_ref,
        w_ref,
        gate_ref,
        y_ref,
        gg_ref,
        normed_ref,
        dgate_ref,
        dy_ref,
        dprm_ref,
        out_ref,
        gain_ref,
        cot_buf,
        total,
    ) = refs
    rows, channels = gate_ref.shape
    step_id = pl.program_id(0)

    @pl.when(step_id == 0)
    def _():
        dprm_ref[...] = jnp.zeros_like(dprm_ref)
        total[...] = jnp.zeros_like(total)

    sums = jnp.concatenate([sums_ref[...], jnp.zeros((LANES - 8, rows), f32)], axis=0).T
    inverse = lax.rsqrt(sums[:, 0:1] * (1.0 / INNER) + EPS)
    inner_mean = sums[:, 1:2] * inverse * (1.0 / INNER)
    normed = normed_ref[...]
    cotangent = take_rows(part_refs, place_ref[place_at + step_id], cot_buf)
    gain = prm_ref[taps + 2 : taps + 3, :]
    gate_pre = gate_ref[...].astype(f32)
    sig_gate = jax.nn.sigmoid(gate_pre)
    act = gate_pre * sig_gate
    y = y_ref[...].astype(f32)
    hat = y * act * inverse
    gated = (hat * gain).astype(bf16)
    total[:, channels:] += tn(cotangent, gated)
    grad_gated = gg_ref[...].astype(f32)
    dprm_ref[taps + 2 : taps + 3, :] += jnp.sum(grad_gated * hat, axis=0, keepdims=True)
    grad_inner = inverse * (grad_gated * gain - hat * inner_mean)
    dy_ref[...] = grad_inner * act
    dgate = (grad_inner * y * sig_gate * (1.0 + gate_pre * (1.0 - sig_gate))).astype(bf16)
    dgate_ref[...] = dgate
    total[:, :channels] += tn(normed, dgate)

    @pl.when(step_id == pl.num_programs(0) - 1)
    def _():
        out_ref[...] = total[...].astype(bf16)
        gain_ref[...] = gain_row(w_ref[...], total[:, :channels])


def backward_kernel(len_ref, first_ref, place_ref, *refs, seqs, taps, halves, place_at):
    (
        w_ref,
        gain_ref,
        terms_ref,
        dprm_gate_ref,
        prm_ref,
        prs_ref,
        prh_ref,
        upper_ref,
        spread_ref,
        gather_ref,
        normed_ref,
        dgate_ref,
        dy_ref,
        v_ref,
        u_ref,
        vs_ref,
        us_ref,
        scan_ref,
        y_ref,
        st_ref,
    ) = refs[:20]
    half_refs = refs[20 : 20 + halves]
    out_ref, small_ref, dprm_ref, dprs_ref, dprh_ref, dbuf, dsbuf, carry, ending, total = refs[20 + halves :]
    rows, channels = dgate_ref.shape
    step_id = pl.program_id(0)
    base = (pl.num_programs(0) - 1 - step_id) * rows
    ends = ends_of(len_ref, seqs)

    @pl.when(step_id == 0)
    def _():
        dbuf[rows : rows + 8, :] = jnp.zeros((8, channels), f32)
        dsbuf[rows : rows + 8, :] = jnp.zeros((8, 2 * STATE), f32)
        carry[...] = jnp.zeros_like(carry)
        ending[...] = jnp.zeros_like(ending)
        dprm_ref[...] = jnp.zeros_like(dprm_ref)
        dprs_ref[...] = jnp.zeros_like(dprs_ref)
        dprh_ref[...] = jnp.zeros_like(dprh_ref)
        total[...] = jnp.zeros_like(total)

    def add_row(ref, at, z):
        ref[at : at + 1, :] += jnp.sum(z, axis=0, keepdims=True)

    skip = prm_ref[taps + 1 : taps + 2, :]
    u = u_ref[...]
    sig_u = jax.nn.sigmoid(u)
    x = u * sig_u
    y_scan = y_ref[...]
    dy = dy_ref[...]
    dy_b = dy.astype(bf16)

    add_row(dprm_ref, taps + 1, dy * x)
    us = us_ref[...]
    sig_us = jax.nn.sigmoid(us)
    maps = us * sig_us
    maps_b = maps.astype(bf16)
    terms = scan_ref[...]
    lane = lax.broadcasted_iota(jnp.int32, (rows, LANES), 1)
    inside = lane < FIELD
    step = jnp.where(inside, terms, 0.0)
    raw = jnp.where(inside, pltpu.roll(terms, LANES - FIELD, 1), 0.0)
    cum = jnp.where(inside, pltpu.roll(terms, LANES - 2 * FIELD, 1), 0.0)
    decay = prh_ref[1:2, :]
    step_w, carried_w, keep_w, survive_w = scan_weights(step, cum, base, ends, spread_ref[...])
    cum = cum * LOG2E
    cum_row = cum.T
    stepped = step_w * x
    stepped_b = stepped.astype(bf16)
    kept_b = (keep_w * stepped).astype(bf16)
    dy_carried = carried_w * dy
    dy_carried_b = dy_carried.astype(bf16)
    row = lax.broadcasted_iota(jnp.int32, (SUB, SUB), 0)
    col = lax.broadcasted_iota(jnp.int32, (SUB, SUB), 1)
    dstate = carry[...]
    state_end = ending[0:1, :]
    subs = rows // SUB
    dsteppeds, dmaps, state_ends = [None] * subs, [None] * subs, [None] * subs
    for q in reversed(range(subs)):
        at = slice(q * SUB, (q + 1) * SUB)
        low = base + q * SUB
        mask = (row <= col) & (segment_of(low + row, ends) == segment_of(low + col, ends))
        b_map, c_map = maps[at, :STATE], maps[at, STATE:]
        gram = jnp.where(mask, nt3(b_map, c_map), 0.0)
        state = st_ref[q]
        dstate_b = dstate.astype(bf16)
        dgram = jnp.zeros((SUB, SUB), f32)
        inner = []
        for pair in range(channels // LANES):
            lanes = slice(pair * LANES, (pair + 1) * LANES)
            dmix = nt(pair_stack(stepped_b[at, lanes]), dy_b[at, lanes])
            mixing = []
            for i, h in enumerate((2 * pair, 2 * pair + 1)):
                spread = cum_row[h : h + 1, at] - cum[at, h : h + 1]
                weight = jnp.exp2(jnp.minimum(spread, 0.0))
                mixing.append((weight * gram).astype(bf16))
                dgram = dgram + dmix[i * SUB : (i + 1) * SUB] * weight
            inner.append(pair_product(mixing, dy[at, lanes]))
        dsteppeds[q] = jnp.concatenate(inner, axis=1) + keep_w[at] * nn3(b_map, dstate)
        dgram = jnp.where(mask, dgram, 0.0).astype(bf16)
        db = nn(dgram, maps_b[at, STATE:]) + nt(kept_b[at], dstate_b)
        dc = tn(dgram, maps_b[at, :STATE]) + nt(dy_carried_b[at], state.astype(bf16))
        dmaps[q] = jnp.concatenate([db, dc], axis=1)
        state_ends[q] = state_end
        dstate = survive_w[q : q + 1] * dstate + nn3(c_map.T, dy_carried[at])
        state_end = jnp.sum(state * dstate, axis=0, keepdims=True)
    carry[...] = dstate
    ending[0:1, :] = state_end
    dstepped = jnp.concatenate(dsteppeds, axis=0)
    dmap = jnp.concatenate(dmaps, axis=0)
    state_ends.append(jnp.zeros((-subs % 8, channels), f32))
    by_head = gather_heads(
        jnp.concatenate([dy * y_scan - stepped * dstepped, x * dstepped] + state_ends, axis=0),
        gather_ref[...],
    )
    dlog = triangle_sum(upper_ref[...], by_head[:rows])
    dlog = jnp.concatenate(
        [
            dlog[q * SUB : (q + 1) * SUB] + by_head[2 * rows + q : 2 * rows + q + 1]
            for q in range(subs)
        ],
        axis=0,
    )
    draw = (by_head[rows : 2 * rows] - decay * dlog) * jax.nn.sigmoid(raw)
    add_row(dprh_ref, 0, draw)
    add_row(dprh_ref, 1, dlog * step * -decay)
    places = base + lax.broadcasted_iota(jnp.int32, (rows, 1), 0)
    segment = segment_of(places, ends)
    usable = [None] + [segment_of(places + lag, ends) == segment for lag in range(1, taps)]
    normed = normed_ref[...]

    def conv_back(du, v, weight_ref, buffer, sums_ref):
        buffer[0:rows, :] = du
        dv = weight_ref[taps - 1 : taps, :] * du
        lines = [jnp.sum(du * v, axis=0, keepdims=True), jnp.sum(du, axis=0, keepdims=True)]
        for lag in range(1, taps):
            later = jnp.where(usable[lag], buffer[lag : lag + rows, :], 0.0)
            dv = dv + weight_ref[taps - 1 - lag : taps - lag, :] * later
            lines.insert(0, jnp.sum(later * v, axis=0, keepdims=True))
        buffer[rows : rows + 8, :] = buffer[0:8, :]
        sums_ref[0 : taps + 1, :] += jnp.concatenate(lines, axis=0)
        return dv.astype(bf16)

    product = nt(dgate_ref[...], w_ref[:, :channels])
    du = (step_w * dstepped + skip * dy) * sig_u * (1.0 + u * (1.0 - sig_u))
    dv = conv_back(du, v_ref[...].astype(f32), prm_ref, dbuf, dprm_ref)
    product = product + nt(dv, w_ref[:, channels : 2 * channels])
    total[:, :channels] += tn(normed, dv)
    dus = dmap * sig_us * (1.0 + us * (1.0 - sig_us))
    dvs = conv_back(dus, vs_ref[...].astype(f32), prs_ref, dsbuf, dprs_ref)
    state_part = jnp.concatenate([dvs, pltpu.roll(draw, first_ref[0], 1).astype(bf16)], axis=1)
    product = product + nt(state_part, w_ref[:, 2 * channels :])
    total[:, channels:] += tn(normed, state_part)
    put_halves(half_refs, place_ref[place_at + step_id], product.astype(bf16))

    @pl.when(step_id == pl.num_programs(0) - 1)
    def _():
        grads = total[...]
        out_ref[...] = grads.astype(bf16)
        gains = (gain_row(w_ref[:, channels:], grads) + terms_ref[...]) / gain_ref[...]
        line = lax.broadcasted_iota(jnp.int32, (8, 1), 0)
        both = jnp.where(line == taps + 2, dprm_gate_ref[...], dprm_ref[...])
        skips = gather_heads(dprm_ref[...], gather_ref[...])
        by_head = jnp.where(line == 2, pltpu.roll(skips, 8 - (taps - 1), 0), dprh_ref[...])
        small_ref[...] = jnp.zeros_like(small_ref)
        small_ref[0:8, :channels] = both
        small_ref[0:8, channels : channels + 2 * STATE] = dprs_ref[...]
        small_ref[0:8, channels + 2 * STATE : channels + 2 * STATE + LANES] = pltpu.roll(
            by_head, first_ref[0], 1
        )
        small_ref[8:16, :] = gains


def held(places):
    last = next(p for p in places if p is not None)
    filled = []
    for p in places:
        last = last if p is None else p
        filled.append(last)
    return filled


def place_table(tensor_place, quarter_blocks, order):
    relative = [(b // quarter_blocks) ^ tensor_place for b in order]
    inside = [b % quarter_blocks for b in order]

    def places(slots):
        return held(
            [slots.index(r) * quarter_blocks + w if r in slots else None for r, w in zip(relative, inside)]
        )

    return [
        relative,
        places([0]),
        places([1]),
        places([2]),
        places([3]),
        places([1, 3]),
        places([0, 2]),
        places([2, 3]),
        places([0, 1]),
    ]


def over_x(z):
    return lax.ppermute(z, "tensor", [(0, 1), (1, 0), (2, 3), (3, 2)])


def over_y(z):
    return lax.ppermute(z, "tensor", [(0, 2), (2, 0), (1, 3), (3, 1)])


def gather_start(z):
    return over_x(z), over_y(z)


def gather_end(z, from_x, from_y, after=()):
    half = z.shape[1] // 2
    far = (from_x[:, :half], from_y[:, half:])
    far, after = lax.optimization_barrier((far, after))
    return [z, from_x, from_y, over_y(far[0]), over_x(far[1])], after


def scatter_start(halves):
    return over_x(halves[0]), over_y(halves[2])


def scatter_middle(halves, from_x, from_y, after=()):
    rows = from_x.shape[0] // 2
    left, right = halves[1], halves[3]
    left_far = left[rows:].astype(f32) + from_x[rows:].astype(f32)
    right_far = right[rows:].astype(f32) + from_y[rows:].astype(f32)
    far = (left_far.astype(bf16), right_far.astype(bf16))
    far, after = lax.optimization_barrier((far, after))
    return (over_y(far[0]), over_x(far[1])), after


def scatter_end(halves, from_x, from_y, far_left, far_right):
    rows = from_x.shape[0] // 2
    left, right = halves[1][:rows].astype(f32), halves[3][:rows].astype(f32)
    left = left + from_x[:rows].astype(f32) + far_left.astype(f32)
    right = right + from_y[:rows].astype(f32) + far_right.astype(f32)
    return left, right


def sum_over_tensor(z):
    z = (z.astype(f32) + over_x(z).astype(f32)).astype(z.dtype)
    return z.astype(f32) + over_y(z).astype(f32)


def sum_over_dp(z):
    count = lax.axis_size("dp")
    bit = 1
    while bit < count:
        z = z + lax.ppermute(z, "dp", [(i, i ^ bit) for i in range(count)])
        bit *= 2
    return z


class Kernels:
    def __init__(self, lengths, first, tensor_place, tensor_count, group_rows, width, channels, taps, head_count):
        self.lengths, self.first = lengths, first
        self.tensor_place, self.tensor_count = tensor_place, tensor_count
        self.square = tensor_count == 4
        self.group_rows, self.width, self.channels = group_rows, width, channels
        self.taps, self.head_count = taps, head_count
        self.seqs = lengths.shape[1]
        self.lower, self.upper, self.spread, self.gather = constants(channels)
        self.tables()

    def tables(self):
        kinds = ((ROWS, False), (ROWS, True), (WIDE_ROWS, False))
        self.kinds = {kind: k for k, kind in enumerate(kinds)}
        places = range(4) if self.square else range(1)
        made = []
        for t in places:
            lines = []
            for block, backwards in kinds:
                order = list(range(self.group_rows // block))[:: -1 if backwards else 1]
                table = place_table(t, len(order) // 4, order) if self.square else [order]
                lines += [line + [0] * (self.group_rows // ROWS - len(order)) for line in table]
            made.append(lines)
        self.lines = len(made[0]) // len(kinds)
        made = jnp.asarray(np.array(made, np.int32).reshape(len(made), -1))
        place = self.tensor_place if self.square else 0
        self.place = lax.dynamic_index_in_dim(made, place, 0, keepdims=False)
        self.steps = self.group_rows // ROWS

    def at(self, block, backwards, line):
        return (self.kinds[(block, backwards)] * self.lines + line) * self.steps

    def call(self, kernel, scalars, steps, ins, outs, scratch, aliases=None, flops=1000):
        specs, arrays = zip(*ins)
        out_specs, out_shapes = zip(*outs)
        return pl.pallas_call(
            kernel,
            grid_spec=pltpu.PrefetchScalarGridSpec(
                num_scalar_prefetch=len(scalars),
                grid=(steps,),
                in_specs=list(specs),
                out_specs=list(out_specs),
                scratch_shapes=scratch,
            ),
            out_shape=list(out_shapes),
            input_output_aliases=aliases or {},
            compiler_params=pltpu.CompilerParams(vmem_limit_bytes=56 * 2**20),
            cost_estimate=pl.CostEstimate(flops=flops, bytes_accessed=1000, transcendentals=0),
            name=getattr(kernel, "func", kernel).__name__,
        )(*scalars, *arrays)

    def whole(self, array):
        return pl.BlockSpec(array.shape, lambda i, *s: (0,) * len(array.shape)), array

    def columns(self, array, width, place):
        return pl.BlockSpec((array.shape[0], width), lambda i, *s: (0, place)), array

    def rows(self, array, block, backwards=False, low=0):
        last = self.group_rows // block - 1

        def at(i, *s):
            return (last - i if backwards else i + low,) + (0,) * (len(array.shape) - 1)

        size = array.shape[0] * block // self.group_rows
        return pl.BlockSpec((size,) + array.shape[1:], at), array

    def across(self, array, block, low=0):
        return pl.BlockSpec((8, block), lambda i, *s: (0, i + low)), array

    def out(self, columns, dtype):
        return jax.ShapeDtypeStruct((self.group_rows, columns), dtype)

    def parts(self, arrays, block, low=0):
        if not self.square:
            return [self.rows(arrays[0], block, low=low)]
        return [
            (
                pl.BlockSpec(
                    (block, z.shape[1]), lambda i, *s, at=self.at(block, False, k): (s[-1][at + i + low], 0)
                ),
                z,
            )
            for k, z in zip((1, 2, 3, 4, 4), arrays)
        ]

    def halves(self, block, backwards=False):
        half = self.width // 2
        lines = (5, 6, 7, 8) if self.square else (0, 0)
        rows = self.group_rows // 2 if self.square else self.group_rows
        shape = jax.ShapeDtypeStruct((rows, half), bf16)
        return [
            (
                pl.BlockSpec((block, half), lambda i, *s, at=self.at(block, backwards, k): (s[-1][at + i], 0)),
                shape,
            )
            for k in lines
        ]

    def parameters(self, packed, cut, state_cut, head_cut, depth):
        shapes = ((8, self.channels), (8, 2 * STATE), (8, LANES), (1, self.width))
        return self.call(
            functools.partial(
                parameter_kernel,
                taps=self.taps,
                heads_here=self.head_count,
                cut=cut,
                state_cut=state_cut,
                head_cut=head_cut,
                depth=depth,
            ),
            (self.first,),
            1,
            [self.whole(packed)],
            [self.whole(jax.ShapeDtypeStruct(shape, f32)) for shape in shapes],
            [],
        )

    def scan(self, low, high, hidden, weights, gain, prm, prs, prh, carried, before=()):
        channels, count = self.channels, self.group_rows
        parts = self.parts(hidden, ROWS, low)
        shapes = [
            self.out(self.width, bf16),
            self.out(channels, bf16),
            self.out(channels, f32),
            self.out(2 * STATE, bf16),
            self.out(2 * STATE, f32),
            self.out(LANES, f32),
            self.out(channels, f32),
            jax.ShapeDtypeStruct((count // SUB, STATE, channels), f32),
            self.out(channels, bf16),
            self.out(channels, bf16),
            self.out(channels, bf16),
        ]
        outs = [self.rows(z, ROWS, low=low) for z in shapes]
        outs.append(self.across(jax.ShapeDtypeStruct((8, count), f32), ROWS, low))
        kept = len(outs)
        ins = parts + [self.whole(z) for z in [weights, gain, prm, prs, prh, self.lower, self.spread] + list(carried)]
        aliases = {3 + len(ins) + k: k for k in range(len(before))}
        ins += [(pl.BlockSpec(memory_space=pl.ANY), z) for z in before]
        sizes = ((8, channels), (8, 2 * STATE), (STATE, channels))
        outs += [self.whole(jax.ShapeDtypeStruct(size, f32)) for size in sizes]
        result = self.call(
            functools.partial(
                scan_kernel,
                parts=len(parts),
                seqs=self.seqs,
                taps=self.taps,
                head_count=self.head_count,
                first_block=low,
                kept=len(before),
                starts=len(carried),
                place_at=self.at(ROWS, False, 0),
            ),
            (self.lengths, self.first, self.place),
            high - low,
            ins,
            outs,
            [
                pltpu.VMEM((ROWS, self.width), bf16),
                pltpu.VMEM((ROWS + 8, channels), f32),
                pltpu.VMEM((ROWS + 8, 2 * STATE), f32),
            ],
            aliases,
        )
        return result[:kept], result[kept:]

    def product(self, ga, weights):
        return self.call(
            functools.partial(product_kernel, place_at=self.at(WIDE_ROWS, False, 0)),
            (self.place,),
            self.group_rows // WIDE_ROWS,
            [self.rows(ga, WIDE_ROWS), self.whole(weights)],
            self.halves(WIDE_ROWS),
            [],
        )

    def cotangent(self, cotangent, weights, ga, square):
        parts = self.parts(cotangent, WIDE_ROWS)
        return self.call(
            functools.partial(cotangent_kernel, parts=len(parts), place_at=self.at(WIDE_ROWS, False, 0)),
            (self.place,),
            self.group_rows // WIDE_ROWS,
            parts + [self.whole(weights), self.rows(ga, WIDE_ROWS), self.across(square, WIDE_ROWS)],
            [
                self.rows(self.out(self.channels, bf16), WIDE_ROWS),
                self.across(jax.ShapeDtypeStruct((8, self.group_rows), f32), WIDE_ROWS),
            ],
            [pltpu.VMEM((WIDE_ROWS, self.width), bf16)],
        )

    def gate(self, cotangent, sums, prm, weights, gate, y, gg, normed):
        channels = self.channels
        parts = self.parts(cotangent, WIDE_ROWS)
        return self.call(
            functools.partial(
                gate_kernel, parts=len(parts), taps=self.taps, place_at=self.at(WIDE_ROWS, False, 0)
            ),
            (self.place,),
            self.group_rows // WIDE_ROWS,
            parts
            + [self.across(sums, WIDE_ROWS), self.whole(prm), self.columns(weights, channels, 0)]
            + [self.rows(z, WIDE_ROWS) for z in (gate, y, gg, normed)],
            [
                self.rows(self.out(channels, bf16), WIDE_ROWS),
                self.rows(self.out(channels, f32), WIDE_ROWS),
                self.whole(jax.ShapeDtypeStruct(prm.shape, f32)),
                self.whole(jax.ShapeDtypeStruct((self.width, 2 * channels), bf16)),
                self.whole(jax.ShapeDtypeStruct((8, self.width), f32)),
            ],
            [pltpu.VMEM((WIDE_ROWS, self.width), bf16), pltpu.VMEM((self.width, 2 * channels), f32)],
            flops=8 * self.group_rows * self.width * channels * 4,
        )

    def backward(self, weights, gain, terms, dprm_gate, prm, prs, prh, saved):
        channels = self.channels
        gradients = channels + 3 * STATE
        halves = self.halves(ROWS, True)
        shapes = [
            jax.ShapeDtypeStruct((self.width, gradients), bf16),
            jax.ShapeDtypeStruct((16, self.width), f32),
        ]
        shapes += [jax.ShapeDtypeStruct(z.shape, f32) for z in (prm, prs, prh)]
        result = self.call(
            functools.partial(
                backward_kernel,
                seqs=self.seqs,
                taps=self.taps,
                halves=len(halves),
                place_at=self.at(ROWS, True, 0),
            ),
            (self.lengths, self.first, self.place),
            self.group_rows // ROWS,
            [
                self.whole(z)
                for z in (weights, gain, terms, dprm_gate, prm, prs, prh, self.upper, self.spread, self.gather)
            ]
            + [self.rows(z, ROWS, True) for z in saved],
            halves + [self.whole(z) for z in shapes],
            [
                pltpu.VMEM((ROWS + 8, channels), f32),
                pltpu.VMEM((ROWS + 8, 2 * STATE), f32),
                pltpu.VMEM((STATE, channels), f32),
                pltpu.VMEM((8, channels), f32),
                pltpu.VMEM((self.width, gradients), f32),
            ],
        )
        return result[: len(halves)], result[len(halves)], result[len(halves) + 1]


def per_device(
    hidden_in,
    norm_gain,
    proj_gate,
    proj_conv,
    proj_state,
    conv_kernel,
    conv_offset,
    state_kernel,
    state_offset,
    step_bias,
    decay_log,
    skip_gain,
    gate_gain,
    proj_out,
    out_cotangent,
    seq_lengths,
):
    tensor_count = lax.axis_size("tensor")
    tensor_place = lax.axis_index("tensor")
    dp_count = lax.axis_size("dp")
    dp_place = lax.axis_index("dp")
    square_mesh = tensor_count == 4
    own_rows, width = hidden_in.shape
    depth, channels = proj_gate.shape
    taps, heads_here, cut = conv_kernel.shape
    head_cut = step_bias.shape[0]
    state_cut = state_kernel.shape[1]
    state_width = proj_state.shape[1]
    group_rows = own_rows * tensor_count
    first_head = (tensor_place * heads_here).astype(jnp.int32)

    state_part = jnp.pad(proj_state, ((0, 0), (0, 3 * STATE - state_width)))
    weights = lax.all_gather(
        jnp.concatenate([proj_gate, proj_conv, state_part], axis=1), "dp", axis=0, tiled=True
    )
    out_weights = lax.all_gather(proj_out.T, "dp", axis=0, tiled=True)
    if square_mesh:
        from_x, from_y = gather_start(hidden_in)

    def padded(z):
        return jnp.pad(z, ((0, 0), (0, LANES - z.shape[1])))

    packed = jnp.concatenate(
        [
            padded(jnp.concatenate([conv_kernel.reshape(taps, -1), state_kernel], axis=1)),
            padded(jnp.concatenate([conv_offset.reshape(1, -1), state_offset[None]], axis=1)),
            padded(
                jnp.concatenate(
                    [gate_gain.reshape(1, -1), step_bias[None], decay_log[None], skip_gain[None]], axis=1
                )
            ),
            padded(norm_gain[None]),
        ],
        axis=0,
    )
    packed = jnp.pad(packed, ((0, PARAMS - packed.shape[0]), (0, 0)))
    packed = lax.all_gather(packed, "dp", axis=1, tiled=True)
    if square_mesh:
        from_x, from_y, packed = lax.optimization_barrier((from_x, from_y, packed))
        hidden_all, _ = gather_end(hidden_in, from_x, from_y)
    else:
        hidden_all = [lax.all_gather(hidden_in, "tensor", axis=0, tiled=True)]

    kernels = Kernels(
        seq_lengths,
        first_head.reshape(1),
        tensor_place,
        tensor_count,
        group_rows,
        width,
        channels,
        taps,
        heads_here,
    )

    prm, prs, prh, gain_in = kernels.parameters(packed, cut, state_cut, head_cut, depth)
    if square_mesh:
        hidden_all, prm, kernels.place, cot = lax.optimization_barrier(
            (hidden_all, prm, kernels.place, out_cotangent)
        )

    blocks = group_rows // ROWS
    common = (hidden_all, weights, gain_in, prm, prs, prh)
    if square_mesh:
        moving = gather_start(cot)
        middle = blocks * 3 // 4
        saved, carried = kernels.scan(0, middle, *common, ())
        carried, moving = lax.optimization_barrier((carried, moving))
        cotangent_all, carried = gather_end(cot, *moving, carried)
        saved, _ = kernels.scan(middle, blocks, *common, carried, saved)
    else:
        cotangent_all = [lax.all_gather(out_cotangent, "tensor", axis=0, tiled=True)]
        saved, _ = kernels.scan(0, blocks, *common, ())
    normed, v, u, vs, us, scan_terms, y_scan, states, gate_pre, ga, y_total, square = saved
    gg, sums = kernels.cotangent(cotangent_all, out_weights, ga, square)
    gg, ga = lax.optimization_barrier((gg, ga))
    out_halves = kernels.product(ga, out_weights)
    if square_mesh:
        sums = sums + over_x(sums)
        sums, out_halves = lax.optimization_barrier((sums, out_halves))
        sums = sums + over_y(sums)
        moving = scatter_start(out_halves)
    else:
        sums = lax.psum(sums, "tensor")

    dgate, dy, dprm_gate, grad_first, terms = kernels.gate(
        cotangent_all, sums, prm, weights, gate_pre, y_total, gg, normed
    )
    if square_mesh:
        dy, grad_first, moving = lax.optimization_barrier((dy, grad_first, moving))
        far, dy = scatter_middle(out_halves, *moving, dy)
        out_moving = moving + far
    own_first = lax.psum_scatter(grad_first, "dp", scatter_dimension=0, tiled=True)
    gn_halves, grad_last, small_sum = kernels.backward(
        weights,
        gain_in,
        terms,
        dprm_gate,
        prm,
        prs,
        prh,
        [normed, dgate, dy, v, u, vs, us, scan_terms, y_scan, states],
    )

    def own_sum(halves):
        return lax.psum_scatter(
            jnp.concatenate(halves, axis=1), "tensor", scatter_dimension=0, tiled=True
        ).astype(f32)

    if square_mesh:
        gn_halves, grad_last, small_sum, own_first, out_moving = lax.optimization_barrier(
            (gn_halves, grad_last, small_sum, own_first, out_moving)
        )
        moving = scatter_start(gn_halves)
    own_last = lax.psum_scatter(grad_last, "dp", scatter_dimension=0, tiled=True)
    small_sum = sum_over_dp(small_sum)
    if square_mesh:
        small_x = small_sum + over_x(small_sum)
        small_x, moving = lax.optimization_barrier((small_x, moving))
        small_shared = small_x + over_y(small_x)
        far, small_shared = scatter_middle(gn_halves, *moving, small_shared)
    else:
        small_shared = lax.psum(small_sum, "tensor")

    if square_mesh:
        far, own_last = lax.optimization_barrier((far, own_last))
        own_state = own_last[:, channels:].astype(f32)
        own_state = (own_state + over_x(own_last[:, channels:]).astype(f32)).astype(bf16)
        grad_normed = scatter_end(gn_halves, *moving, *far)
        grad_normed, own_state = lax.optimization_barrier((grad_normed, own_state))
        own_state = own_state.astype(f32) + over_y(own_state).astype(f32)
        grad_normed = jnp.concatenate(grad_normed, axis=1)
        branch = jnp.concatenate(scatter_end(out_halves, *out_moving), axis=1)
    else:
        grad_normed = own_sum(gn_halves)
        own_state = lax.psum(own_last[:, channels:].astype(f32), "tensor")
        branch = own_sum(out_halves)

    own_square = lax.dynamic_slice_in_dim(sums[0], tensor_place * own_rows, own_rows, 0)
    inverse_gate = lax.rsqrt(own_square * (1.0 / INNER) + EPS)[:, None]
    values = hidden_in.astype(f32)
    block_out = (values + branch * inverse_gate).astype(bf16)

    inverse_in = lax.rsqrt(jnp.mean(values * values, axis=1, keepdims=True) + EPS)
    scaled = values * inverse_in
    grad_scaled = grad_normed * gain_in
    grad_hidden = out_cotangent.astype(f32) + inverse_in * (
        grad_scaled - scaled * jnp.mean(grad_scaled * scaled, axis=1, keepdims=True)
    )

    own_part = depth // tensor_count
    own_state = lax.dynamic_slice_in_dim(own_state, tensor_place * own_part, own_part, 0)[:, :state_width]

    def own_cut(z, size, axis):
        return lax.dynamic_slice_in_dim(z, dp_place * size, size, axis)

    by_channel = small_sum[: taps + 3, :channels].reshape(taps + 3, heads_here, HEADDIM)
    by_channel = own_cut(by_channel, cut, 2)
    by_map = own_cut(small_shared[: taps + 1, channels : channels + 2 * STATE], state_cut, 1)
    heads_at = channels + 2 * STATE
    by_head = own_cut(small_shared[:3, heads_at : heads_at + LANES], head_cut, 1)
    gain_grad = lax.dynamic_slice_in_dim(
        small_shared[8], (dp_place * tensor_count + tensor_place) * own_part, own_part, 0
    )
    own_first = own_first.astype(f32)
    return (
        block_out,
        grad_hidden,
        gain_grad,
        own_first[:, :channels],
        own_last[:, :channels].astype(f32),
        own_state,
        own_first[:, channels:].T,
        by_channel[:taps],
        by_channel[taps],
        by_map[:taps],
        by_map[taps],
        by_head[0],
        by_head[1],
        by_head[2],
        by_channel[taps + 2],
    )


def solution(mesh):
    placed = (
        P(("dp", "tensor"), None),
        P("dp"),
        P("dp", "tensor"),
        P("dp", "tensor"),
        P("dp", None),
        P(None, "tensor", "dp"),
        P("tensor", "dp"),
        P(None, "dp"),
        P("dp"),
        P("dp"),
        P("dp"),
        P("dp"),
        P("tensor", "dp"),
        P("tensor", "dp"),
        P(("dp", "tensor"), None),
        P("dp", None),
    )
    return jax.shard_map(
        per_device,
        mesh=mesh,
        in_specs=placed,
        out_specs=(
            P(("dp", "tensor"), None),
            P(("dp", "tensor"), None),
            P(("dp", "tensor")),
            P("dp", "tensor"),
            P("dp", "tensor"),
            P(("dp", "tensor"), None),
            P("tensor", "dp"),
            P(None, "tensor", "dp"),
            P("tensor", "dp"),
            P(None, "dp"),
            P("dp"),
            P("dp"),
            P("dp"),
            P("dp"),
            P("tensor", "dp"),
        ),
        check_vma=False,
    )
```

```python
import functools

import jax
import jax.numpy as jnp
import numpy as np
from jax import lax
from jax.experimental import pallas as pl
from jax.experimental.pallas import tpu as pltpu
from jax.sharding import PartitionSpec as P

HEADDIM = 64
STATE = 128
INNER = 2048
LANES = 128
ROWS = 256
WIDE_ROWS = 512
FIELD = 32
PARAMS = 16
SUB = 128
EPS = 1e-05
LOG2E = 1.4426950408889634

f32 = jnp.float32
bf16 = jnp.bfloat16


def nn(a, b):
    return lax.dot_general(a, b, (((1,), (0,)), ((), ())), preferred_element_type=f32)


def nt(a, b):
    return lax.dot_general(a, b, (((1,), (1,)), ((), ())), preferred_element_type=f32)


def tn(a, b):
    return lax.dot_general(a, b, (((0,), (0,)), ((), ())), preferred_element_type=f32)


def pieces(z, count):
    parts = []
    for _ in range(count - 1):
        part = z.astype(bf16)
        parts.append(part)
        z = z - part.astype(f32)
    parts.append(z.astype(bf16))
    return parts


def spread_heads(z, heads):
    return nn(jnp.concatenate(pieces(z, 2), axis=1), heads)


def gather_heads(z, heads):
    return nn(jnp.concatenate(pieces(z, 2), axis=1), heads)


def triangle_sum(triangle, z):
    return nn(triangle, jnp.concatenate(pieces(z, 3), axis=0))


def constants(channels):
    row, col = np.arange(ROWS)[:, None], np.arange(ROWS)[None, :]
    same = row // SUB == col // SUB
    lower = np.concatenate([same & (row >= col)] * 3, axis=1)
    upper = np.concatenate([same & (row <= col)] * 3, axis=1)
    heads = np.arange(LANES)[:, None] == np.arange(channels)[None, :] // HEADDIM
    spread = np.concatenate([heads] * 2, axis=0)
    gather = np.concatenate([heads.T] * 2, axis=0)
    return [jnp.asarray(z, bf16) for z in (lower, upper, spread, gather)]


def ends_of(len_ref, count):
    ends, total = [], 0
    for s in range(count):
        total = total + len_ref[0, s]
        ends.append(total)
    return ends


def segment_of(places, ends):
    return sum((places >= end).astype(jnp.int32) for end in ends)


def start_of(places, ends):
    start = jnp.zeros_like(places)
    for end in ends:
        start = jnp.where(places >= end, end, start)
    return start


def scan_steps(raw, decay, lower):
    step = jnp.maximum(raw, 0.0) + jnp.log1p(jnp.exp(-jnp.abs(raw)))
    return step, triangle_sum(lower, -decay * step)


def scan_weights(step, cum, base, ends, spread):
    rows = step.shape[0]
    segment = segment_of(base + lax.broadcasted_iota(jnp.int32, (rows, 1), 0), ends)
    carried, keep, survive = [], [], []
    for low in range(0, rows, SUB):
        before = segment_of(base + low - 1, ends)
        tail = segment_of(base + low + SUB - 1, ends)
        part, own = cum[low : low + SUB], segment[low : low + SUB]
        last = part[SUB - 1 :]
        carried.append(jnp.where(own == before, jnp.exp(part), 0.0))
        keep.append(jnp.where(own == tail, jnp.exp(last - part), 0.0))
        survive.append(jnp.where(tail == before, jnp.exp(last), 0.0))
    survive.append(jnp.zeros((-len(survive) % 8, LANES), f32))
    wide = spread_heads(jnp.concatenate([step] + carried + keep + survive, axis=0), spread)
    return wide[:rows], wide[rows : 2 * rows], wide[2 * rows : 3 * rows], wide[3 * rows :]


def pair_stack(z):
    lane = lax.broadcasted_iota(jnp.int32, z.shape, 1)
    zero = jnp.zeros_like(z)
    return jnp.concatenate(
        [jnp.where(lane < HEADDIM, z, zero), jnp.where(lane >= HEADDIM, z, zero)], axis=0
    )


def silu(u):
    return u * jax.nn.sigmoid(u)


def own_lanes(z, shift, count):
    moved = pltpu.roll(z, (z.shape[1] - shift) % z.shape[1], 1)
    lane = lax.broadcasted_iota(jnp.int32, z.shape, 1)
    return jnp.where(lane < count, moved, 0.0)


def nn3(a, b):
    a, a_low = pieces(a, 2)
    b, b_low = pieces(b, 2)
    return nn(jnp.concatenate([a, a_low, a], axis=1), jnp.concatenate([b, b, b_low], axis=0))


def nt3(a, b):
    a, a_low = pieces(a, 2)
    b, b_low = pieces(b, 2)
    return nt(jnp.concatenate([a, a_low, a], axis=1), jnp.concatenate([b, b, b_low], axis=1))


def pair_product(mixing, z):
    high, low = pieces(z, 2)
    both = nn(
        jnp.concatenate(mixing, axis=1),
        jnp.concatenate([pair_stack(high), pair_stack(low)], axis=1),
    )
    return both[:, :LANES] + both[:, LANES:]


def take_rows(refs, which, buffer):
    if len(refs) == 1:
        return refs[0][...]
    half = buffer.shape[1] // 2
    slots, at = [], 0
    while at < len(refs):
        count = 1 if refs[at].shape[1] == 2 * half else 2
        slots.append(refs[at : at + count])
        at += count
    for k, slot in enumerate(slots):

        @pl.when(which == k)
        def _(slot=slot):
            if len(slot) == 1:
                buffer[...] = slot[0][...]
            else:
                buffer[:, :half] = slot[0][...]
                buffer[:, half:] = slot[1][...]

    return buffer[...]


def put_halves(refs, which, product):
    half = product.shape[1] // 2
    left, right = product[:, :half], product[:, half:]
    if len(refs) == 2:
        refs[0][...] = left
        refs[1][...] = right
        return
    left_sent, left_kept, right_sent, right_kept = refs

    @pl.when(which % 2 == 1)
    def _():
        left_sent[...] = left

    @pl.when(which % 2 == 0)
    def _():
        left_kept[...] = left

    @pl.when(which >= 2)
    def _():
        right_sent[...] = right

    @pl.when(which < 2)
    def _():
        right_kept[...] = right


def scan_kernel(
    len_ref, first_ref, place_ref, *refs, parts, seqs, taps, head_count, first_block, kept, starts, place_at
):
    part_refs, refs = refs[:parts], refs[parts:]
    w_ref, gain_ref, prm_ref, prs_ref, prh_ref, lower_ref, spread_ref = refs[:7]
    start_refs, refs = refs[7 : 7 + starts], refs[7 + starts :]
    (
        normed_ref,
        v_ref,
        u_ref,
        vs_ref,
        us_ref,
        terms_ref,
        y_ref,
        st_ref,
        gate_ref,
        ga_ref,
        total_ref,
        square_ref,
        vtail_out,
        stail_out,
        carry,
        hid_buf,
        vbuf,
        sbuf,
    ) = refs[kept:]
    rows, channels = v_ref.shape
    step_id = pl.program_id(0)
    block = step_id + first_block
    base = block * rows
    ends = ends_of(len_ref, seqs)

    @pl.when(step_id == 0)
    def _():
        if start_refs:
            vbuf[0:8, :] = start_refs[0][...]
            sbuf[0:8, :] = start_refs[1][...]
            carry[...] = start_refs[2][...]
        else:
            vbuf[0:8, :] = jnp.zeros((8, channels), f32)
            sbuf[0:8, :] = jnp.zeros((8, 2 * STATE), f32)
            carry[...] = jnp.zeros_like(carry)

    values = take_rows(part_refs, place_ref[place_at + block], hid_buf).astype(f32)
    inverse = lax.rsqrt(jnp.mean(values * values, axis=1, keepdims=True) + EPS)
    normed = (values * inverse * gain_ref[...]).astype(bf16)
    normed_ref[...] = normed
    gate_pre = nn(normed, w_ref[:, :channels])
    gate_ref[...] = gate_pre.astype(bf16)
    conv_pre = nn(normed, w_ref[:, channels : 2 * channels])
    state_all = nn(normed, w_ref[:, 2 * channels :])
    v_ref[...] = conv_pre.astype(bf16)
    vs_ref[...] = state_all[:, : 2 * STATE].astype(bf16)
    vbuf[8 : 8 + rows, :] = conv_pre
    sbuf[8 : 8 + rows, :] = state_all[:, : 2 * STATE]
    start = start_of(base + lax.broadcasted_iota(jnp.int32, (rows, 1), 0), ends)
    u = prm_ref[taps : taps + 1, :] + prm_ref[taps - 1 : taps, :] * conv_pre
    us = prs_ref[taps : taps + 1, :] + prs_ref[taps - 1 : taps, :] * state_all[:, : 2 * STATE]
    for lag in range(1, taps):
        usable = base + lax.broadcasted_iota(jnp.int32, (rows, 1), 0) - lag >= start
        tap = taps - 1 - lag
        u = u + prm_ref[tap : tap + 1, :] * jnp.where(usable, vbuf[8 - lag : 8 - lag + rows, :], 0.0)
        us = us + prs_ref[tap : tap + 1, :] * jnp.where(usable, sbuf[8 - lag : 8 - lag + rows, :], 0.0)
    vbuf[0:8, :] = vbuf[rows : rows + 8, :]
    sbuf[0:8, :] = sbuf[rows : rows + 8, :]
    vtail_out[...] = vbuf[0:8, :]
    stail_out[...] = sbuf[0:8, :]
    u_ref[...] = u
    us_ref[...] = us
    raw = own_lanes(state_all[:, 2 * STATE :], first_ref[0], head_count) + prh_ref[0:1, :]

    x = silu(u)
    maps = silu(us)
    step, cum = scan_steps(raw, prh_ref[1:2, :], lower_ref[...])
    lane = lax.broadcasted_iota(jnp.int32, (rows, LANES), 1)
    terms_ref[...] = jnp.where(
        lane < FIELD,
        step,
        jnp.where(lane < 2 * FIELD, pltpu.roll(raw, FIELD, 1), pltpu.roll(cum, 2 * FIELD, 1)),
    )
    step_w, carried_w, keep_w, survive_w = scan_weights(step, cum, base, ends, spread_ref[...])
    cum = cum * LOG2E
    cum_row = cum.T
    stepped = step_w * x
    kept_b = keep_w * stepped
    row = lax.broadcasted_iota(jnp.int32, (SUB, SUB), 0)
    col = lax.broadcasted_iota(jnp.int32, (SUB, SUB), 1)
    state = carry[...]
    y_parts = []
    for q in range(rows // SUB):
        at = slice(q * SUB, (q + 1) * SUB)
        low = base + q * SUB
        mask = (row >= col) & (segment_of(low + row, ends) == segment_of(low + col, ends))
        b_map, c_map = maps[at, :STATE], maps[at, STATE:]
        gram = jnp.where(mask, nt3(c_map, b_map), 0.0)
        st_ref[q] = state
        outer = carried_w[at] * nn3(c_map, state)
        inner = []
        for pair in range(channels // LANES):
            mixing = []
            for h in (2 * pair, 2 * pair + 1):
                spread = cum[at, h : h + 1] - cum_row[h : h + 1, at]
                mixing.append((jnp.exp2(jnp.minimum(spread, 0.0)) * gram).astype(bf16))
            inner.append(pair_product(mixing, stepped[at, pair * LANES : (pair + 1) * LANES]))
        y_parts.append(jnp.concatenate(inner, axis=1) + outer)
        state = survive_w[q : q + 1] * state + nn3(b_map.T, kept_b[at])
    carry[...] = state
    y_scan = jnp.concatenate(y_parts, axis=0)
    y_ref[...] = y_scan
    y_total = y_scan + prm_ref[taps + 1 : taps + 2, :] * x
    total_ref[...] = y_total.astype(bf16)
    g = y_total * silu(gate_pre)
    ga_ref[...] = (g * prm_ref[taps + 2 : taps + 3, :]).astype(bf16)
    square = jnp.sum(g * g, axis=1, keepdims=True)
    square_ref[...] = jnp.broadcast_to(square, (rows, LANES)).T[:8, :]


def parameter_kernel(
    first_ref, packed_ref, prm_ref, prs_ref, prh_ref, gain_ref, *, taps, heads_here, cut, state_cut, head_cut, depth
):
    packed = packed_ref[...]
    total = packed.shape[1]
    rows = prm_ref.shape[0]
    source = lax.broadcasted_iota(jnp.int32, (total, 1), 0)
    maps_at = heads_here * cut

    def split(z, size):
        return z >> (size.bit_length() - 1), z & (size - 1)

    def moved(columns, lane_of):
        lane = lane_of(lax.broadcasted_iota(jnp.int32, (1, columns), 1))
        return nn(packed, jnp.where(source == lane, 1.0, 0.0).astype(bf16))[:rows]

    def by_channel(c):
        head, inside = split(c, HEADDIM)
        owner, place = split(inside, cut)
        return owner * LANES + head * cut + place

    def by_part(size, at):
        def lane_of(c):
            owner, place = split(c, size)
            return owner * LANES + at + place

        return lane_of

    def own_head(at):
        part = by_part(head_cut, at)
        return lambda h: jnp.where(h < heads_here, part(first_ref[0] + h), -1)

    channels = prm_ref.shape[1]
    row = lax.broadcasted_iota(jnp.int32, (rows, 1), 0)
    by_head = moved(channels, by_channel)
    skip = by_part(head_cut, maps_at + 2 * head_cut)
    skips = moved(channels, lambda c: skip(first_ref[0] + split(c, HEADDIM)[0]))
    prm_ref[...] = jnp.where(
        row <= taps,
        by_head,
        jnp.where(row == taps + 1, skips, jnp.where(row == taps + 2, pltpu.roll(by_head, 1, 0), 0.0)),
    )
    prs_ref[...] = jnp.where(row <= taps, moved(2 * STATE, by_part(state_cut, maps_at)), 0.0)
    bias = moved(LANES, own_head(maps_at))[taps + 1 : taps + 2]
    rate = jnp.exp(moved(LANES, own_head(maps_at + head_cut))[taps + 1 : taps + 2])
    lane = lax.broadcasted_iota(jnp.int32, (1, LANES), 1)
    rate = jnp.where(lane < heads_here, rate, 0.0)
    prh_ref[...] = jnp.where(row == 0, bias, jnp.where(row == 1, rate, 0.0))
    gain_ref[...] = moved(gain_ref.shape[1], by_part(depth, 0))[taps + 2 : taps + 3]


def product_kernel(place_ref, ga_ref, w_ref, *refs, place_at):
    product = nt(ga_ref[...], w_ref[...]).astype(bf16)
    put_halves(refs, place_ref[place_at + pl.program_id(0)], product)


def cotangent_kernel(place_ref, *refs, parts, place_at):
    part_refs, refs = refs[:parts], refs[parts:]
    w_ref, ga_ref, square_ref, gg_ref, sums_ref, cot_buf = refs
    rows = gg_ref.shape[0]
    cotangent = take_rows(part_refs, place_ref[place_at + pl.program_id(0)], cot_buf)
    grad_gated = nn(cotangent, w_ref[...])
    gg_ref[...] = grad_gated.astype(bf16)
    inner = jnp.sum(grad_gated * ga_ref[...].astype(f32), axis=1, keepdims=True)
    inner_row = jnp.broadcast_to(inner, (rows, LANES)).T[:8, :]
    sublane = lax.broadcasted_iota(jnp.int32, (8, rows), 0)
    sums_ref[...] = jnp.where(sublane == 0, square_ref[...], inner_row)


def gain_row(weights, grads):
    terms = jnp.sum(weights.astype(f32) * grads, axis=1, keepdims=True)
    return jnp.broadcast_to(terms, (terms.shape[0], LANES)).T[:8, :]


def gate_kernel(place_ref, *refs, parts, taps, place_at):
    part_refs, refs = refs[:parts], refs[parts:]
    (
        sums_ref,
        prm_ref,
        w_ref,
        gate_ref,
        y_ref,
        gg_ref,
        normed_ref,
        dgate_ref,
        dy_ref,
        dprm_ref,
        out_ref,
        gain_ref,
        cot_buf,
        total,
    ) = refs
    rows, channels = gate_ref.shape
    step_id = pl.program_id(0)

    @pl.when(step_id == 0)
    def _():
        dprm_ref[...] = jnp.zeros_like(dprm_ref)
        total[...] = jnp.zeros_like(total)

    sums = jnp.concatenate([sums_ref[...], jnp.zeros((LANES - 8, rows), f32)], axis=0).T
    inverse = lax.rsqrt(sums[:, 0:1] * (1.0 / INNER) + EPS)
    inner_mean = sums[:, 1:2] * inverse * (1.0 / INNER)
    normed = normed_ref[...]
    cotangent = take_rows(part_refs, place_ref[place_at + step_id], cot_buf)
    gain = prm_ref[taps + 2 : taps + 3, :]
    gate_pre = gate_ref[...].astype(f32)
    sig_gate = jax.nn.sigmoid(gate_pre)
    act = gate_pre * sig_gate
    y = y_ref[...].astype(f32)
    hat = y * act * inverse
    gated = (hat * gain).astype(bf16)
    total[:, channels:] += tn(cotangent, gated)
    grad_gated = gg_ref[...].astype(f32)
    dprm_ref[taps + 2 : taps + 3, :] += jnp.sum(grad_gated * hat, axis=0, keepdims=True)
    grad_inner = inverse * (grad_gated * gain - hat * inner_mean)
    dy_ref[...] = grad_inner * act
    dgate = (grad_inner * y * sig_gate * (1.0 + gate_pre * (1.0 - sig_gate))).astype(bf16)
    dgate_ref[...] = dgate
    total[:, :channels] += tn(normed, dgate)

    @pl.when(step_id == pl.num_programs(0) - 1)
    def _():
        out_ref[...] = total[...].astype(bf16)
        gain_ref[...] = gain_row(w_ref[...], total[:, :channels])


def backward_kernel(len_ref, first_ref, place_ref, *refs, seqs, taps, halves, place_at):
    (
        w_ref,
        gain_ref,
        terms_ref,
        dprm_gate_ref,
        prm_ref,
        prs_ref,
        prh_ref,
        upper_ref,
        spread_ref,
        gather_ref,
        normed_ref,
        dgate_ref,
        dy_ref,
        v_ref,
        u_ref,
        vs_ref,
        us_ref,
        scan_ref,
        y_ref,
        st_ref,
    ) = refs[:20]
    half_refs = refs[20 : 20 + halves]
    out_ref, small_ref, dprm_ref, dprs_ref, dprh_ref, dbuf, dsbuf, carry, ending, total = refs[20 + halves :]
    rows, channels = dgate_ref.shape
    step_id = pl.program_id(0)
    base = (pl.num_programs(0) - 1 - step_id) * rows
    ends = ends_of(len_ref, seqs)

    @pl.when(step_id == 0)
    def _():
        dbuf[rows : rows + 8, :] = jnp.zeros((8, channels), f32)
        dsbuf[rows : rows + 8, :] = jnp.zeros((8, 2 * STATE), f32)
        carry[...] = jnp.zeros_like(carry)
        ending[...] = jnp.zeros_like(ending)
        dprm_ref[...] = jnp.zeros_like(dprm_ref)
        dprs_ref[...] = jnp.zeros_like(dprs_ref)
        dprh_ref[...] = jnp.zeros_like(dprh_ref)
        total[...] = jnp.zeros_like(total)

    def add_row(ref, at, z):
        ref[at : at + 1, :] += jnp.sum(z, axis=0, keepdims=True)

    skip = prm_ref[taps + 1 : taps + 2, :]
    u = u_ref[...]
    sig_u = jax.nn.sigmoid(u)
    x = u * sig_u
    y_scan = y_ref[...]
    dy = dy_ref[...]
    dy_b = dy.astype(bf16)

    add_row(dprm_ref, taps + 1, dy * x)
    us = us_ref[...]
    sig_us = jax.nn.sigmoid(us)
    maps = us * sig_us
    maps_b = maps.astype(bf16)
    terms = scan_ref[...]
    lane = lax.broadcasted_iota(jnp.int32, (rows, LANES), 1)
    inside = lane < FIELD
    step = jnp.where(inside, terms, 0.0)
    raw = jnp.where(inside, pltpu.roll(terms, LANES - FIELD, 1), 0.0)
    cum = jnp.where(inside, pltpu.roll(terms, LANES - 2 * FIELD, 1), 0.0)
    decay = prh_ref[1:2, :]
    step_w, carried_w, keep_w, survive_w = scan_weights(step, cum, base, ends, spread_ref[...])
    cum = cum * LOG2E
    cum_row = cum.T
    stepped = step_w * x
    stepped_b = stepped.astype(bf16)
    kept_b = (keep_w * stepped).astype(bf16)
    dy_carried = carried_w * dy
    dy_carried_b = dy_carried.astype(bf16)
    row = lax.broadcasted_iota(jnp.int32, (SUB, SUB), 0)
    col = lax.broadcasted_iota(jnp.int32, (SUB, SUB), 1)
    dstate = carry[...]
    state_end = ending[0:1, :]
    subs = rows // SUB
    dsteppeds, dmaps, state_ends = [None] * subs, [None] * subs, [None] * subs
    for q in reversed(range(subs)):
        at = slice(q * SUB, (q + 1) * SUB)
        low = base + q * SUB
        mask = (row <= col) & (segment_of(low + row, ends) == segment_of(low + col, ends))
        b_map, c_map = maps[at, :STATE], maps[at, STATE:]
        gram = jnp.where(mask, nt3(b_map, c_map), 0.0)
        state = st_ref[q]
        dstate_b = dstate.astype(bf16)
        dgram = jnp.zeros((SUB, SUB), f32)
        inner = []
        for pair in range(channels // LANES):
            lanes = slice(pair * LANES, (pair + 1) * LANES)
            dmix = nt(pair_stack(stepped_b[at, lanes]), dy_b[at, lanes])
            mixing = []
            for i, h in enumerate((2 * pair, 2 * pair + 1)):
                spread = cum_row[h : h + 1, at] - cum[at, h : h + 1]
                weight = jnp.exp2(jnp.minimum(spread, 0.0))
                mixing.append((weight * gram).astype(bf16))
                dgram = dgram + dmix[i * SUB : (i + 1) * SUB] * weight
            inner.append(pair_product(mixing, dy[at, lanes]))
        dsteppeds[q] = jnp.concatenate(inner, axis=1) + keep_w[at] * nn3(b_map, dstate)
        dgram = jnp.where(mask, dgram, 0.0).astype(bf16)
        db = nn(dgram, maps_b[at, STATE:]) + nt(kept_b[at], dstate_b)
        dc = tn(dgram, maps_b[at, :STATE]) + nt(dy_carried_b[at], state.astype(bf16))
        dmaps[q] = jnp.concatenate([db, dc], axis=1)
        state_ends[q] = state_end
        dstate = survive_w[q : q + 1] * dstate + nn3(c_map.T, dy_carried[at])
        state_end = jnp.sum(state * dstate, axis=0, keepdims=True)
    carry[...] = dstate
    ending[0:1, :] = state_end
    dstepped = jnp.concatenate(dsteppeds, axis=0)
    dmap = jnp.concatenate(dmaps, axis=0)
    state_ends.append(jnp.zeros((-subs % 8, channels), f32))
    by_head = gather_heads(
        jnp.concatenate([dy * y_scan - stepped * dstepped, x * dstepped] + state_ends, axis=0),
        gather_ref[...],
    )
    dlog = triangle_sum(upper_ref[...], by_head[:rows])
    dlog = jnp.concatenate(
        [
            dlog[q * SUB : (q + 1) * SUB] + by_head[2 * rows + q : 2 * rows + q + 1]
            for q in range(subs)
        ],
        axis=0,
    )
    draw = (by_head[rows : 2 * rows] - decay * dlog) * jax.nn.sigmoid(raw)
    add_row(dprh_ref, 0, draw)
    add_row(dprh_ref, 1, dlog * step * -decay)
    places = base + lax.broadcasted_iota(jnp.int32, (rows, 1), 0)
    segment = segment_of(places, ends)
    usable = [None] + [segment_of(places + lag, ends) == segment for lag in range(1, taps)]
    normed = normed_ref[...]

    def conv_back(du, v, weight_ref, buffer, sums_ref):
        buffer[0:rows, :] = du
        dv = weight_ref[taps - 1 : taps, :] * du
        lines = [jnp.sum(du * v, axis=0, keepdims=True), jnp.sum(du, axis=0, keepdims=True)]
        for lag in range(1, taps):
            later = jnp.where(usable[lag], buffer[lag : lag + rows, :], 0.0)
            dv = dv + weight_ref[taps - 1 - lag : taps - lag, :] * later
            lines.insert(0, jnp.sum(later * v, axis=0, keepdims=True))
        buffer[rows : rows + 8, :] = buffer[0:8, :]
        sums_ref[0 : taps + 1, :] += jnp.concatenate(lines, axis=0)
        return dv.astype(bf16)

    product = nt(dgate_ref[...], w_ref[:, :channels])
    du = (step_w * dstepped + skip * dy) * sig_u * (1.0 + u * (1.0 - sig_u))
    dv = conv_back(du, v_ref[...].astype(f32), prm_ref, dbuf, dprm_ref)
    product = product + nt(dv, w_ref[:, channels : 2 * channels])
    total[:, :channels] += tn(normed, dv)
    dus = dmap * sig_us * (1.0 + us * (1.0 - sig_us))
    dvs = conv_back(dus, vs_ref[...].astype(f32), prs_ref, dsbuf, dprs_ref)
    state_part = jnp.concatenate([dvs, pltpu.roll(draw, first_ref[0], 1).astype(bf16)], axis=1)
    product = product + nt(state_part, w_ref[:, 2 * channels :])
    total[:, channels:] += tn(normed, state_part)
    put_halves(half_refs, place_ref[place_at + step_id], product.astype(bf16))

    @pl.when(step_id == pl.num_programs(0) - 1)
    def _():
        grads = total[...]
        out_ref[...] = grads.astype(bf16)
        gains = (gain_row(w_ref[:, channels:], grads) + terms_ref[...]) / gain_ref[...]
        line = lax.broadcasted_iota(jnp.int32, (8, 1), 0)
        both = jnp.where(line == taps + 2, dprm_gate_ref[...], dprm_ref[...])
        skips = gather_heads(dprm_ref[...], gather_ref[...])
        by_head = jnp.where(line == 2, pltpu.roll(skips, 8 - (taps - 1), 0), dprh_ref[...])
        small_ref[...] = jnp.zeros_like(small_ref)
        small_ref[0:8, :channels] = both
        small_ref[0:8, channels : channels + 2 * STATE] = dprs_ref[...]
        small_ref[0:8, channels + 2 * STATE : channels + 2 * STATE + LANES] = pltpu.roll(
            by_head, first_ref[0], 1
        )
        small_ref[8:16, :] = gains


def held(places):
    last = next(p for p in places if p is not None)
    filled = []
    for p in places:
        last = last if p is None else p
        filled.append(last)
    return filled


def place_table(tensor_place, quarter_blocks, order):
    relative = [(b // quarter_blocks) ^ tensor_place for b in order]
    inside = [b % quarter_blocks for b in order]

    def places(slots):
        return held(
            [slots.index(r) * quarter_blocks + w if r in slots else None for r, w in zip(relative, inside)]
        )

    return [
        relative,
        places([0]),
        places([1]),
        places([2]),
        places([3]),
        places([1, 3]),
        places([0, 2]),
        places([2, 3]),
        places([0, 1]),
    ]


def over_x(z):
    return lax.ppermute(z, "tensor", [(0, 1), (1, 0), (2, 3), (3, 2)])


def over_y(z):
    return lax.ppermute(z, "tensor", [(0, 2), (2, 0), (1, 3), (3, 1)])


def gather_start(z):
    return over_x(z), over_y(z)


def gather_end(z, from_x, from_y, after=()):
    half = z.shape[1] // 2
    far = (from_x[:, :half], from_y[:, half:])
    far, after = lax.optimization_barrier((far, after))
    return [z, from_x, from_y, over_y(far[0]), over_x(far[1])], after


def scatter_start(halves):
    return over_x(halves[0]), over_y(halves[2])


def scatter_middle(halves, from_x, from_y, after=()):
    rows = from_x.shape[0] // 2
    left, right = halves[1], halves[3]
    left_far = left[rows:].astype(f32) + from_x[rows:].astype(f32)
    right_far = right[rows:].astype(f32) + from_y[rows:].astype(f32)
    far = (left_far.astype(bf16), right_far.astype(bf16))
    far, after = lax.optimization_barrier((far, after))
    return (over_y(far[0]), over_x(far[1])), after


def scatter_end(halves, from_x, from_y, far_left, far_right):
    rows = from_x.shape[0] // 2
    left, right = halves[1][:rows].astype(f32), halves[3][:rows].astype(f32)
    left = left + from_x[:rows].astype(f32) + far_left.astype(f32)
    right = right + from_y[:rows].astype(f32) + far_right.astype(f32)
    return left, right


def sum_over_tensor(z):
    z = (z.astype(f32) + over_x(z).astype(f32)).astype(z.dtype)
    return z.astype(f32) + over_y(z).astype(f32)


def sum_over_dp(z):
    count = lax.axis_size("dp")
    bit = 1
    while bit < count:
        z = z + lax.ppermute(z, "dp", [(i, i ^ bit) for i in range(count)])
        bit *= 2
    return z


class Kernels:
    def __init__(self, lengths, first, tensor_place, tensor_count, group_rows, width, channels, taps, head_count):
        self.lengths, self.first = lengths, first
        self.tensor_place, self.tensor_count = tensor_place, tensor_count
        self.square = tensor_count == 4
        self.group_rows, self.width, self.channels = group_rows, width, channels
        self.taps, self.head_count = taps, head_count
        self.seqs = lengths.shape[1]
        self.lower, self.upper, self.spread, self.gather = constants(channels)
        self.tables()

    def tables(self):
        kinds = ((ROWS, False), (ROWS, True), (WIDE_ROWS, False))
        self.kinds = {kind: k for k, kind in enumerate(kinds)}
        places = range(4) if self.square else range(1)
        made = []
        for t in places:
            lines = []
            for block, backwards in kinds:
                order = list(range(self.group_rows // block))[:: -1 if backwards else 1]
                table = place_table(t, len(order) // 4, order) if self.square else [order]
                lines += [line + [0] * (self.group_rows // ROWS - len(order)) for line in table]
            made.append(lines)
        self.lines = len(made[0]) // len(kinds)
        made = jnp.asarray(np.array(made, np.int32).reshape(len(made), -1))
        place = self.tensor_place if self.square else 0
        self.place = lax.dynamic_index_in_dim(made, place, 0, keepdims=False)
        self.steps = self.group_rows // ROWS

    def at(self, block, backwards, line):
        return (self.kinds[(block, backwards)] * self.lines + line) * self.steps

    def call(self, kernel, scalars, steps, ins, outs, scratch, aliases=None, flops=1000):
        specs, arrays = zip(*ins)
        out_specs, out_shapes = zip(*outs)
        return pl.pallas_call(
            kernel,
            grid_spec=pltpu.PrefetchScalarGridSpec(
                num_scalar_prefetch=len(scalars),
                grid=(steps,),
                in_specs=list(specs),
                out_specs=list(out_specs),
                scratch_shapes=scratch,
            ),
            out_shape=list(out_shapes),
            input_output_aliases=aliases or {},
            compiler_params=pltpu.CompilerParams(vmem_limit_bytes=56 * 2**20),
            cost_estimate=pl.CostEstimate(flops=flops, bytes_accessed=1000, transcendentals=0),
            name=getattr(kernel, "func", kernel).__name__,
        )(*scalars, *arrays)

    def whole(self, array):
        return pl.BlockSpec(array.shape, lambda i, *s: (0,) * len(array.shape)), array

    def columns(self, array, width, place):
        return pl.BlockSpec((array.shape[0], width), lambda i, *s: (0, place)), array

    def rows(self, array, block, backwards=False, low=0):
        last = self.group_rows // block - 1

        def at(i, *s):
            return (last - i if backwards else i + low,) + (0,) * (len(array.shape) - 1)

        size = array.shape[0] * block // self.group_rows
        return pl.BlockSpec((size,) + array.shape[1:], at), array

    def across(self, array, block, low=0):
        return pl.BlockSpec((8, block), lambda i, *s: (0, i + low)), array

    def out(self, columns, dtype):
        return jax.ShapeDtypeStruct((self.group_rows, columns), dtype)

    def parts(self, arrays, block, low=0):
        if not self.square:
            return [self.rows(arrays[0], block, low=low)]
        return [
            (
                pl.BlockSpec(
                    (block, z.shape[1]), lambda i, *s, at=self.at(block, False, k): (s[-1][at + i + low], 0)
                ),
                z,
            )
            for k, z in zip((1, 2, 3, 4, 4) if len(arrays) == 5 else (1, 2, 2, 3, 3, 4, 4), arrays)
        ]

    def halves(self, block, backwards=False):
        half = self.width // 2
        lines = (5, 6, 7, 8) if self.square else (0, 0)
        rows = self.group_rows // 2 if self.square else self.group_rows
        shape = jax.ShapeDtypeStruct((rows, half), bf16)
        return [
            (
                pl.BlockSpec((block, half), lambda i, *s, at=self.at(block, backwards, k): (s[-1][at + i], 0)),
                shape,
            )
            for k in lines
        ]

    def parameters(self, packed, cut, state_cut, head_cut, depth):
        shapes = ((8, self.channels), (8, 2 * STATE), (8, LANES), (1, self.width))
        return self.call(
            functools.partial(
                parameter_kernel,
                taps=self.taps,
                heads_here=self.head_count,
                cut=cut,
                state_cut=state_cut,
                head_cut=head_cut,
                depth=depth,
            ),
            (self.first,),
            1,
            [self.whole(packed)],
            [self.whole(jax.ShapeDtypeStruct(shape, f32)) for shape in shapes],
            [],
        )

    def scan(self, low, high, hidden, weights, gain, prm, prs, prh, carried, before=()):
        channels, count = self.channels, self.group_rows
        parts = self.parts(hidden, ROWS, low)
        shapes = [
            self.out(self.width, bf16),
            self.out(channels, bf16),
            self.out(channels, f32),
            self.out(2 * STATE, bf16),
            self.out(2 * STATE, f32),
            self.out(LANES, f32),
            self.out(channels, f32),
            jax.ShapeDtypeStruct((count // SUB, STATE, channels), f32),
            self.out(channels, bf16),
            self.out(channels, bf16),
            self.out(channels, bf16),
        ]
        outs = [self.rows(z, ROWS, low=low) for z in shapes]
        outs.append(self.across(jax.ShapeDtypeStruct((8, count), f32), ROWS, low))
        kept = len(outs)
        ins = parts + [self.whole(z) for z in [weights, gain, prm, prs, prh, self.lower, self.spread] + list(carried)]
        aliases = {3 + len(ins) + k: k for k in range(len(before))}
        ins += [(pl.BlockSpec(memory_space=pl.ANY), z) for z in before]
        sizes = ((8, channels), (8, 2 * STATE), (STATE, channels))
        outs += [self.whole(jax.ShapeDtypeStruct(size, f32)) for size in sizes]
        result = self.call(
            functools.partial(
                scan_kernel,
                parts=len(parts),
                seqs=self.seqs,
                taps=self.taps,
                head_count=self.head_count,
                first_block=low,
                kept=len(before),
                starts=len(carried),
                place_at=self.at(ROWS, False, 0),
            ),
            (self.lengths, self.first, self.place),
            high - low,
            ins,
            outs,
            [
                pltpu.VMEM((ROWS, self.width), bf16),
                pltpu.VMEM((ROWS + 8, channels), f32),
                pltpu.VMEM((ROWS + 8, 2 * STATE), f32),
            ],
            aliases,
        )
        return result[:kept], result[kept:]

    def product(self, ga, weights):
        return self.call(
            functools.partial(product_kernel, place_at=self.at(WIDE_ROWS, False, 0)),
            (self.place,),
            self.group_rows // WIDE_ROWS,
            [self.rows(ga, WIDE_ROWS), self.whole(weights)],
            self.halves(WIDE_ROWS),
            [],
        )

    def cotangent(self, cotangent, weights, ga, square):
        parts = self.parts(cotangent, WIDE_ROWS)
        return self.call(
            functools.partial(cotangent_kernel, parts=len(parts), place_at=self.at(WIDE_ROWS, False, 0)),
            (self.place,),
            self.group_rows // WIDE_ROWS,
            parts + [self.whole(weights), self.rows(ga, WIDE_ROWS), self.across(square, WIDE_ROWS)],
            [
                self.rows(self.out(self.channels, bf16), WIDE_ROWS),
                self.across(jax.ShapeDtypeStruct((8, self.group_rows), f32), WIDE_ROWS),
            ],
            [pltpu.VMEM((WIDE_ROWS, self.width), bf16)],
        )

    def gate(self, cotangent, sums, prm, weights, gate, y, gg, normed):
        channels = self.channels
        parts = self.parts(cotangent, WIDE_ROWS)
        return self.call(
            functools.partial(
                gate_kernel, parts=len(parts), taps=self.taps, place_at=self.at(WIDE_ROWS, False, 0)
            ),
            (self.place,),
            self.group_rows // WIDE_ROWS,
            parts
            + [self.across(sums, WIDE_ROWS), self.whole(prm), self.columns(weights, channels, 0)]
            + [self.rows(z, WIDE_ROWS) for z in (gate, y, gg, normed)],
            [
                self.rows(self.out(channels, bf16), WIDE_ROWS),
                self.rows(self.out(channels, f32), WIDE_ROWS),
                self.whole(jax.ShapeDtypeStruct(prm.shape, f32)),
                self.whole(jax.ShapeDtypeStruct((self.width, 2 * channels), bf16)),
                self.whole(jax.ShapeDtypeStruct((8, self.width), f32)),
            ],
            [pltpu.VMEM((WIDE_ROWS, self.width), bf16), pltpu.VMEM((self.width, 2 * channels), f32)],
            flops=8 * self.group_rows * self.width * channels * 4,
        )

    def backward(self, weights, gain, terms, dprm_gate, prm, prs, prh, saved):
        channels = self.channels
        gradients = channels + 3 * STATE
        halves = self.halves(ROWS, True)
        shapes = [
            jax.ShapeDtypeStruct((self.width, gradients), bf16),
            jax.ShapeDtypeStruct((16, self.width), f32),
        ]
        shapes += [jax.ShapeDtypeStruct(z.shape, f32) for z in (prm, prs, prh)]
        result = self.call(
            functools.partial(
                backward_kernel,
                seqs=self.seqs,
                taps=self.taps,
                halves=len(halves),
                place_at=self.at(ROWS, True, 0),
            ),
            (self.lengths, self.first, self.place),
            self.group_rows // ROWS,
            [
                self.whole(z)
                for z in (weights, gain, terms, dprm_gate, prm, prs, prh, self.upper, self.spread, self.gather)
            ]
            + [self.rows(z, ROWS, True) for z in saved],
            halves + [self.whole(z) for z in shapes],
            [
                pltpu.VMEM((ROWS + 8, channels), f32),
                pltpu.VMEM((ROWS + 8, 2 * STATE), f32),
                pltpu.VMEM((STATE, channels), f32),
                pltpu.VMEM((8, channels), f32),
                pltpu.VMEM((self.width, gradients), f32),
            ],
        )
        return result[: len(halves)], result[len(halves)], result[len(halves) + 1]


def per_device(
    hidden_in,
    norm_gain,
    proj_gate,
    proj_conv,
    proj_state,
    conv_kernel,
    conv_offset,
    state_kernel,
    state_offset,
    step_bias,
    decay_log,
    skip_gain,
    gate_gain,
    proj_out,
    out_cotangent,
    seq_lengths,
):
    tensor_count = lax.axis_size("tensor")
    tensor_place = lax.axis_index("tensor")
    dp_count = lax.axis_size("dp")
    dp_place = lax.axis_index("dp")
    square_mesh = tensor_count == 4
    own_rows, width = hidden_in.shape
    depth, channels = proj_gate.shape
    taps, heads_here, cut = conv_kernel.shape
    head_cut = step_bias.shape[0]
    state_cut = state_kernel.shape[1]
    state_width = proj_state.shape[1]
    group_rows = own_rows * tensor_count
    first_head = (tensor_place * heads_here).astype(jnp.int32)

    state_part = jnp.pad(proj_state, ((0, 0), (0, 3 * STATE - state_width)))
    weights = lax.all_gather(
        jnp.concatenate([proj_gate, proj_conv, state_part], axis=1), "dp", axis=0, tiled=True
    )
    out_weights = lax.all_gather(proj_out.T, "dp", axis=0, tiled=True)
    if square_mesh:
        half = width // 2
        left, right = hidden_in[:, :half], hidden_in[:, half:]
        x_left, y_right = over_x(left), over_y(right)
        x_right, y_left = over_x(right), over_y(left)

    def padded(z):
        return jnp.pad(z, ((0, 0), (0, LANES - z.shape[1])))

    packed = jnp.concatenate(
        [
            padded(jnp.concatenate([conv_kernel.reshape(taps, -1), state_kernel], axis=1)),
            padded(jnp.concatenate([conv_offset.reshape(1, -1), state_offset[None]], axis=1)),
            padded(
                jnp.concatenate(
                    [gate_gain.reshape(1, -1), step_bias[None], decay_log[None], skip_gain[None]], axis=1
                )
            ),
            padded(norm_gain[None]),
        ],
        axis=0,
    )
    packed = jnp.pad(packed, ((0, PARAMS - packed.shape[0]), (0, 0)))
    packed = lax.all_gather(packed, "dp", axis=1, tiled=True)
    if square_mesh:
        x_left, y_right, packed = lax.optimization_barrier((x_left, y_right, packed))
        far_left, far_right = over_y(x_left), over_x(y_right)
        hidden_all = [hidden_in, x_left, x_right, y_left, y_right, far_left, far_right]
    else:
        hidden_all = [lax.all_gather(hidden_in, "tensor", axis=0, tiled=True)]

    kernels = Kernels(
        seq_lengths,
        first_head.reshape(1),
        tensor_place,
        tensor_count,
        group_rows,
        width,
        channels,
        taps,
        heads_here,
    )

    prm, prs, prh, gain_in = kernels.parameters(packed, cut, state_cut, head_cut, depth)
    if square_mesh:
        hidden_all, prm, kernels.place, cot = lax.optimization_barrier(
            (hidden_all, prm, kernels.place, out_cotangent)
        )

    blocks = group_rows // ROWS
    common = (hidden_all, weights, gain_in, prm, prs, prh)
    if square_mesh:
        moving = gather_start(cot)
        middle = blocks * 3 // 4
        saved, carried = kernels.scan(0, middle, *common, ())
        carried, moving = lax.optimization_barrier((carried, moving))
        cotangent_all, carried = gather_end(cot, *moving, carried)
        saved, _ = kernels.scan(middle, blocks, *common, carried, saved)
    else:
        cotangent_all = [lax.all_gather(out_cotangent, "tensor", axis=0, tiled=True)]
        saved, _ = kernels.scan(0, blocks, *common, ())
    normed, v, u, vs, us, scan_terms, y_scan, states, gate_pre, ga, y_total, square = saved
    gg, sums = kernels.cotangent(cotangent_all, out_weights, ga, square)
    gg, ga = lax.optimization_barrier((gg, ga))
    out_halves = kernels.product(ga, out_weights)
    if square_mesh:
        sums = sums + over_x(sums)
        sums, out_halves = lax.optimization_barrier((sums, out_halves))
        sums = sums + over_y(sums)
        moving = scatter_start(out_halves)
    else:
        sums = lax.psum(sums, "tensor")

    dgate, dy, dprm_gate, grad_first, terms = kernels.gate(
        cotangent_all, sums, prm, weights, gate_pre, y_total, gg, normed
    )
    if square_mesh:
        dy, grad_first, moving = lax.optimization_barrier((dy, grad_first, moving))
        far, dy = scatter_middle(out_halves, *moving, dy)
        out_moving = moving + far
    own_first = lax.psum_scatter(grad_first, "dp", scatter_dimension=0, tiled=True)
    gn_halves, grad_last, small_sum = kernels.backward(
        weights,
        gain_in,
        terms,
        dprm_gate,
        prm,
        prs,
        prh,
        [normed, dgate, dy, v, u, vs, us, scan_terms, y_scan, states],
    )

    def own_sum(halves):
        return lax.psum_scatter(
            jnp.concatenate(halves, axis=1), "tensor", scatter_dimension=0, tiled=True
        ).astype(f32)

    if square_mesh:
        gn_halves, grad_last, small_sum, own_first, out_moving = lax.optimization_barrier(
            (gn_halves, grad_last, small_sum, own_first, out_moving)
        )
        moving = scatter_start(gn_halves)
    own_last = lax.psum_scatter(grad_last, "dp", scatter_dimension=0, tiled=True)
    small_sum = sum_over_dp(small_sum)
    if square_mesh:
        small_x = small_sum + over_x(small_sum)
        small_x, moving = lax.optimization_barrier((small_x, moving))
        small_shared = small_x + over_y(small_x)
        far, small_shared = scatter_middle(gn_halves, *moving, small_shared)
    else:
        small_shared = lax.psum(small_sum, "tensor")

    if square_mesh:
        far, own_last = lax.optimization_barrier((far, own_last))
        own_state = own_last[:, channels:].astype(f32)
        own_state = (own_state + over_x(own_last[:, channels:]).astype(f32)).astype(bf16)
        grad_normed = scatter_end(gn_halves, *moving, *far)
        grad_normed, own_state = lax.optimization_barrier((grad_normed, own_state))
        own_state = own_state.astype(f32) + over_y(own_state).astype(f32)
        grad_normed = jnp.concatenate(grad_normed, axis=1)
        branch = jnp.concatenate(scatter_end(out_halves, *out_moving), axis=1)
    else:
        grad_normed = own_sum(gn_halves)
        own_state = lax.psum(own_last[:, channels:].astype(f32), "tensor")
        branch = own_sum(out_halves)

    own_square = lax.dynamic_slice_in_dim(sums[0], tensor_place * own_rows, own_rows, 0)
    inverse_gate = lax.rsqrt(own_square * (1.0 / INNER) + EPS)[:, None]
    values = hidden_in.astype(f32)
    block_out = (values + branch * inverse_gate).astype(bf16)

    inverse_in = lax.rsqrt(jnp.mean(values * values, axis=1, keepdims=True) + EPS)
    scaled = values * inverse_in
    grad_scaled = grad_normed * gain_in
    grad_hidden = out_cotangent.astype(f32) + inverse_in * (
        grad_scaled - scaled * jnp.mean(grad_scaled * scaled, axis=1, keepdims=True)
    )

    own_part = depth // tensor_count
    own_state = lax.dynamic_slice_in_dim(own_state, tensor_place * own_part, own_part, 0)[:, :state_width]

    def own_cut(z, size, axis):
        return lax.dynamic_slice_in_dim(z, dp_place * size, size, axis)

    by_channel = small_sum[: taps + 3, :channels].reshape(taps + 3, heads_here, HEADDIM)
    by_channel = own_cut(by_channel, cut, 2)
    by_map = own_cut(small_shared[: taps + 1, channels : channels + 2 * STATE], state_cut, 1)
    heads_at = channels + 2 * STATE
    by_head = own_cut(small_shared[:3, heads_at : heads_at + LANES], head_cut, 1)
    gain_grad = lax.dynamic_slice_in_dim(
        small_shared[8], (dp_place * tensor_count + tensor_place) * own_part, own_part, 0
    )
    own_first = own_first.astype(f32)
    return (
        block_out,
        grad_hidden,
        gain_grad,
        own_first[:, :channels],
        own_last[:, :channels].astype(f32),
        own_state,
        own_first[:, channels:].T,
        by_channel[:taps],
        by_channel[taps],
        by_map[:taps],
        by_map[taps],
        by_head[0],
        by_head[1],
        by_head[2],
        by_channel[taps + 2],
    )


def solution(mesh):
    placed = (
        P(("dp", "tensor"), None),
        P("dp"),
        P("dp", "tensor"),
        P("dp", "tensor"),
        P("dp", None),
        P(None, "tensor", "dp"),
        P("tensor", "dp"),
        P(None, "dp"),
        P("dp"),
        P("dp"),
        P("dp"),
        P("dp"),
        P("tensor", "dp"),
        P("tensor", "dp"),
        P(("dp", "tensor"), None),
        P("dp", None),
    )
    return jax.shard_map(
        per_device,
        mesh=mesh,
        in_specs=placed,
        out_specs=(
            P(("dp", "tensor"), None),
            P(("dp", "tensor"), None),
            P(("dp", "tensor")),
            P("dp", "tensor"),
            P("dp", "tensor"),
            P(("dp", "tensor"), None),
            P("tensor", "dp"),
            P(None, "tensor", "dp"),
            P("tensor", "dp"),
            P(None, "dp"),
            P("dp"),
            P("dp"),
            P("dp"),
            P("dp"),
            P("tensor", "dp"),
        ),
        check_vma=False,
    )
```

```python
import functools

import jax
import jax.numpy as jnp
import numpy as np
from jax import lax
from jax.experimental import pallas as pl
from jax.experimental.pallas import tpu as pltpu
from jax.sharding import PartitionSpec as P

HEADDIM = 64
STATE = 128
INNER = 2048
LANES = 128
ROWS = 256
WIDE_ROWS = 512
FIELD = 32
PARAMS = 16
SUB = 128
EPS = 1e-05
LOG2E = 1.4426950408889634

f32 = jnp.float32
bf16 = jnp.bfloat16


def nn(a, b):
    return lax.dot_general(a, b, (((1,), (0,)), ((), ())), preferred_element_type=f32)


def nt(a, b):
    return lax.dot_general(a, b, (((1,), (1,)), ((), ())), preferred_element_type=f32)


def tn(a, b):
    return lax.dot_general(a, b, (((0,), (0,)), ((), ())), preferred_element_type=f32)


def pieces(z, count):
    parts = []
    for _ in range(count - 1):
        part = z.astype(bf16)
        parts.append(part)
        z = z - part.astype(f32)
    parts.append(z.astype(bf16))
    return parts


def spread_heads(z, heads):
    return nn(jnp.concatenate(pieces(z, 2), axis=1), heads)


def gather_heads(z, heads):
    return nn(jnp.concatenate(pieces(z, 2), axis=1), heads)


def triangle_sum(triangle, z):
    return nn(triangle, jnp.concatenate(pieces(z, 3), axis=0))


def constants(channels):
    row, col = np.arange(ROWS)[:, None], np.arange(ROWS)[None, :]
    same = row // SUB == col // SUB
    lower = np.concatenate([same & (row >= col)] * 3, axis=1)
    upper = np.concatenate([same & (row <= col)] * 3, axis=1)
    heads = np.arange(LANES)[:, None] == np.arange(channels)[None, :] // HEADDIM
    spread = np.concatenate([heads] * 2, axis=0)
    gather = np.concatenate([heads.T] * 2, axis=0)
    return [jnp.asarray(z, bf16) for z in (lower, upper, spread, gather)]


def ends_of(len_ref, count):
    ends, total = [], 0
    for s in range(count):
        total = total + len_ref[0, s]
        ends.append(total)
    return ends


def segment_of(places, ends):
    return sum((places >= end).astype(jnp.int32) for end in ends)


def start_of(places, ends):
    start = jnp.zeros_like(places)
    for end in ends:
        start = jnp.where(places >= end, end, start)
    return start


def scan_steps(raw, decay, lower):
    step = jnp.maximum(raw, 0.0) + jnp.log1p(jnp.exp(-jnp.abs(raw)))
    return step, triangle_sum(lower, -decay * step)


def scan_weights(step, cum, base, ends, spread):
    rows = step.shape[0]
    segment = segment_of(base + lax.broadcasted_iota(jnp.int32, (rows, 1), 0), ends)
    carried, keep, survive = [], [], []
    for low in range(0, rows, SUB):
        before = segment_of(base + low - 1, ends)
        tail = segment_of(base + low + SUB - 1, ends)
        part, own = cum[low : low + SUB], segment[low : low + SUB]
        last = part[SUB - 1 :]
        carried.append(jnp.where(own == before, jnp.exp(part), 0.0))
        keep.append(jnp.where(own == tail, jnp.exp(last - part), 0.0))
        survive.append(jnp.where(tail == before, jnp.exp(last), 0.0))
    survive.append(jnp.zeros((-len(survive) % 8, LANES), f32))
    wide = spread_heads(jnp.concatenate([step] + carried + keep + survive, axis=0), spread)
    return wide[:rows], wide[rows : 2 * rows], wide[2 * rows : 3 * rows], wide[3 * rows :]


def pair_stack(z):
    lane = lax.broadcasted_iota(jnp.int32, z.shape, 1)
    zero = jnp.zeros_like(z)
    return jnp.concatenate(
        [jnp.where(lane < HEADDIM, z, zero), jnp.where(lane >= HEADDIM, z, zero)], axis=0
    )


def silu(u):
    return u * jax.nn.sigmoid(u)


def own_lanes(z, shift, count):
    moved = pltpu.roll(z, (z.shape[1] - shift) % z.shape[1], 1)
    lane = lax.broadcasted_iota(jnp.int32, z.shape, 1)
    return jnp.where(lane < count, moved, 0.0)


def nn3(a, b):
    a, a_low = pieces(a, 2)
    b, b_low = pieces(b, 2)
    return nn(jnp.concatenate([a, a_low, a], axis=1), jnp.concatenate([b, b, b_low], axis=0))


def nt3(a, b):
    a, a_low = pieces(a, 2)
    b, b_low = pieces(b, 2)
    return nt(jnp.concatenate([a, a_low, a], axis=1), jnp.concatenate([b, b, b_low], axis=1))


def pair_product(mixing, z):
    high, low = pieces(z, 2)
    both = nn(
        jnp.concatenate(mixing, axis=1),
        jnp.concatenate([pair_stack(high), pair_stack(low)], axis=1),
    )
    return both[:, :LANES] + both[:, LANES:]


def take_rows(refs, which, buffer):
    if len(refs) == 1:
        return refs[0][...]
    half = buffer.shape[1] // 2
    slots, at = [], 0
    while at < len(refs):
        count = 1 if refs[at].shape[1] == 2 * half else 2
        slots.append(refs[at : at + count])
        at += count
    for k, slot in enumerate(slots):

        @pl.when(which == k)
        def _(slot=slot):
            if len(slot) == 1:
                buffer[...] = slot[0][...]
            else:
                buffer[:, :half] = slot[0][...]
                buffer[:, half:] = slot[1][...]

    return buffer[...]


def put_halves(refs, which, product):
    half = product.shape[1] // 2
    left, right = product[:, :half], product[:, half:]
    if len(refs) == 2:
        refs[0][...] = left
        refs[1][...] = right
        return
    left_sent, left_kept, right_sent, right_kept = refs

    @pl.when(which % 2 == 1)
    def _():
        left_sent[...] = left

    @pl.when(which % 2 == 0)
    def _():
        left_kept[...] = left

    @pl.when(which >= 2)
    def _():
        right_sent[...] = right

    @pl.when(which < 2)
    def _():
        right_kept[...] = right


def scan_kernel(
    len_ref, first_ref, place_ref, *refs, parts, seqs, taps, head_count, first_block, kept, starts, place_at
):
    part_refs, refs = refs[:parts], refs[parts:]
    w_ref, gain_ref, prm_ref, prs_ref, prh_ref, lower_ref, spread_ref = refs[:7]
    start_refs, refs = refs[7 : 7 + starts], refs[7 + starts :]
    (
        normed_ref,
        v_ref,
        u_ref,
        vs_ref,
        us_ref,
        terms_ref,
        y_ref,
        st_ref,
        gate_ref,
        ga_ref,
        total_ref,
        square_ref,
        vtail_out,
        stail_out,
        carry,
        hid_buf,
        vbuf,
        sbuf,
    ) = refs[kept:]
    rows, channels = v_ref.shape
    step_id = pl.program_id(0)
    block = step_id + first_block
    base = block * rows
    ends = ends_of(len_ref, seqs)

    @pl.when(step_id == 0)
    def _():
        if start_refs:
            vbuf[0:8, :] = start_refs[0][...]
            sbuf[0:8, :] = start_refs[1][...]
            carry[...] = start_refs[2][...]
        else:
            vbuf[0:8, :] = jnp.zeros((8, channels), f32)
            sbuf[0:8, :] = jnp.zeros((8, 2 * STATE), f32)
            carry[...] = jnp.zeros_like(carry)

    values = take_rows(part_refs, place_ref[place_at + block], hid_buf).astype(f32)
    inverse = lax.rsqrt(jnp.mean(values * values, axis=1, keepdims=True) + EPS)
    normed = (values * inverse * gain_ref[...]).astype(bf16)
    normed_ref[...] = normed
    gate_pre = nn(normed, w_ref[:, :channels])
    gate_ref[...] = gate_pre.astype(bf16)
    conv_pre = nn(normed, w_ref[:, channels : 2 * channels])
    state_all = nn(normed, w_ref[:, 2 * channels :])
    v_ref[...] = conv_pre.astype(bf16)
    vs_ref[...] = state_all[:, : 2 * STATE].astype(bf16)
    vbuf[8 : 8 + rows, :] = conv_pre
    sbuf[8 : 8 + rows, :] = state_all[:, : 2 * STATE]
    start = start_of(base + lax.broadcasted_iota(jnp.int32, (rows, 1), 0), ends)
    u = prm_ref[taps : taps + 1, :] + prm_ref[taps - 1 : taps, :] * conv_pre
    us = prs_ref[taps : taps + 1, :] + prs_ref[taps - 1 : taps, :] * state_all[:, : 2 * STATE]
    for lag in range(1, taps):
        usable = base + lax.broadcasted_iota(jnp.int32, (rows, 1), 0) - lag >= start
        tap = taps - 1 - lag
        u = u + prm_ref[tap : tap + 1, :] * jnp.where(usable, vbuf[8 - lag : 8 - lag + rows, :], 0.0)
        us = us + prs_ref[tap : tap + 1, :] * jnp.where(usable, sbuf[8 - lag : 8 - lag + rows, :], 0.0)
    vbuf[0:8, :] = vbuf[rows : rows + 8, :]
    sbuf[0:8, :] = sbuf[rows : rows + 8, :]
    vtail_out[...] = vbuf[0:8, :]
    stail_out[...] = sbuf[0:8, :]
    u_ref[...] = u
    us_ref[...] = us
    raw = own_lanes(state_all[:, 2 * STATE :], first_ref[0], head_count) + prh_ref[0:1, :]

    x = silu(u)
    maps = silu(us)
    step, cum = scan_steps(raw, prh_ref[1:2, :], lower_ref[...])
    lane = lax.broadcasted_iota(jnp.int32, (rows, LANES), 1)
    terms_ref[...] = jnp.where(
        lane < FIELD,
        step,
        jnp.where(lane < 2 * FIELD, pltpu.roll(raw, FIELD, 1), pltpu.roll(cum, 2 * FIELD, 1)),
    )
    step_w, carried_w, keep_w, survive_w = scan_weights(step, cum, base, ends, spread_ref[...])
    cum = cum * LOG2E
    cum_row = cum.T
    stepped = step_w * x
    kept_b = keep_w * stepped
    row = lax.broadcasted_iota(jnp.int32, (SUB, SUB), 0)
    col = lax.broadcasted_iota(jnp.int32, (SUB, SUB), 1)
    state = carry[...]
    y_parts = []
    for q in range(rows // SUB):
        at = slice(q * SUB, (q + 1) * SUB)
        low = base + q * SUB
        mask = (row >= col) & (segment_of(low + row, ends) == segment_of(low + col, ends))
        b_map, c_map = maps[at, :STATE], maps[at, STATE:]
        gram = jnp.where(mask, nt3(c_map, b_map), 0.0)
        st_ref[q] = state
        outer = carried_w[at] * nn3(c_map, state)
        inner = []
        for pair in range(channels // LANES):
            mixing = []
            for h in (2 * pair, 2 * pair + 1):
                spread = cum[at, h : h + 1] - cum_row[h : h + 1, at]
                mixing.append((jnp.exp2(jnp.minimum(spread, 0.0)) * gram).astype(bf16))
            inner.append(pair_product(mixing, stepped[at, pair * LANES : (pair + 1) * LANES]))
        y_parts.append(jnp.concatenate(inner, axis=1) + outer)
        state = survive_w[q : q + 1] * state + nn3(b_map.T, kept_b[at])
    carry[...] = state
    y_scan = jnp.concatenate(y_parts, axis=0)
    y_ref[...] = y_scan
    y_total = y_scan + prm_ref[taps + 1 : taps + 2, :] * x
    total_ref[...] = y_total.astype(bf16)
    g = y_total * silu(gate_pre)
    ga_ref[...] = (g * prm_ref[taps + 2 : taps + 3, :]).astype(bf16)
    square = jnp.sum(g * g, axis=1, keepdims=True)
    square_ref[...] = jnp.broadcast_to(square, (rows, LANES)).T[:8, :]


def parameter_kernel(
    first_ref, packed_ref, prm_ref, prs_ref, prh_ref, gain_ref, *, taps, heads_here, cut, state_cut, head_cut, depth
):
    packed = packed_ref[...]
    total = packed.shape[1]
    rows = prm_ref.shape[0]
    source = lax.broadcasted_iota(jnp.int32, (total, 1), 0)
    maps_at = heads_here * cut

    def split(z, size):
        return z >> (size.bit_length() - 1), z & (size - 1)

    def moved(columns, lane_of):
        lane = lane_of(lax.broadcasted_iota(jnp.int32, (1, columns), 1))
        return nn(packed, jnp.where(source == lane, 1.0, 0.0).astype(bf16))[:rows]

    def by_channel(c):
        head, inside = split(c, HEADDIM)
        owner, place = split(inside, cut)
        return owner * LANES + head * cut + place

    def by_part(size, at):
        def lane_of(c):
            owner, place = split(c, size)
            return owner * LANES + at + place

        return lane_of

    def own_head(at):
        part = by_part(head_cut, at)
        return lambda h: jnp.where(h < heads_here, part(first_ref[0] + h), -1)

    channels = prm_ref.shape[1]
    row = lax.broadcasted_iota(jnp.int32, (rows, 1), 0)
    by_head = moved(channels, by_channel)
    skip = by_part(head_cut, maps_at + 2 * head_cut)
    skips = moved(channels, lambda c: skip(first_ref[0] + split(c, HEADDIM)[0]))
    prm_ref[...] = jnp.where(
        row <= taps,
        by_head,
        jnp.where(row == taps + 1, skips, jnp.where(row == taps + 2, pltpu.roll(by_head, 1, 0), 0.0)),
    )
    prs_ref[...] = jnp.where(row <= taps, moved(2 * STATE, by_part(state_cut, maps_at)), 0.0)
    bias = moved(LANES, own_head(maps_at))[taps + 1 : taps + 2]
    rate = jnp.exp(moved(LANES, own_head(maps_at + head_cut))[taps + 1 : taps + 2])
    lane = lax.broadcasted_iota(jnp.int32, (1, LANES), 1)
    rate = jnp.where(lane < heads_here, rate, 0.0)
    prh_ref[...] = jnp.where(row == 0, bias, jnp.where(row == 1, rate, 0.0))
    gain_ref[...] = moved(gain_ref.shape[1], by_part(depth, 0))[taps + 2 : taps + 3]


def product_kernel(place_ref, ga_ref, w_ref, *refs, place_at):
    product = nt(ga_ref[...], w_ref[...]).astype(bf16)
    put_halves(refs, place_ref[place_at + pl.program_id(0)], product)


def cotangent_kernel(place_ref, *refs, parts, place_at):
    part_refs, refs = refs[:parts], refs[parts:]
    w_ref, ga_ref, square_ref, gg_ref, sums_ref, cot_buf = refs
    rows = gg_ref.shape[0]
    cotangent = take_rows(part_refs, place_ref[place_at + pl.program_id(0)], cot_buf)
    grad_gated = nn(cotangent, w_ref[...])
    gg_ref[...] = grad_gated.astype(bf16)
    inner = jnp.sum(grad_gated * ga_ref[...].astype(f32), axis=1, keepdims=True)
    inner_row = jnp.broadcast_to(inner, (rows, LANES)).T[:8, :]
    sublane = lax.broadcasted_iota(jnp.int32, (8, rows), 0)
    sums_ref[...] = jnp.where(sublane == 0, square_ref[...], inner_row)


def gain_row(weights, grads):
    terms = jnp.sum(weights.astype(f32) * grads, axis=1, keepdims=True)
    return jnp.broadcast_to(terms, (terms.shape[0], LANES)).T[:8, :]


def gate_kernel(place_ref, *refs, parts, taps, place_at):
    part_refs, refs = refs[:parts], refs[parts:]
    (
        sums_ref,
        prm_ref,
        w_ref,
        gate_ref,
        y_ref,
        gg_ref,
        normed_ref,
        dgate_ref,
        dy_ref,
        dprm_ref,
        out_ref,
        gain_ref,
        cot_buf,
        total,
    ) = refs
    rows, channels = gate_ref.shape
    step_id = pl.program_id(0)

    @pl.when(step_id == 0)
    def _():
        dprm_ref[...] = jnp.zeros_like(dprm_ref)
        total[...] = jnp.zeros_like(total)

    sums = jnp.concatenate([sums_ref[...], jnp.zeros((LANES - 8, rows), f32)], axis=0).T
    inverse = lax.rsqrt(sums[:, 0:1] * (1.0 / INNER) + EPS)
    inner_mean = sums[:, 1:2] * inverse * (1.0 / INNER)
    normed = normed_ref[...]
    cotangent = take_rows(part_refs, place_ref[place_at + step_id], cot_buf)
    gain = prm_ref[taps + 2 : taps + 3, :]
    gate_pre = gate_ref[...].astype(f32)
    sig_gate = jax.nn.sigmoid(gate_pre)
    act = gate_pre * sig_gate
    y = y_ref[...].astype(f32)
    hat = y * act * inverse
    gated = (hat * gain).astype(bf16)
    total[:, channels:] += tn(cotangent, gated)
    grad_gated = gg_ref[...].astype(f32)
    dprm_ref[taps + 2 : taps + 3, :] += jnp.sum(grad_gated * hat, axis=0, keepdims=True)
    grad_inner = inverse * (grad_gated * gain - hat * inner_mean)
    dy_ref[...] = grad_inner * act
    dgate = (grad_inner * y * sig_gate * (1.0 + gate_pre * (1.0 - sig_gate))).astype(bf16)
    dgate_ref[...] = dgate
    total[:, :channels] += tn(normed, dgate)

    @pl.when(step_id == pl.num_programs(0) - 1)
    def _():
        out_ref[...] = total[...].astype(bf16)
        gain_ref[...] = gain_row(w_ref[...], total[:, :channels])


def backward_kernel(len_ref, first_ref, place_ref, *refs, seqs, taps, halves, place_at):
    (
        w_ref,
        gain_ref,
        terms_ref,
        dprm_gate_ref,
        prm_ref,
        prs_ref,
        prh_ref,
        upper_ref,
        spread_ref,
        gather_ref,
        normed_ref,
        dgate_ref,
        dy_ref,
        v_ref,
        u_ref,
        vs_ref,
        us_ref,
        scan_ref,
        y_ref,
        st_ref,
    ) = refs[:20]
    half_refs = refs[20 : 20 + halves]
    out_ref, small_ref, dprm_ref, dprs_ref, dprh_ref, dbuf, dsbuf, carry, ending, total = refs[20 + halves :]
    rows, channels = dgate_ref.shape
    step_id = pl.program_id(0)
    base = (pl.num_programs(0) - 1 - step_id) * rows
    ends = ends_of(len_ref, seqs)

    @pl.when(step_id == 0)
    def _():
        dbuf[...] = jnp.zeros_like(dbuf)
        dsbuf[...] = jnp.zeros_like(dsbuf)
        carry[...] = jnp.zeros_like(carry)
        ending[...] = jnp.zeros_like(ending)
        dprm_ref[...] = jnp.zeros_like(dprm_ref)
        dprs_ref[...] = jnp.zeros_like(dprs_ref)
        dprh_ref[...] = jnp.zeros_like(dprh_ref)
        total[...] = jnp.zeros_like(total)

    def add_row(ref, at, z):
        ref[at : at + 1, :] += jnp.sum(z, axis=0, keepdims=True)

    skip = prm_ref[taps + 1 : taps + 2, :]
    u = u_ref[...]
    sig_u = jax.nn.sigmoid(u)
    x = u * sig_u
    y_scan = y_ref[...]
    dy = dy_ref[...]
    dy_b = dy.astype(bf16)

    add_row(dprm_ref, taps + 1, dy * x)
    us = us_ref[...]
    sig_us = jax.nn.sigmoid(us)
    maps = us * sig_us
    maps_b = maps.astype(bf16)
    terms = scan_ref[...]
    lane = lax.broadcasted_iota(jnp.int32, (rows, LANES), 1)
    inside = lane < FIELD
    step = jnp.where(inside, terms, 0.0)
    raw = jnp.where(inside, pltpu.roll(terms, LANES - FIELD, 1), 0.0)
    cum = jnp.where(inside, pltpu.roll(terms, LANES - 2 * FIELD, 1), 0.0)
    decay = prh_ref[1:2, :]
    step_w, carried_w, keep_w, survive_w = scan_weights(step, cum, base, ends, spread_ref[...])
    cum = cum * LOG2E
    cum_row = cum.T
    stepped = step_w * x
    stepped_b = stepped.astype(bf16)
    kept_b = (keep_w * stepped).astype(bf16)
    dy_carried = carried_w * dy
    dy_carried_b = dy_carried.astype(bf16)
    row = lax.broadcasted_iota(jnp.int32, (SUB, SUB), 0)
    col = lax.broadcasted_iota(jnp.int32, (SUB, SUB), 1)
    dstate = carry[...]
    state_end = ending[0:1, :]
    subs = rows // SUB
    dsteppeds, dmaps, state_ends = [None] * subs, [None] * subs, [None] * subs
    for q in reversed(range(subs)):
        at = slice(q * SUB, (q + 1) * SUB)
        low = base + q * SUB
        mask = (row <= col) & (segment_of(low + row, ends) == segment_of(low + col, ends))
        b_map, c_map = maps[at, :STATE], maps[at, STATE:]
        gram = jnp.where(mask, nt3(b_map, c_map), 0.0)
        state = st_ref[q]
        dstate_b = dstate.astype(bf16)
        dgram = jnp.zeros((SUB, SUB), f32)
        inner = []
        for pair in range(channels // LANES):
            lanes = slice(pair * LANES, (pair + 1) * LANES)
            dmix = nt(pair_stack(stepped_b[at, lanes]), dy_b[at, lanes])
            mixing = []
            for i, h in enumerate((2 * pair, 2 * pair + 1)):
                spread = cum_row[h : h + 1, at] - cum[at, h : h + 1]
                weight = jnp.exp2(jnp.minimum(spread, 0.0))
                mixing.append((weight * gram).astype(bf16))
                dgram = dgram + dmix[i * SUB : (i + 1) * SUB] * weight
            inner.append(pair_product(mixing, dy[at, lanes]))
        dsteppeds[q] = jnp.concatenate(inner, axis=1) + keep_w[at] * nn3(b_map, dstate)
        dgram = jnp.where(mask, dgram, 0.0).astype(bf16)
        db = nn(dgram, maps_b[at, STATE:]) + nt(kept_b[at], dstate_b)
        dc = tn(dgram, maps_b[at, :STATE]) + nt(dy_carried_b[at], state.astype(bf16))
        dmaps[q] = jnp.concatenate([db, dc], axis=1)
        state_ends[q] = state_end
        dstate = survive_w[q : q + 1] * dstate + nn3(c_map.T, dy_carried[at])
        state_end = jnp.sum(state * dstate, axis=0, keepdims=True)
    carry[...] = dstate
    ending[0:1, :] = state_end
    dstepped = jnp.concatenate(dsteppeds, axis=0)
    dmap = jnp.concatenate(dmaps, axis=0)
    state_ends.append(jnp.zeros((-subs % 8, channels), f32))
    by_head = gather_heads(
        jnp.concatenate([dy * y_scan - stepped * dstepped, x * dstepped] + state_ends, axis=0),
        gather_ref[...],
    )
    dlog = triangle_sum(upper_ref[...], by_head[:rows])
    dlog = jnp.concatenate(
        [
            dlog[q * SUB : (q + 1) * SUB] + by_head[2 * rows + q : 2 * rows + q + 1]
            for q in range(subs)
        ],
        axis=0,
    )
    draw = (by_head[rows : 2 * rows] - decay * dlog) * jax.nn.sigmoid(raw)
    add_row(dprh_ref, 0, draw)
    add_row(dprh_ref, 1, dlog * step * -decay)
    places = base + lax.broadcasted_iota(jnp.int32, (rows, 1), 0)
    segment = segment_of(places, ends)
    usable = [None] + [segment_of(places + lag, ends) == segment for lag in range(1, taps)]
    normed = normed_ref[...]

    line = lax.broadcasted_iota(jnp.int32, (rows, 1), 0)

    def conv_back(du, v, weight_ref, tail_ref, sums_ref):
        edge = jnp.concatenate([du[rows - 8 :], tail_ref[...]], axis=0)
        dv = weight_ref[taps - 1 : taps, :] * du
        edge_dv = jnp.zeros((8, du.shape[1]), f32)
        lines = [jnp.sum(du * v, axis=0, keepdims=True), jnp.sum(du, axis=0, keepdims=True)]
        for lag in range(1, taps):
            weight = weight_ref[taps - 1 - lag : taps - lag, :]
            later = jnp.where(usable[lag] & (line < rows - lag), pltpu.roll(du, rows - lag, 0), 0.0)
            inside = usable[lag][rows - 8 :] & (line[:8] >= 8 - lag)
            edge_later = jnp.where(inside, edge[lag : lag + 8], 0.0)
            dv = dv + weight * later
            edge_dv = edge_dv + weight * edge_later
            total_line = jnp.sum(later * v, axis=0, keepdims=True)
            lines.insert(0, total_line + jnp.sum(edge_later * v[rows - 8 :], axis=0, keepdims=True))
        tail_ref[...] = du[0:8]
        sums_ref[0 : taps + 1, :] += jnp.concatenate(lines, axis=0)
        return jnp.concatenate([dv[: rows - 8], dv[rows - 8 :] + edge_dv], axis=0).astype(bf16)

    product = nt(dgate_ref[...], w_ref[:, :channels])
    du = (step_w * dstepped + skip * dy) * sig_u * (1.0 + u * (1.0 - sig_u))
    dv = conv_back(du, v_ref[...].astype(f32), prm_ref, dbuf, dprm_ref)
    product = product + nt(dv, w_ref[:, channels : 2 * channels])
    total[:, :channels] += tn(normed, dv)
    dus = dmap * sig_us * (1.0 + us * (1.0 - sig_us))
    dvs = conv_back(dus, vs_ref[...].astype(f32), prs_ref, dsbuf, dprs_ref)
    state_part = jnp.concatenate([dvs, pltpu.roll(draw, first_ref[0], 1).astype(bf16)], axis=1)
    product = product + nt(state_part, w_ref[:, 2 * channels :])
    total[:, channels:] += tn(normed, state_part)
    put_halves(half_refs, place_ref[place_at + step_id], product.astype(bf16))

    @pl.when(step_id == pl.num_programs(0) - 1)
    def _():
        grads = total[...]
        out_ref[...] = grads.astype(bf16)
        gains = (gain_row(w_ref[:, channels:], grads) + terms_ref[...]) / gain_ref[...]
        line = lax.broadcasted_iota(jnp.int32, (8, 1), 0)
        both = jnp.where(line == taps + 2, dprm_gate_ref[...], dprm_ref[...])
        skips = gather_heads(dprm_ref[...], gather_ref[...])
        by_head = jnp.where(line == 2, pltpu.roll(skips, 8 - (taps - 1), 0), dprh_ref[...])
        small_ref[...] = jnp.zeros_like(small_ref)
        small_ref[0:8, :channels] = both
        small_ref[0:8, channels : channels + 2 * STATE] = dprs_ref[...]
        small_ref[0:8, channels + 2 * STATE : channels + 2 * STATE + LANES] = pltpu.roll(
            by_head, first_ref[0], 1
        )
        small_ref[8:16, :] = gains


def held(places):
    last = next(p for p in places if p is not None)
    filled = []
    for p in places:
        last = last if p is None else p
        filled.append(last)
    return filled


def place_table(tensor_place, quarter_blocks, order):
    relative = [(b // quarter_blocks) ^ tensor_place for b in order]
    inside = [b % quarter_blocks for b in order]

    def places(slots):
        return held(
            [slots.index(r) * quarter_blocks + w if r in slots else None for r, w in zip(relative, inside)]
        )

    return [
        relative,
        places([0]),
        places([1]),
        places([2]),
        places([3]),
        places([1, 3]),
        places([0, 2]),
        places([2, 3]),
        places([0, 1]),
    ]


def over_x(z):
    return lax.ppermute(z, "tensor", [(0, 1), (1, 0), (2, 3), (3, 2)])


def over_y(z):
    return lax.ppermute(z, "tensor", [(0, 2), (2, 0), (1, 3), (3, 1)])


def gather_start(z):
    return over_x(z), over_y(z)


def gather_end(z, from_x, from_y, after=()):
    half = z.shape[1] // 2
    far = (from_x[:, :half], from_y[:, half:])
    far, after = lax.optimization_barrier((far, after))
    return [z, from_x, from_y, over_y(far[0]), over_x(far[1])], after


def scatter_start(halves):
    return over_x(halves[0]), over_y(halves[2])


def scatter_middle(halves, from_x, from_y, after=()):
    rows = from_x.shape[0] // 2
    left, right = halves[1], halves[3]
    left_far = left[rows:].astype(f32) + from_x[rows:].astype(f32)
    right_far = right[rows:].astype(f32) + from_y[rows:].astype(f32)
    far = (left_far.astype(bf16), right_far.astype(bf16))
    far, after = lax.optimization_barrier((far, after))
    return (over_y(far[0]), over_x(far[1])), after


def scatter_end(halves, from_x, from_y, far_left, far_right):
    rows = from_x.shape[0] // 2
    left, right = halves[1][:rows].astype(f32), halves[3][:rows].astype(f32)
    left = left + from_x[:rows].astype(f32) + far_left.astype(f32)
    right = right + from_y[:rows].astype(f32) + far_right.astype(f32)
    return left, right


def sum_over_tensor(z):
    z = (z.astype(f32) + over_x(z).astype(f32)).astype(z.dtype)
    return z.astype(f32) + over_y(z).astype(f32)


def sum_over_dp(z):
    count = lax.axis_size("dp")
    bit = 1
    while bit < count:
        z = z + lax.ppermute(z, "dp", [(i, i ^ bit) for i in range(count)])
        bit *= 2
    return z


class Kernels:
    def __init__(self, lengths, first, tensor_place, tensor_count, group_rows, width, channels, taps, head_count):
        self.lengths, self.first = lengths, first
        self.tensor_place, self.tensor_count = tensor_place, tensor_count
        self.square = tensor_count == 4
        self.group_rows, self.width, self.channels = group_rows, width, channels
        self.taps, self.head_count = taps, head_count
        self.seqs = lengths.shape[1]
        self.lower, self.upper, self.spread, self.gather = constants(channels)
        self.tables()

    def tables(self):
        kinds = ((ROWS, False), (ROWS, True), (WIDE_ROWS, False))
        self.kinds = {kind: k for k, kind in enumerate(kinds)}
        places = range(4) if self.square else range(1)
        made = []
        for t in places:
            lines = []
            for block, backwards in kinds:
                order = list(range(self.group_rows // block))[:: -1 if backwards else 1]
                table = place_table(t, len(order) // 4, order) if self.square else [order]
                lines += [line + [0] * (self.group_rows // ROWS - len(order)) for line in table]
            made.append(lines)
        self.lines = len(made[0]) // len(kinds)
        made = jnp.asarray(np.array(made, np.int32).reshape(len(made), -1))
        place = self.tensor_place if self.square else 0
        self.place = lax.dynamic_index_in_dim(made, place, 0, keepdims=False)
        self.steps = self.group_rows // ROWS

    def at(self, block, backwards, line):
        return (self.kinds[(block, backwards)] * self.lines + line) * self.steps

    def call(self, kernel, scalars, steps, ins, outs, scratch, aliases=None, flops=1000):
        specs, arrays = zip(*ins)
        out_specs, out_shapes = zip(*outs)
        return pl.pallas_call(
            kernel,
            grid_spec=pltpu.PrefetchScalarGridSpec(
                num_scalar_prefetch=len(scalars),
                grid=(steps,),
                in_specs=list(specs),
                out_specs=list(out_specs),
                scratch_shapes=scratch,
            ),
            out_shape=list(out_shapes),
            input_output_aliases=aliases or {},
            compiler_params=pltpu.CompilerParams(vmem_limit_bytes=56 * 2**20),
            cost_estimate=pl.CostEstimate(flops=flops, bytes_accessed=1000, transcendentals=0),
            name=getattr(kernel, "func", kernel).__name__,
        )(*scalars, *arrays)

    def whole(self, array):
        return pl.BlockSpec(array.shape, lambda i, *s: (0,) * len(array.shape)), array

    def columns(self, array, width, place):
        return pl.BlockSpec((array.shape[0], width), lambda i, *s: (0, place)), array

    def rows(self, array, block, backwards=False, low=0):
        last = self.group_rows // block - 1

        def at(i, *s):
            return (last - i if backwards else i + low,) + (0,) * (len(array.shape) - 1)

        size = array.shape[0] * block // self.group_rows
        return pl.BlockSpec((size,) + array.shape[1:], at), array

    def across(self, array, block, low=0):
        return pl.BlockSpec((8, block), lambda i, *s: (0, i + low)), array

    def out(self, columns, dtype):
        return jax.ShapeDtypeStruct((self.group_rows, columns), dtype)

    def parts(self, arrays, block, low=0):
        if not self.square:
            return [self.rows(arrays[0], block, low=low)]
        return [
            (
                pl.BlockSpec(
                    (block, z.shape[1]), lambda i, *s, at=self.at(block, False, k): (s[-1][at + i + low], 0)
                ),
                z,
            )
            for k, z in zip((1, 2, 3, 4, 4) if len(arrays) == 5 else (1, 2, 2, 3, 3, 4, 4), arrays)
        ]

    def halves(self, block, backwards=False):
        half = self.width // 2
        lines = (5, 6, 7, 8) if self.square else (0, 0)
        rows = self.group_rows // 2 if self.square else self.group_rows
        shape = jax.ShapeDtypeStruct((rows, half), bf16)
        return [
            (
                pl.BlockSpec((block, half), lambda i, *s, at=self.at(block, backwards, k): (s[-1][at + i], 0)),
                shape,
            )
            for k in lines
        ]

    def parameters(self, packed, cut, state_cut, head_cut, depth):
        shapes = ((8, self.channels), (8, 2 * STATE), (8, LANES), (1, self.width))
        return self.call(
            functools.partial(
                parameter_kernel,
                taps=self.taps,
                heads_here=self.head_count,
                cut=cut,
                state_cut=state_cut,
                head_cut=head_cut,
                depth=depth,
            ),
            (self.first,),
            1,
            [self.whole(packed)],
            [self.whole(jax.ShapeDtypeStruct(shape, f32)) for shape in shapes],
            [],
        )

    def scan(self, low, high, hidden, weights, gain, prm, prs, prh, carried, before=()):
        channels, count = self.channels, self.group_rows
        parts = self.parts(hidden, ROWS, low)
        shapes = [
            self.out(self.width, bf16),
            self.out(channels, bf16),
            self.out(channels, f32),
            self.out(2 * STATE, bf16),
            self.out(2 * STATE, f32),
            self.out(LANES, f32),
            self.out(channels, f32),
            jax.ShapeDtypeStruct((count // SUB, STATE, channels), f32),
            self.out(channels, bf16),
            self.out(channels, bf16),
            self.out(channels, bf16),
        ]
        outs = [self.rows(z, ROWS, low=low) for z in shapes]
        outs.append(self.across(jax.ShapeDtypeStruct((8, count), f32), ROWS, low))
        kept = len(outs)
        ins = parts + [self.whole(z) for z in [weights, gain, prm, prs, prh, self.lower, self.spread] + list(carried)]
        aliases = {3 + len(ins) + k: k for k in range(len(before))}
        ins += [(pl.BlockSpec(memory_space=pl.ANY), z) for z in before]
        sizes = ((8, channels), (8, 2 * STATE), (STATE, channels))
        outs += [self.whole(jax.ShapeDtypeStruct(size, f32)) for size in sizes]
        result = self.call(
            functools.partial(
                scan_kernel,
                parts=len(parts),
                seqs=self.seqs,
                taps=self.taps,
                head_count=self.head_count,
                first_block=low,
                kept=len(before),
                starts=len(carried),
                place_at=self.at(ROWS, False, 0),
            ),
            (self.lengths, self.first, self.place),
            high - low,
            ins,
            outs,
            [
                pltpu.VMEM((ROWS, self.width), bf16),
                pltpu.VMEM((ROWS + 8, channels), f32),
                pltpu.VMEM((ROWS + 8, 2 * STATE), f32),
            ],
            aliases,
        )
        return result[:kept], result[kept:]

    def product(self, ga, weights):
        return self.call(
            functools.partial(product_kernel, place_at=self.at(WIDE_ROWS, False, 0)),
            (self.place,),
            self.group_rows // WIDE_ROWS,
            [self.rows(ga, WIDE_ROWS), self.whole(weights)],
            self.halves(WIDE_ROWS),
            [],
        )

    def cotangent(self, cotangent, weights, ga, square):
        parts = self.parts(cotangent, WIDE_ROWS)
        return self.call(
            functools.partial(cotangent_kernel, parts=len(parts), place_at=self.at(WIDE_ROWS, False, 0)),
            (self.place,),
            self.group_rows // WIDE_ROWS,
            parts + [self.whole(weights), self.rows(ga, WIDE_ROWS), self.across(square, WIDE_ROWS)],
            [
                self.rows(self.out(self.channels, bf16), WIDE_ROWS),
                self.across(jax.ShapeDtypeStruct((8, self.group_rows), f32), WIDE_ROWS),
            ],
            [pltpu.VMEM((WIDE_ROWS, self.width), bf16)],
        )

    def gate(self, cotangent, sums, prm, weights, gate, y, gg, normed):
        channels = self.channels
        parts = self.parts(cotangent, WIDE_ROWS)
        return self.call(
            functools.partial(
                gate_kernel, parts=len(parts), taps=self.taps, place_at=self.at(WIDE_ROWS, False, 0)
            ),
            (self.place,),
            self.group_rows // WIDE_ROWS,
            parts
            + [self.across(sums, WIDE_ROWS), self.whole(prm), self.columns(weights, channels, 0)]
            + [self.rows(z, WIDE_ROWS) for z in (gate, y, gg, normed)],
            [
                self.rows(self.out(channels, bf16), WIDE_ROWS),
                self.rows(self.out(channels, f32), WIDE_ROWS),
                self.whole(jax.ShapeDtypeStruct(prm.shape, f32)),
                self.whole(jax.ShapeDtypeStruct((self.width, 2 * channels), bf16)),
                self.whole(jax.ShapeDtypeStruct((8, self.width), f32)),
            ],
            [pltpu.VMEM((WIDE_ROWS, self.width), bf16), pltpu.VMEM((self.width, 2 * channels), f32)],
            flops=8 * self.group_rows * self.width * channels * 4,
        )

    def backward(self, weights, gain, terms, dprm_gate, prm, prs, prh, saved):
        channels = self.channels
        gradients = channels + 3 * STATE
        halves = self.halves(ROWS, True)
        shapes = [
            jax.ShapeDtypeStruct((self.width, gradients), bf16),
            jax.ShapeDtypeStruct((16, self.width), f32),
        ]
        shapes += [jax.ShapeDtypeStruct(z.shape, f32) for z in (prm, prs, prh)]
        result = self.call(
            functools.partial(
                backward_kernel,
                seqs=self.seqs,
                taps=self.taps,
                halves=len(halves),
                place_at=self.at(ROWS, True, 0),
            ),
            (self.lengths, self.first, self.place),
            self.group_rows // ROWS,
            [
                self.whole(z)
                for z in (weights, gain, terms, dprm_gate, prm, prs, prh, self.upper, self.spread, self.gather)
            ]
            + [self.rows(z, ROWS, True) for z in saved],
            halves + [self.whole(z) for z in shapes],
            [
                pltpu.VMEM((8, channels), f32),
                pltpu.VMEM((8, 2 * STATE), f32),
                pltpu.VMEM((STATE, channels), f32),
                pltpu.VMEM((8, channels), f32),
                pltpu.VMEM((self.width, gradients), f32),
            ],
        )
        return result[: len(halves)], result[len(halves)], result[len(halves) + 1]


def per_device(
    hidden_in,
    norm_gain,
    proj_gate,
    proj_conv,
    proj_state,
    conv_kernel,
    conv_offset,
    state_kernel,
    state_offset,
    step_bias,
    decay_log,
    skip_gain,
    gate_gain,
    proj_out,
    out_cotangent,
    seq_lengths,
):
    tensor_count = lax.axis_size("tensor")
    tensor_place = lax.axis_index("tensor")
    dp_count = lax.axis_size("dp")
    dp_place = lax.axis_index("dp")
    square_mesh = tensor_count == 4
    own_rows, width = hidden_in.shape
    depth, channels = proj_gate.shape
    taps, heads_here, cut = conv_kernel.shape
    head_cut = step_bias.shape[0]
    state_cut = state_kernel.shape[1]
    state_width = proj_state.shape[1]
    group_rows = own_rows * tensor_count
    first_head = (tensor_place * heads_here).astype(jnp.int32)

    state_part = jnp.pad(proj_state, ((0, 0), (0, 3 * STATE - state_width)))
    weights = lax.all_gather(
        jnp.concatenate([proj_gate, proj_conv, state_part], axis=1), "dp", axis=0, tiled=True
    )
    out_weights = lax.all_gather(proj_out.T, "dp", axis=0, tiled=True)
    if square_mesh:
        half = width // 2
        left, right = hidden_in[:, :half], hidden_in[:, half:]
        x_left, y_right = over_x(left), over_y(right)
        x_right, y_left = over_x(right), over_y(left)

    def padded(z):
        return jnp.pad(z, ((0, 0), (0, LANES - z.shape[1])))

    packed = jnp.concatenate(
        [
            padded(jnp.concatenate([conv_kernel.reshape(taps, -1), state_kernel], axis=1)),
            padded(jnp.concatenate([conv_offset.reshape(1, -1), state_offset[None]], axis=1)),
            padded(
                jnp.concatenate(
                    [gate_gain.reshape(1, -1), step_bias[None], decay_log[None], skip_gain[None]], axis=1
                )
            ),
            padded(norm_gain[None]),
        ],
        axis=0,
    )
    packed = jnp.pad(packed, ((0, PARAMS - packed.shape[0]), (0, 0)))
    packed = lax.all_gather(packed, "dp", axis=1, tiled=True)
    if square_mesh:
        x_left, y_right, packed = lax.optimization_barrier((x_left, y_right, packed))
        far_left, far_right = over_y(x_left), over_x(y_right)
        hidden_all = [hidden_in, x_left, x_right, y_left, y_right, far_left, far_right]
    else:
        hidden_all = [lax.all_gather(hidden_in, "tensor", axis=0, tiled=True)]

    kernels = Kernels(
        seq_lengths,
        first_head.reshape(1),
        tensor_place,
        tensor_count,
        group_rows,
        width,
        channels,
        taps,
        heads_here,
    )

    prm, prs, prh, gain_in = kernels.parameters(packed, cut, state_cut, head_cut, depth)
    if square_mesh:
        hidden_all, prm, kernels.place, cot = lax.optimization_barrier(
            (hidden_all, prm, kernels.place, out_cotangent)
        )

    blocks = group_rows // ROWS
    common = (hidden_all, weights, gain_in, prm, prs, prh)
    if square_mesh:
        moving = gather_start(cot)
        middle = blocks * 3 // 4
        saved, carried = kernels.scan(0, middle, *common, ())
        carried, moving = lax.optimization_barrier((carried, moving))
        cotangent_all, carried = gather_end(cot, *moving, carried)
        saved, _ = kernels.scan(middle, blocks, *common, carried, saved)
    else:
        cotangent_all = [lax.all_gather(out_cotangent, "tensor", axis=0, tiled=True)]
        saved, _ = kernels.scan(0, blocks, *common, ())
    normed, v, u, vs, us, scan_terms, y_scan, states, gate_pre, ga, y_total, square = saved
    gg, sums = kernels.cotangent(cotangent_all, out_weights, ga, square)
    gg, ga = lax.optimization_barrier((gg, ga))
    out_halves = kernels.product(ga, out_weights)
    if square_mesh:
        sums = sums + over_x(sums)
        sums, out_halves = lax.optimization_barrier((sums, out_halves))
        sums = sums + over_y(sums)
        moving = scatter_start(out_halves)
    else:
        sums = lax.psum(sums, "tensor")

    dgate, dy, dprm_gate, grad_first, terms = kernels.gate(
        cotangent_all, sums, prm, weights, gate_pre, y_total, gg, normed
    )
    if square_mesh:
        dy, grad_first, moving = lax.optimization_barrier((dy, grad_first, moving))
        far, dy = scatter_middle(out_halves, *moving, dy)
        out_moving = moving + far
    own_first = lax.psum_scatter(grad_first, "dp", scatter_dimension=0, tiled=True)
    gn_halves, grad_last, small_sum = kernels.backward(
        weights,
        gain_in,
        terms,
        dprm_gate,
        prm,
        prs,
        prh,
        [normed, dgate, dy, v, u, vs, us, scan_terms, y_scan, states],
    )

    def own_sum(halves):
        return lax.psum_scatter(
            jnp.concatenate(halves, axis=1), "tensor", scatter_dimension=0, tiled=True
        ).astype(f32)

    if square_mesh:
        gn_halves, grad_last, small_sum, own_first, out_moving = lax.optimization_barrier(
            (gn_halves, grad_last, small_sum, own_first, out_moving)
        )
        moving = scatter_start(gn_halves)
    own_last = lax.psum_scatter(grad_last, "dp", scatter_dimension=0, tiled=True)
    small_sum = sum_over_dp(small_sum)
    if square_mesh:
        small_x = small_sum + over_x(small_sum)
        small_x, moving = lax.optimization_barrier((small_x, moving))
        small_shared = small_x + over_y(small_x)
        far, small_shared = scatter_middle(gn_halves, *moving, small_shared)
    else:
        small_shared = lax.psum(small_sum, "tensor")

    if square_mesh:
        far, own_last = lax.optimization_barrier((far, own_last))
        own_state = own_last[:, channels:].astype(f32)
        own_state = (own_state + over_x(own_last[:, channels:]).astype(f32)).astype(bf16)
        grad_normed = scatter_end(gn_halves, *moving, *far)
        grad_normed, own_state = lax.optimization_barrier((grad_normed, own_state))
        own_state = own_state.astype(f32) + over_y(own_state).astype(f32)
        grad_normed = jnp.concatenate(grad_normed, axis=1)
        branch = jnp.concatenate(scatter_end(out_halves, *out_moving), axis=1)
    else:
        grad_normed = own_sum(gn_halves)
        own_state = lax.psum(own_last[:, channels:].astype(f32), "tensor")
        branch = own_sum(out_halves)

    own_square = lax.dynamic_slice_in_dim(sums[0], tensor_place * own_rows, own_rows, 0)
    inverse_gate = lax.rsqrt(own_square * (1.0 / INNER) + EPS)[:, None]
    values = hidden_in.astype(f32)
    block_out = (values + branch * inverse_gate).astype(bf16)

    inverse_in = lax.rsqrt(jnp.mean(values * values, axis=1, keepdims=True) + EPS)
    scaled = values * inverse_in
    grad_scaled = grad_normed * gain_in
    grad_hidden = out_cotangent.astype(f32) + inverse_in * (
        grad_scaled - scaled * jnp.mean(grad_scaled * scaled, axis=1, keepdims=True)
    )

    own_part = depth // tensor_count
    own_state = lax.dynamic_slice_in_dim(own_state, tensor_place * own_part, own_part, 0)[:, :state_width]

    def own_cut(z, size, axis):
        return lax.dynamic_slice_in_dim(z, dp_place * size, size, axis)

    by_channel = small_sum[: taps + 3, :channels].reshape(taps + 3, heads_here, HEADDIM)
    by_channel = own_cut(by_channel, cut, 2)
    by_map = own_cut(small_shared[: taps + 1, channels : channels + 2 * STATE], state_cut, 1)
    heads_at = channels + 2 * STATE
    by_head = own_cut(small_shared[:3, heads_at : heads_at + LANES], head_cut, 1)
    gain_grad = lax.dynamic_slice_in_dim(
        small_shared[8], (dp_place * tensor_count + tensor_place) * own_part, own_part, 0
    )
    own_first = own_first.astype(f32)
    return (
        block_out,
        grad_hidden,
        gain_grad,
        own_first[:, :channels],
        own_last[:, :channels].astype(f32),
        own_state,
        own_first[:, channels:].T,
        by_channel[:taps],
        by_channel[taps],
        by_map[:taps],
        by_map[taps],
        by_head[0],
        by_head[1],
        by_head[2],
        by_channel[taps + 2],
    )


def solution(mesh):
    placed = (
        P(("dp", "tensor"), None),
        P("dp"),
        P("dp", "tensor"),
        P("dp", "tensor"),
        P("dp", None),
        P(None, "tensor", "dp"),
        P("tensor", "dp"),
        P(None, "dp"),
        P("dp"),
        P("dp"),
        P("dp"),
        P("dp"),
        P("tensor", "dp"),
        P("tensor", "dp"),
        P(("dp", "tensor"), None),
        P("dp", None),
    )
    return jax.shard_map(
        per_device,
        mesh=mesh,
        in_specs=placed,
        out_specs=(
            P(("dp", "tensor"), None),
            P(("dp", "tensor"), None),
            P(("dp", "tensor")),
            P("dp", "tensor"),
            P("dp", "tensor"),
            P(("dp", "tensor"), None),
            P("tensor", "dp"),
            P(None, "tensor", "dp"),
            P("tensor", "dp"),
            P(None, "dp"),
            P("dp"),
            P("dp"),
            P("dp"),
            P("dp"),
            P("tensor", "dp"),
        ),
        check_vma=False,
    )
```
